32 devices in a mesh: ctx: 8 (over y, x, core), shard: 4 (over z).
Axes of the slice: x: 2, y: 2, z: 4, core: 2. Of those that a mesh axis runs over, the one named last changes fastest.
Arguments:
- tokens: bfloat16 [4, 1024, 2048], P('shard', 'ctx'), may hold values from -6 to 6
- qkv_weight: bfloat16 [2048, 6144], P('shard'), may hold values from -0.1875 to 0.1875
- qkv_bias: float32 [6144], replicated, may hold values from -1.5 to 1.5
- out_weight: bfloat16 [2048, 2048], P('shard'), may hold values from -0.75 to 0.75
- out_bias: float32 [2048], replicated, may hold values from -1.5 to 1.5
- up_weight: bfloat16 [2048, 8192], P('shard'), may hold values from -0.125 to 0.125
- up_bias: float32 [8192], replicated, may hold values from -2.5 to 2.5
- down_weight: bfloat16 [2048, 8192], P('shard'), may hold values from -0.0625 to 0.0625
- down_bias: float32 [2048], replicated, may hold values from -1.5 to 1.5
- attn_norm_gain: float32 [2048], replicated, may hold values from 0.5 to 1.5
- attn_norm_bias: float32 [2048], replicated, may hold values from -1.5 to 1.5
- mlp_norm_gain: float32 [2048], replicated, may hold values from 0.5 to 1.5
- mlp_norm_bias: float32 [2048], replicated, may hold values from -1.5 to 1.5
- cotangent: bfloat16 [4, 1024, 2048], P('shard', 'ctx'), may hold values from -6 to 6
Outputs:
- output: bfloat16 [4, 1024, 2048], P('shard', 'ctx')
- tokens_grad: float32 [4, 1024, 2048], P('shard', 'ctx')
- qkv_weight_grad: float32 [2048, 6144], P(('ctx', 'shard'))
- qkv_bias_grad: float32 [6144], replicated
- out_weight_grad: float32 [2048, 2048], P(('ctx', 'shard'))
- out_bias_grad: float32 [2048], replicated
- up_weight_grad: float32 [2048, 8192], P(('ctx', 'shard'))
- up_bias_grad: float32 [8192], replicated
- down_weight_grad: float32 [2048, 8192], P(('ctx', 'shard'))
- down_bias_grad: float32 [2048], replicated
- attn_norm_gain_grad: float32 [2048], replicated
- attn_norm_bias_grad: float32 [2048], replicated
- mlp_norm_gain_grad: float32 [2048], replicated
- mlp_norm_bias_grad: float32 [2048], replicated
The draws below stay inside these ranges and needn't reach their ends.
All inputs are finite; a program needn't handle non-finite values.
Results may differ from the reference program's by a relative error of at most 0.012.
The reference program's roundings to bfloat16 on the way count: a program that leaves them out, or rounds other values in their place, can miss the bound.
Values may be sent and summed in bfloat16 or wider, within the bound.
A program may use at most 704 MiB of HBM per device.

```python
import math
import jax
import jax.numpy as jnp
from jax import lax

H = 8
HD = 256
ROT = 64
FF = 8192
D = 2048
LEN = 1024
SEQS = 4


def spiked(values, stream_key, source, target, shards_of, factor):
    def block_of(position):
        return (jnp.arange(values.shape[position]) // (values.shape[position] // shards_of)).reshape((-1,) + (1,) * (values.ndim - 1 - position))

    one_side = jax.random.permutation(stream_key, shards_of)[block_of(target)]
    far = (block_of(target) + shards_of // 2) % shards_of
    return jnp.where((block_of(source) == one_side) | (block_of(source) == far), factor * values, values)


def block_levels(own_key, dims, pieces, smallest, top_value):
    loudness, own = 1.0, jax.random.fold_in(own_key, 6)
    for axis_at, shards_of in pieces:
        draws = jnp.exp(jax.random.uniform(jax.random.fold_in(own, axis_at), (shards_of,), jnp.float32, smallest / len(pieces), top_value / len(pieces)))
        loudness = loudness * jnp.repeat(draws, dims[axis_at] // shards_of).reshape([-1 if axis == axis_at else 1 for axis in range(len(dims))])
    return loudness


def centred(stream_key, extent, width, most, pieces=(), kind=jnp.bfloat16):
    entries = jax.random.normal(stream_key, extent, jnp.float32) * width
    if len(pieces) > 0:
        entries = block_levels(stream_key, extent, pieces, -0.22, 0.18) * entries
    return jnp.clip(entries, min=-most, max=most).astype(kind)


def heavy_noise(key, shape, width, limit, pieces, heavy, held_as=jnp.bfloat16):
    array = width * jax.random.normal(key, shape, jnp.float32)
    if pieces:
        array = array * block_levels(key, shape, pieces, -0.22, 0.18)
    return jnp.clip(spiked(array, jax.random.fold_in(key, 3), *heavy), -limit, limit).astype(held_as)


def setup_inputs(seed: int = 0) -> dict:
    key_of = jax.random.split(jax.random.key(seed), 15)
    tokens = centred(key_of[0], (SEQS, LEN, D), 1.0, 6.0, ((0, 4), (1, 8)))
    qkv_weight = centred(key_of[1], (D, 3 * D), (D // 2) ** -0.5, 0.1875, ((0, 4),))
    qkv_bias = centred(key_of[2], (3 * D,), 0.3, 1.5, (), jnp.float32)
    out_weight = centred(key_of[3], (D, D), 64 ** -0.5, 0.75, ((0, 4),))
    out_bias = centred(key_of[4], (D,), 0.3, 1.5, (), jnp.float32)
    up_weight = centred(key_of[5], (D, FF), D ** -0.5, 0.125, ((0, 4),))
    up_bias = centred(key_of[6], (FF,), 0.5, 2.5, (), jnp.float32)
    down_weight = centred(key_of[7], (D, FF), FF ** -0.5, 0.0625, ((0, 4),))
    down_bias = centred(key_of[8], (D,), 0.3, 1.5, (), jnp.float32)
    attn_norm_gain = jnp.clip(1.0 + 0.1 * jax.random.normal(key_of[9], (D,), jnp.float32), 0.5, 1.5)
    attn_norm_bias = centred(key_of[10], (D,), 0.3, 1.5, (), jnp.float32)
    mlp_norm_gain = jnp.clip(1.0 + 0.1 * jax.random.normal(key_of[11], (D,), jnp.float32), 0.5, 1.5)
    mlp_norm_bias = centred(key_of[12], (D,), 0.3, 1.5, (), jnp.float32)
    cotangent = heavy_noise(key_of[13], (SEQS, LEN, D), 1.0, 6.0, ((0, 4), (1, 8)), (1, 2, 8, 2.0))
    return dict(tokens=tokens, qkv_weight=qkv_weight, qkv_bias=qkv_bias, out_weight=out_weight, out_bias=out_bias, up_weight=up_weight, up_bias=up_bias, down_weight=down_weight, down_bias=down_bias, attn_norm_gain=attn_norm_gain, attn_norm_bias=attn_norm_bias, mlp_norm_gain=mlp_norm_gain, mlp_norm_bias=mlp_norm_bias, cotangent=cotangent)


@jax.custom_vjp
def low(v):
    return lax.optimization_barrier(v.astype(jnp.bfloat16)).astype(jnp.float32)

@jax.custom_vjp
def low_back(v):
    return v

def low_keep(v):
    return (low(v), None)

def low_pass(kept, grad):
    return (grad,)

def back_keep(v):
    return (v, None)

def back_low(kept, grad):
    return (low(grad),)
low.defvjp(low_keep, low_pass)
low_back.defvjp(back_keep, back_low)
norm_epsilon = 1e-05
masked_score = -1e+30

def layer_norm(values, gain, shift):
    center = values - lax.optimization_barrier(jnp.mean(values, axis=-1, keepdims=True))
    spread = lax.optimization_barrier(jnp.mean(center * center, axis=-1, keepdims=True))
    return center * lax.rsqrt(spread + norm_epsilon) * gain + shift

def rotary(values, positions):
    half_rot = ROT // 2
    inv_freq = 10000.0 ** (-(jnp.arange(half_rot, dtype=jnp.float32) * 2.0) / ROT)
    angles = positions.astype(jnp.float32)[:, None] * inv_freq[None, :]
    cosine = jnp.cos(angles)[:, None, :]
    sine = jnp.sin(angles)[:, None, :]
    first_half = values[..., :half_rot]
    second_half = values[..., half_rot:ROT]
    return jnp.concatenate([first_half * cosine - second_half * sine, second_half * cosine + first_half * sine, values[..., ROT:]], axis=-1)

def attend(queries, keys, values):
    block_rows = math.gcd(LEN, 512)
    count_blocks = LEN // block_rows
    score_scale = HD ** (-0.5)
    key_pos = jnp.arange(LEN, dtype=jnp.int32)

    def one_block(block_index):
        first_row = (block_index * block_rows).astype(jnp.int32)
        query_block = lax.dynamic_slice_in_dim(queries, first_row, block_rows, 0)
        scores = jnp.einsum('qhd,khd->hqk', query_block, keys, precision=lax.Precision.HIGHEST) * score_scale
        scores = low_back(scores)
        query_pos = first_row + jnp.arange(block_rows, dtype=jnp.int32)
        causal = query_pos[:, None] >= key_pos[None, :]
        scores = jnp.where(causal[None], scores, masked_score)
        probs = jax.nn.softmax(scores, axis=-1)
        return jnp.einsum('hqk,khd->qhd', low(probs), values, precision=lax.Precision.HIGHEST)
    blocks = lax.map(jax.checkpoint(one_block), jnp.arange(count_blocks, dtype=jnp.int32))
    return blocks.reshape(LEN, H, HD)

def forward(tokens_seq, qkv_weight, qkv_bias, out_weight, out_bias, up_weight, up_bias, down_weight, down_bias, attn_gain, attn_shift, mlp_gain, mlp_shift):
    highest = lax.Precision.HIGHEST
    normed_attn = low(layer_norm(tokens_seq, attn_gain, attn_shift))
    normed_mlp = low(layer_norm(tokens_seq, mlp_gain, mlp_shift))
    projected = low_back(jnp.dot(normed_attn, qkv_weight, precision=highest) + qkv_bias)
    positions = jnp.arange(LEN, dtype=jnp.int32)
    queries = low(rotary(projected[:, :D].reshape(LEN, H, HD), positions))
    keys = low(rotary(projected[:, D:2 * D].reshape(LEN, H, HD), positions))
    values = low(projected[:, 2 * D:].reshape(LEN, H, HD))
    mixed = attend(queries, keys, values).reshape(LEN, D)
    mixed = low_back(low(mixed))
    attn_branch = jnp.dot(mixed, out_weight, precision=highest) + out_bias
    hidden = low_back(jnp.dot(normed_mlp, up_weight, precision=highest) + up_bias)
    activated = low(jax.nn.gelu(hidden, approximate=False))
    mlp_branch = jnp.dot(activated, down_weight.T, precision=highest) + down_bias
    return tokens_seq + attn_branch + mlp_branch

def reference(tokens, qkv_weight, qkv_bias, out_weight, out_bias, up_weight, up_bias, down_weight, down_bias, attn_norm_gain, attn_norm_bias, mlp_norm_gain, mlp_norm_bias, cotangent):
    params = tuple((member.astype(jnp.float32) for member in (qkv_weight, qkv_bias, out_weight, out_bias, up_weight, up_bias, down_weight, down_bias, attn_norm_gain, attn_norm_bias, mlp_norm_gain, mlp_norm_bias)))

    def one_sequence(totals, inputs):
        tokens_seq, cotangent_seq = inputs
        result, pullback = jax.vjp(forward, tokens_seq, *params)
        grads = pullback(cotangent_seq)
        new_totals = jax.tree.map(lambda summed, addend: summed + addend, totals, tuple(grads[1:]))
        return (new_totals, (result.astype(jnp.bfloat16), grads[0]))
    start_totals = tuple((jnp.zeros_like(member) for member in params))
    totals, outputs = lax.scan(one_sequence, start_totals, (tokens.astype(jnp.float32), cotangent.astype(jnp.float32)))
    output, tokens_grad = outputs
    return (output, tokens_grad, totals[0], totals[1], totals[2], totals[3], totals[4], totals[5], totals[6], totals[7], totals[8], totals[9], totals[10], totals[11])
```

```python
import jax
import jax.numpy as jnp
from jax import lax
from jax.sharding import PartitionSpec as P

H = 8
HD = 256
ROT = 64
AXES = ("ctx", "shard")

norm_epsilon = 1e-05
masked_score = -1e30
contract_last = (((1,), (1,)), ((), ()))
contract_first = (((0,), (0,)), ((), ()))


def dot32(left, right, dims=(((1,), (0,)), ((), ()))):
    return lax.dot_general(left, right, dims, preferred_element_type=jnp.float32)


def normalize(values):
    center = values - jnp.mean(values, axis=-1, keepdims=True)
    spread = jnp.mean(center * center, axis=-1, keepdims=True)
    scale = lax.rsqrt(spread + norm_epsilon)
    return center * scale, scale


def rotary(values, positions):
    half_rot = ROT // 2
    inv_freq = 10000.0 ** (-(jnp.arange(half_rot, dtype=jnp.float32) * 2.0) / ROT)
    angles = positions.astype(jnp.float32)[:, None] * inv_freq[None, :]
    cosine = jnp.cos(angles)
    sine = jnp.sin(angles)
    first_half = values[:, :half_rot]
    second_half = values[:, half_rot:ROT]
    return jnp.concatenate(
        [
            first_half * cosine - second_half * sine,
            second_half * cosine + first_half * sine,
            values[:, ROT:],
        ],
        axis=-1,
    )


def exact_gelu(values):
    return jax.nn.gelu(values, approximate=False)


class Layout:
    def __init__(self, mesh):
        self.nz = mesh.shape["shard"]
        self.nc = mesh.shape["ctx"]
        self.nlo = self.nz
        self.nhi = self.nc // self.nlo
        assert self.nhi == 2 and self.nz * self.nhi == self.nc
        self.bits = [1 << b for b in range(self.nlo.bit_length() - 1)]
        assert 1 << len(self.bits) == self.nlo
        self.seq_of_lo = [
            lo // 2 if lo % 2 == 0 else self.nz - 1 - lo // 2 for lo in range(self.nlo)
        ]
        self.lo_of_seq = [self.seq_of_lo.index(s) for s in range(self.nz)]

    def flat(self, z, hi, lo):
        return (hi * self.nlo + lo) * self.nz + z

    def permute(self, value, pairs):
        return lax.ppermute(
            value, AXES, [(self.flat(*a), self.flat(*b)) for a, b in pairs]
        )

    def everywhere(self, where_to):
        pairs = []
        for z in range(self.nz):
            for hi in range(self.nhi):
                for lo in range(self.nlo):
                    pairs.append(((z, hi, lo), where_to(z, hi, lo)))
        return pairs

    def swap_lo(self, value, bit):
        return self.permute(value, self.everywhere(lambda z, hi, lo: (z, hi, lo ^ bit)))

    def swap_hi(self, value):
        return self.permute(value, self.everywhere(lambda z, hi, lo: (z, 1 - hi, lo)))

    def shift_z(self, value, by):
        return self.permute(
            value, self.everywhere(lambda z, hi, lo: ((z + by) % self.nz, hi, lo))
        )

    def in_plane(self, j):
        pairs = []
        for z in range(self.nz):
            home = self.lo_of_seq[z]
            for hi in range(self.nhi):
                pairs.append(((z, hi, home ^ j), (z, hi, home)))
        return pairs

    def chain(self):
        steps = [[] for _ in range(self.nz - 1)]
        for lo in range(self.nlo):
            s = self.seq_of_lo[lo]
            late = 1 if s < self.nz - 1 else 0
            for hi in range(self.nhi):
                for k in range(self.nz - 1 - s):
                    steps[k].append(((s + k, hi, lo), (s + k + 1, hi, lo)))
                for k in range(s):
                    steps[k + late].append(((s - k, hi, lo), (s - k - 1, hi, lo)))
        return steps


def lookup(table, index):
    return jnp.asarray(table, jnp.int32)[index]


def local_block(
    lay,
    tokens,
    qkv_weight,
    qkv_bias,
    out_weight,
    out_bias,
    up_weight,
    up_bias,
    down_weight,
    down_bias,
    attn_norm_gain,
    attn_norm_bias,
    mlp_norm_gain,
    mlp_norm_bias,
    cotangent,
):
    f32, bf16 = jnp.float32, jnp.bfloat16
    nz, nlo, nhi = lay.nz, lay.nlo, lay.nhi
    ranks = nz * nhi
    rows = tokens.shape[1]
    width = tokens.shape[2]
    hidden_width = up_weight.shape[1]
    weight_rows = qkv_weight.shape[0]
    half = nlo * rows
    ctx = lax.axis_index("ctx")
    z = lax.axis_index("shard")
    hi, lo = ctx // nlo, ctx % nlo
    rank = z * nhi + hi
    ff = hidden_width // ranks
    repeat = max(1, ranks // H)
    head = rank // repeat
    score_scale = HD ** (-0.5)
    steps = lay.chain()

    def received(step):
        table = [0] * (nz * nhi * nlo)
        for _, target in steps[step]:
            table[lay.flat(*target)] = 1
        return lookup(table, ctx * nz + z) > 0

    def gather_sequence(block):
        parts = [block] + [lay.permute(block, lay.in_plane(j)) for j in range(1, nlo)]
        current = jnp.concatenate(parts, axis=0)
        for k in range(nz - 1):
            arrived = lay.permute(current, steps[k])
            current = jnp.where(received(k), arrived, current)
        return jnp.concatenate([current, lay.swap_hi(current)], axis=0)

    def reduce_sequence(partial):
        other = lay.swap_hi(partial[half:].astype(bf16))
        current = (partial[:half] + other.astype(f32)).astype(bf16)
        for k in reversed(range(nz - 1)):
            arrived = lay.permute(current, [(b, a) for a, b in steps[k]])
            current = (current.astype(f32) + arrived.astype(f32)).astype(bf16)
        home = lookup(lay.lo_of_seq, z)
        mine = jnp.where(lo == home, current[:rows].astype(f32), 0.0)
        for j in range(1, nlo):
            block = current[j * rows : (j + 1) * rows]
            arrived = lay.permute(block, [(b, a) for a, b in lay.in_plane(j)])
            mine = mine + arrived.astype(f32)
        return mine

    quarter = weight_rows // nlo

    def gather_weight(columns_of):
        pieces = []
        for by in range(1, nz):
            target = ((z + by) % nz) * nhi + hi
            pieces.append(lay.shift_z(columns_of(target, lo * quarter, quarter), by))
        held = jnp.stack(pieces)[:, None]
        for bit in reversed(lay.bits):
            other = lay.swap_lo(held, bit)
            first = (lo & bit) == 0
            held = jnp.concatenate(
                [jnp.where(first, held, other), jnp.where(first, other, held)], axis=1
            )
        order = [0]
        for bit in reversed(lay.bits):
            order = [v for v in order] + [v + bit for v in order]
        inverse = [order.index(v) for v in range(nlo)]
        held = held[:, jnp.asarray(inverse)] if inverse != list(range(nlo)) else held
        held = held.reshape(nz - 1, weight_rows, -1)
        mine = columns_of(rank, 0, weight_rows)
        stack = jnp.concatenate([mine[None], held], axis=0)
        return jnp.concatenate(
            [
                lax.dynamic_index_in_dim(stack, (z - k) % nz, 0, keepdims=False)
                for k in range(nz)
            ],
            axis=0,
        )

    def qkv_columns(of_rank, row, count):
        first = (of_rank // repeat) * HD
        return jnp.concatenate(
            [
                lax.dynamic_slice(qkv_weight, (row, part * width + first), (count, HD))
                for part in range(3)
            ],
            axis=1,
        )

    def up_columns(of_rank, row, count):
        return lax.dynamic_slice(up_weight, (row, of_rank * ff), (count, ff))

    def down_columns(of_rank, row, count):
        return lax.dynamic_slice(down_weight, (row, of_rank * ff), (count, ff))

    own = tokens[0]
    own_cotangent = cotangent[0]
    seq_tokens = gather_sequence(own)
    qkv_here = gather_weight(qkv_columns)
    up_here = gather_weight(up_columns)
    seq_cotangent = gather_sequence(own_cotangent)
    down_here = gather_weight(down_columns)
    out_head = lax.dynamic_slice(out_weight, (head * HD - z * weight_rows, 0), (HD, width))
    out_rows = width // ranks
    out_at = rank * out_rows - head * HD

    block_index = lo ^ jnp.arange(nlo, dtype=jnp.int32)
    within = (block_index[:, None] * rows + jnp.arange(rows, dtype=jnp.int32)[None, :]).reshape(-1)
    positions = jnp.concatenate([hi * half + within, (1 - hi) * half + within])

    normed, _ = normalize(seq_tokens.astype(f32))
    attn_in = (normed * attn_norm_gain + attn_norm_bias).astype(bf16)
    mlp_in = (normed * mlp_norm_gain + mlp_norm_bias).astype(bf16)
    bias_here = jnp.concatenate(
        [lax.dynamic_slice(qkv_bias, (part * width + head * HD,), (HD,)) for part in range(3)]
    )
    projected = dot32(attn_in, qkv_here) + bias_here
    queries = rotary(projected[:, :HD], positions).astype(bf16)
    keys = rotary(projected[:, HD : 2 * HD], positions).astype(bf16)
    values = projected[:, 2 * HD :].astype(bf16)
    causal = positions[:, None] >= positions[None, :]
    scores = jnp.where(causal, dot32(queries, keys, contract_last) * score_scale, masked_score)
    top = jnp.max(scores, axis=-1, keepdims=True)
    weights = jnp.where(causal, jnp.exp(scores - top), 0.0)
    total = jnp.sum(weights, axis=-1, keepdims=True)
    mixed_full = dot32(weights.astype(bf16), values) / total
    log_total = top + jnp.log(total)
    mixed = mixed_full.astype(bf16)
    mixed_mine = lax.dynamic_slice(mixed, (0, out_at), (mixed.shape[0], out_rows))
    out_mine = lax.dynamic_slice(out_head, (out_at, 0), (out_rows, width))
    hidden = dot32(mlp_in, up_here) + lax.dynamic_slice(up_bias, (rank * ff,), (ff,))
    activated_full, gelu_pull = jax.vjp(exact_gelu, hidden)
    activated = activated_full.astype(bf16)
    out_partial = dot32(mixed_mine, out_mine) + dot32(activated, down_here, contract_last)
    summed_out = reduce_sequence(out_partial)
    output = (own.astype(f32) + summed_out + (out_bias + down_bias)).astype(bf16)[None]

    down_grad = dot32(seq_cotangent, activated, contract_first)
    out_grad = dot32(mixed_mine, seq_cotangent, contract_first)
    grad_hidden = gelu_pull(dot32(seq_cotangent, down_here))[0].astype(bf16)
    up_grad = dot32(mlp_in, grad_hidden, contract_first)
    grad_mixed = dot32(seq_cotangent, out_head, contract_last).astype(bf16)
    row_dot = jnp.sum(grad_mixed.astype(f32) * mixed_full, axis=-1, keepdims=True)
    probs = jnp.where(causal, jnp.exp(scores - log_total), 0.0)
    grad_values = dot32(probs.astype(bf16), grad_mixed, contract_first)
    grad_probs = dot32(grad_mixed, values, contract_last)
    grad_scores = (probs * (grad_probs - row_dot)).astype(bf16)
    grad_queries = dot32(grad_scores, keys) * score_scale
    grad_keys = dot32(grad_scores, queries, contract_first) * score_scale
    grad_projected = jnp.concatenate(
        [rotary(grad_queries, -positions), rotary(grad_keys, -positions), grad_values], axis=1
    ).astype(bf16)
    qkv_grad = dot32(attn_in, grad_projected, contract_first)
    grad_attn_in = dot32(grad_projected, qkv_here, contract_last) * (1.0 / repeat)
    grad_mlp_in = dot32(grad_hidden, up_here, contract_last)
    summed_in = reduce_sequence(grad_attn_in * attn_norm_gain + grad_mlp_in * mlp_norm_gain)
    own_normed, own_scale = normalize(own.astype(f32))
    input_grad = own_scale * (
        summed_in
        - jnp.mean(summed_in, axis=-1, keepdims=True)
        - own_normed * jnp.mean(summed_in * own_normed, axis=-1, keepdims=True)
    )
    tokens_grad = (own_cotangent.astype(f32) + input_grad)[None]

    first_copy = jnp.where(rank % repeat == 0, 1.0, 0.0)
    qkv_bias_part = jnp.sum(grad_projected.astype(f32), axis=0) * first_copy
    qkv_bias_full = jnp.zeros((3, width), f32)
    qkv_bias_full = lax.dynamic_update_slice(
        qkv_bias_full, qkv_bias_part.reshape(3, HD), (0, head * HD)
    ).reshape(-1)
    up_bias_full = lax.dynamic_update_slice(
        jnp.zeros((hidden_width,), f32),
        jnp.sum(grad_hidden.astype(f32), axis=0),
        (rank * ff,),
    )
    small = lax.psum(
        jnp.concatenate(
            [
                qkv_bias_full,
                up_bias_full,
                jnp.sum(own_cotangent.astype(f32), axis=0),
                jnp.sum(grad_attn_in * normed, axis=0),
                jnp.sum(grad_attn_in, axis=0),
                jnp.sum(grad_mlp_in * normed, axis=0),
                jnp.sum(grad_mlp_in, axis=0),
            ]
        ),
        AXES,
    )
    cuts = [3 * width, hidden_width, width, width, width, width, width]
    small_parts, at = [], 0
    for size in cuts:
        small_parts.append(small[at : at + size])
        at += size

    grain = width // (lay.nc * nz)

    def scatter_weight(partial):
        cols = partial.shape[1]
        held = partial.astype(bf16).reshape((nhi,) + (2,) * len(lay.bits) + (nz, grain, cols))
        for bit in lay.bits:
            axis = len(held.shape) - 4
            which = jnp.where((lo & bit) == 0, 0, 1)
            send = lax.dynamic_index_in_dim(held, 1 - which, axis, keepdims=False)
            keep = lax.dynamic_index_in_dim(held, which, axis, keepdims=False)
            held = (keep.astype(f32) + lay.swap_lo(send, bit).astype(f32)).astype(bf16)
        pieces = [lax.dynamic_index_in_dim(held, z, 1, keepdims=False)]
        for by in range(1, nz):
            pieces.append(
                lay.shift_z(
                    lax.dynamic_index_in_dim(held, (z + by) % nz, 1, keepdims=False), by
                )
            )
        stack = jnp.stack(pieces)
        other = lay.swap_hi(lax.dynamic_index_in_dim(stack, 1 - hi, 1, keepdims=False))
        keep = lax.dynamic_index_in_dim(stack, hi, 1, keepdims=False)
        result = []
        for k in range(nz):
            a = lax.dynamic_index_in_dim(keep, (z - k) % nz, 0, keepdims=False)
            b = lax.dynamic_index_in_dim(other, (z - k) % nz, 0, keepdims=False)
            result.append(jnp.where(hi == 0, a, b))
            result.append(jnp.where(hi == 0, b, a))
        return jnp.stack(result).astype(f32)

    down_all = scatter_weight(down_grad)
    up_all = scatter_weight(up_grad)
    qkv_all = scatter_weight(qkv_grad)[::repeat]
    down_weight_grad = jnp.transpose(down_all, (1, 0, 2)).reshape(grain, hidden_width)
    up_weight_grad = jnp.transpose(up_all, (1, 0, 2)).reshape(grain, hidden_width)
    qkv_weight_grad = jnp.transpose(
        qkv_all.reshape(H, grain, 3, HD), (1, 2, 0, 3)
    ).reshape(grain, 3 * width)

    held = out_grad.astype(bf16).reshape((2,) * len(lay.bits) + (grain, width))
    for bit in lay.bits:
        axis = len(held.shape) - 3
        which = jnp.where((lo & bit) == 0, 0, 1)
        send = lax.dynamic_index_in_dim(held, 1 - which, axis, keepdims=False)
        keep = lax.dynamic_index_in_dim(held, which, axis, keepdims=False)
        held = (keep.astype(f32) + lay.swap_lo(send, bit).astype(f32)).astype(bf16)
    pairs = []
    for zz in range(nz):
        for h in range(nhi):
            for l in range(nlo):
                owner = zz * nhi + h
                pairs.append(((zz, h, l), (l, owner // nlo, owner % nlo)))
    out_weight_grad = lay.permute(held, pairs).astype(f32)

    return (
        output,
        tokens_grad,
        qkv_weight_grad,
        small_parts[0],
        out_weight_grad,
        small_parts[2],
        up_weight_grad,
        small_parts[1],
        down_weight_grad,
        small_parts[2],
        small_parts[3],
        small_parts[4],
        small_parts[5],
        small_parts[6],
    )


def solution(mesh):
    lay = Layout(mesh)

    def local(*args):
        return local_block(lay, *args)

    sharded = P("shard", "ctx", None)
    by_rows = P("shard", None)
    owned = P(("ctx", "shard"), None)
    in_specs = (
        sharded, by_rows, P(), by_rows, P(), by_rows, P(), by_rows, P(),
        P(), P(), P(), P(), sharded,
    )
    out_specs = (
        sharded, sharded, owned, P(), owned, P(), owned, P(), owned,
        P(), P(), P(), P(), P(),
    )
    return jax.shard_map(
        local, mesh=mesh, in_specs=in_specs, out_specs=out_specs, check_vma=False
    )
```

```python
import functools

import jax
import jax.numpy as jnp
from jax import lax
from jax.experimental import pallas as pl
from jax.experimental.pallas import tpu as pltpu
from jax.sharding import PartitionSpec as P

H = 8
HD = 256
ROT = 64
AXES = ("ctx", "shard")
MESH = pl.DeviceIdType.MESH

norm_epsilon = 1e-05
masked_score = -1e30
contract_last = (((1,), (1,)), ((), ()))
contract_first = (((0,), (0,)), ((), ()))


def dot32(left, right, dims=(((1,), (0,)), ((), ()))):
    return lax.dot_general(left, right, dims, preferred_element_type=jnp.float32)


def normalize(values):
    center = values - jnp.mean(values, axis=-1, keepdims=True)
    spread = jnp.mean(center * center, axis=-1, keepdims=True)
    scale = lax.rsqrt(spread + norm_epsilon)
    return center * scale, scale


def rotary(values, positions):
    half_rot = ROT // 2
    inv_freq = 10000.0 ** (-(jnp.arange(half_rot, dtype=jnp.float32) * 2.0) / ROT)
    angles = positions.astype(jnp.float32)[:, None] * inv_freq[None, :]
    cosine = jnp.cos(angles)
    sine = jnp.sin(angles)
    first_half = values[:, :half_rot]
    second_half = values[:, half_rot:ROT]
    return jnp.concatenate(
        [
            first_half * cosine - second_half * sine,
            second_half * cosine + first_half * sine,
            values[:, ROT:],
        ],
        axis=-1,
    )


def exact_gelu(values):
    return jax.nn.gelu(values, approximate=False)


class Layout:
    def __init__(self, mesh):
        self.nz = mesh.shape["shard"]
        self.nc = mesh.shape["ctx"]
        self.nlo = self.nz
        self.nhi = self.nc // self.nlo
        assert self.nhi == 2 and self.nz * self.nhi == self.nc
        self.bits = [1 << b for b in range(self.nlo.bit_length() - 1)]
        assert 1 << len(self.bits) == self.nlo
        self.seq_of_lo = [
            lo // 2 if lo % 2 == 0 else self.nz - 1 - lo // 2 for lo in range(self.nlo)
        ]
        self.lo_of_seq = [self.seq_of_lo.index(s) for s in range(self.nz)]

    def flat(self, z, hi, lo):
        return (hi * self.nlo + lo) * self.nz + z


def flip(value, mask, count):
    bit = 1
    while bit < count:
        if mask & bit:
            value = value + bit - 2 * bit * ((value // bit) % 2)
        bit *= 2
    return value


def low_bit(mask):
    return mask & -mask


def place(lay):
    ctx = lax.axis_index("ctx")
    z = lax.axis_index("shard")
    return z, ctx // lay.nlo, ctx % lay.nlo


def remote(src, dst, send, recv, device):
    return pltpu.make_async_remote_copy(
        src_ref=src, dst_ref=dst, send_sem=send, recv_sem=recv, device_id=device, device_id_type=MESH
    )


def enter(devices):
    barrier = pltpu.get_barrier_semaphore()
    for device in devices:
        pl.semaphore_signal(barrier, inc=1, device_id=device, device_id_type=MESH)
    pl.semaphore_wait(barrier, len(devices))


def gather_schedule(order_w, nlo, by_bit, n_groups):
    w = [("W", g, i) for g, i in order_w]
    arrive = [("E", g, i, 0) for g, i in order_w]
    last = [("E", g, i, r) for r in by_bit for g, i in order_w]

    def tokens(a):
        events = [("D", a, 0)]
        for k in range(1, nlo):
            events += [("Z", a, k), ("D", a, k)]
        return events

    first, second = tokens(0), tokens(1)
    events = [("N", 0)] + first[:3] + [("N", 1)] + first[3:]
    k = 0
    for item in second:
        events += [item] + arrive[k : k + 2]
        k += 2
    events += arrive[k:] + last
    window, start = 3, 4
    schedule, k = [], window
    for n, item in enumerate(events):
        if n == start:
            schedule += w[:window]
        schedule.append(item)
        if item[0] == "E" and item[3] == 0 and k < len(w):
            schedule.append(w[k])
            k += 1
    return schedule


def gather_kernel(lay, sizes, tok, cot, qkv, up, down, seq_t, seq_c, w_qkv, w_up, w_down, stage_t, stage_c,
                  near_r, near_s, home_c, z_r, z_s, y_r, y_s, wz_r, wz_s, wf_r, wf_s):
    rows, width, weight_rows, ff, repeat = sizes
    nz, nlo, nhi = lay.nz, lay.nlo, lay.nhi
    z, hi, lo = place(lay)
    half, quarter = nlo * rows, weight_rows // nlo
    odd = lo % 2
    s = (1 - odd) * (lo // 2) + odd * (nz - 1 - lo // 2)

    def dev(z, hi, lo):
        return (hi * nlo + lo, z)

    enter(
        [dev((z + i) % nz, hi, lo) for i in range(1, nz)]
        + [dev(z, hi, flip(lo, r, nlo)) for r in range(1, nlo)]
        + [dev(z, 1 - hi, lo)]
    )

    groups = []
    for part in range(3):
        groups.append((qkv, w_qkv, lambda rank, part=part: part * width + (rank // repeat) * HD, part * HD, HD))
    groups.append((up, w_up, lambda rank: rank * ff, 0, ff))
    groups.append((down, w_down, lambda rank: rank * ff, 0, ff))
    bits = list(reversed(lay.bits))

    def weight_z(g, i):
        src, dst, column, at, wide = groups[g]
        to = (z + i) % nz
        first = pl.multiple_of(column(to * nhi + hi), 128)
        return remote(
            src.at[pl.ds(pl.multiple_of(lo * quarter, quarter), quarter), pl.ds(first, wide)],
            dst.at[pl.ds(pl.multiple_of(z * weight_rows + lo * quarter, quarter), quarter), pl.ds(at, wide)],
            wz_s.at[g, i - 1], wz_r.at[g, i - 1], dev(to, hi, lo),
        )

    def weight_forward(g, i, r, b):
        _, dst, _, at, wide = groups[g]
        row = ((z + nz - i) % nz) * weight_rows + flip(lo, r, nlo) * quarter
        piece = dst.at[pl.ds(pl.multiple_of(row, quarter), quarter), pl.ds(at, wide)]
        k = bits.index(b)
        return remote(piece, piece, wf_s.at[g, i - 1, r, k], wf_r.at[g, i - 1, r ^ b], dev(z, hi, flip(lo, b, nlo)))

    inputs, staged, sequences = (tok, cot), (stage_t, stage_c), (seq_t, seq_c)
    distance = jnp.abs(z - s)

    def home_of(seq):
        late = seq // (nz // 2)
        return (1 - late) * (2 * seq) + late * (2 * (nz - 1 - seq) + 1)

    def seq_rows(a, which, r):
        row = which * half + flip(lo, r, nlo) * rows
        return sequences[a].at[pl.ds(pl.multiple_of(row, rows), rows)]

    def along(a, src, seq, way):
        return remote(src, staged[a].at[seq], z_s.at[a, seq, way], z_r.at[a, seq], dev((z + 1 - 2 * way + nz) % nz, hi, lo))

    def near(a, src, seq):
        return remote(src, seq_rows(a, hi, 0), near_s.at[a, seq], near_r.at[a, lo], dev(z, hi, home_of(seq)))

    def near_arrival(a, r):
        piece = seq_rows(a, hi, r)
        return remote(piece, piece, near_s.at[a, 0], near_r.at[a, flip(lo, r, nlo)], dev(z, hi, flip(lo, r, nlo)))

    def stay(a, src):
        return pltpu.make_async_copy(src, seq_rows(a, hi, 0), home_c.at[a])

    def across(a, src, r):
        return remote(src, seq_rows(a, hi, r), y_s.at[a, r], y_r.at[a, r], dev(z, 1 - hi, lo))

    def across_arrival(a, r):
        piece = seq_rows(a, 1 - hi, r)
        return remote(piece, piece, y_s.at[a, r], y_r.at[a, r], dev(z, 1 - hi, lo))

    def sources(a):
        yield (z >= 0, inputs[a], z, z < nz - 1, z > 0)
        for k in range(1, nz):
            yield (z >= k, staged[a].at[(z + nz - k) % nz], (z + nz - k) % nz, z < nz - 1, z < 0)
            yield (z < nz - k, staged[a].at[(z + k) % nz], (z + k) % nz, z < 0, z > 0)

    def dispatch(a, which):
        valid, src, seq, up, down = list(sources(a))[which]

        @pl.when(valid & up)
        def _():
            along(a, src, seq, 0).start()

        @pl.when(valid & down)
        def _():
            along(a, src, seq, 1).start()

        @pl.when(valid & (lo == home_of(seq)))
        def _():
            across(a, src, 0).start()
            stay(a, src).start()

        @pl.when(valid & (lo != home_of(seq)))
        def _():
            near(a, src, seq).start()

    def settle(a, which):
        valid, src, seq, up, down = list(sources(a))[which]

        @pl.when(valid & up)
        def _():
            along(a, src, seq, 0).wait_send()

        @pl.when(valid & down)
        def _():
            along(a, src, seq, 1).wait_send()

        @pl.when(valid & (lo == home_of(seq)))
        def _():
            across(a, src, 0).wait_send()
            stay(a, src).wait()

        @pl.when(valid & (lo != home_of(seq)))
        def _():
            near(a, src, seq).wait_send()

    def chain_event(a, k):
        for which, valid, seq in ((2 * k - 1, z >= k, (z + nz - k) % nz), (2 * k, z < nz - k, (z + k) % nz)):
            @pl.when(valid)
            def _(seq=seq):
                along(a, staged[a].at[seq], seq, 0).wait_recv()

            dispatch(a, which)

    def near_event(a, d):
        @pl.when(distance == d)
        def _():
            for r in range(1, nlo):
                near_arrival(a, r).wait_recv()
                across(a, seq_rows(a, hi, r), r).start()

    def forward_from(g, i, r):
        for b in bits:
            if r == 0 or b < low_bit(r):
                weight_forward(g, i, r, b).start()

    def weight_event(g, i, r):
        if r == 0:
            weight_z(g, i).wait_recv()
        else:
            weight_forward(g, i, r ^ low_bit(r), low_bit(r)).wait_recv()
        forward_from(g, i, r)

    order_w = [(g, i) for g in range(len(groups)) for i in range(1, nz)]
    by_bit = sorted(range(1, nlo), key=lambda r: -low_bit(r))
    act = dict(N=lambda a: dispatch(a, 0), Z=chain_event, D=near_event, W=lambda g, i: weight_z(g, i).start(), E=weight_event)
    for item in gather_schedule(order_w, nlo, by_bit, len(groups)):
        act[item[0]](*item[1:])
    for a in range(2):
        for j in range(nlo):
            across_arrival(a, j).wait_recv()
    for g, i in order_w:
        weight_z(g, i).wait_send()
        for r in range(nlo):
            for b in bits:
                if r == 0 or b < low_bit(r):
                    weight_forward(g, i, r, b).wait_send()
    for a in range(2):
        for which in range(2 * nz - 1):
            settle(a, which)
        for r in range(1, nlo):
            across(a, seq_rows(a, hi, r), r).wait_send()


def gather_all(lay, tok, cot, qkv, up, down):
    rows, width = tok.shape
    nz, nlo = lay.nz, lay.nlo
    ranks = nz * lay.nhi
    ff = up.shape[1] // ranks
    repeat = max(1, ranks // H)
    sizes = (rows, width, qkv.shape[0], ff, repeat)
    bits = len(lay.bits)
    anywhere = pl.BlockSpec(memory_space=pl.ANY)
    dma = pltpu.SemaphoreType.DMA
    bf16 = jnp.bfloat16
    total = 2 * nlo * rows
    return pl.pallas_call(
        functools.partial(gather_kernel, lay, sizes),
        out_shape=[
            jax.ShapeDtypeStruct((total, width), bf16),
            jax.ShapeDtypeStruct((total, width), bf16),
            jax.ShapeDtypeStruct((width, 3 * HD), bf16),
            jax.ShapeDtypeStruct((width, ff), bf16),
            jax.ShapeDtypeStruct((width, ff), bf16),
            jax.ShapeDtypeStruct((nz, rows, width), bf16),
            jax.ShapeDtypeStruct((nz, rows, width), bf16),
        ],
        in_specs=[anywhere] * 5,
        out_specs=[anywhere] * 7,
        scratch_shapes=[
            dma((2, nlo)), dma((2, nz)), dma((2,)), dma((2, nz)), dma((2, nz, 2)), dma((2, nlo)), dma((2, nlo)),
            dma((5, nz - 1)), dma((5, nz - 1)), dma((5, nz - 1, nlo)), dma((5, nz - 1, nlo, bits)),
        ],
        compiler_params=pltpu.CompilerParams(collective_id=1, has_side_effects=True),
        name="gather_all",
    )(tok, cot, qkv, up, down)[:5]

def add_rows(into, left, right, step):
    rows = into.shape[0]
    step = min(step, rows)

    def body(k, carry):
        at = pl.ds(pl.multiple_of(k * step, step), step)
        into[at, :] = (left[at, :].astype(jnp.float32) + right[at, :].astype(jnp.float32)).astype(into.dtype)
        return carry

    lax.fori_loop(0, rows // step, body, 0)


def scatter_chunks(width, ff, repeat):
    cut = max(ff // 2, 256)
    chunks = []
    for source in (0, 1):
        for first in range(0, ff, cut):
            chunks.append((source, first, cut, lambda rank, first=first: rank * ff + first, True))
    for part in range(3):
        chunks.append((2, part * HD, HD, lambda rank, part=part: part * width + (rank // repeat) * HD, repeat == 1))
    return chunks


def scatter_schedule(nz, nlo, n_chunks, stages):
    schedule = [("Y", 0), ("M",), ("P",)] + [("C", g) for g in range(n_chunks)] + [("Y", 1)]
    schedule += [("X", g, 0) for g in range(3)]
    schedule += [("A", 0, q) for q in range(nlo)]
    schedule += [("X", g, 0) for g in range(3, n_chunks)]
    schedule += [("X", g, 1) for g in range(2)]
    chain = []
    for a in range(2):
        part = []
        for m in range(nz):
            if m < nz - 1:
                part.append(("B", a, nz - 1 - m, 0))
            if m < nz - 1:
                part.append(("B", a, m, 1))
        chain.append(part + [("F", a)])
    schedule += chain[0]
    schedule += [("A", 1, q) for q in range(nlo)]
    schedule += [("X", g, 1) for g in range(2, n_chunks)]
    schedule += chain[1]
    for t in range(2, stages):
        schedule += [("X", g, t) for g in range(n_chunks)]
    schedule += [("Q", t) for t in range(stages)] + [("N", t) for t in range(2 * stages + 1)]
    schedule += [("G", g) for g in range(n_chunks)]
    return schedule


def scatter_kernel(lay, sizes, *refs):
    rows, width, ff, repeat = sizes
    nz, nlo, nhi = lay.nz, lay.nlo, lay.nhi
    stages = len(lay.bits)
    chunks = scatter_chunks(width, ff, repeat)
    n = len(chunks)
    refs = list(refs)

    def take(count):
        taken = refs[:count]
        del refs[:count]
        return taken

    partial_o, partial_s, wg_down, wg_up, wg_qkv, wg_out, small = take(7)
    sum_o, sum_s, all_down, all_up, all_qkv, all_out, small_sum = take(7)
    own, across_buf, near_buf, up_buf, down_buf = take(5)
    acc = take(n)
    got = [take(stages) for _ in range(n)]
    out_acc, = take(1)
    out_got = take(stages)
    small_buf, small_got = take(2)
    (own_c, y_r, y_s, near_r, near_s, z_r, z_s, acc_c, st_r, st_s, g_r, g_s, keep_c,
     out_c, out_r, out_s, move_r, move_s, sm_r, sm_s) = take(20)

    z, hi, lo = place(lay)
    rank = z * nhi + hi
    half = nlo * rows
    grain = width // (nz * nhi * nlo)
    span = nz * grain

    def dev(z, hi, lo):
        return (hi * nlo + lo, z)

    ctx = hi * nlo + lo
    moves = (ctx != rank) | (z != lo)
    barrier = pltpu.get_barrier_semaphore()
    mates = [
        dev((z + dz) % nz, flip(hi, dh, nhi), lo) for dz in range(nz) for dh in range(nhi) if dz or dh
    ] + [dev(z, hi, flip(lo, r, nlo)) for r in range(1, nlo)]
    for device in mates:
        pl.semaphore_signal(barrier, inc=1, device_id=device, device_id_type=MESH)

    @pl.when(moves)
    def _():
        pl.semaphore_signal(barrier, inc=1, device_id=(rank, lo), device_id_type=MESH)
        pl.semaphore_signal(barrier, inc=1, device_id=dev(ctx // nhi, ctx % nhi, z), device_id_type=MESH)
        pl.semaphore_wait(barrier, len(mates) + 2)

    @pl.when(jnp.logical_not(moves))
    def _():
        pl.semaphore_wait(barrier, len(mates))

    partial, summed = (partial_o, partial_s), (sum_o, sum_s)

    def load_own(a):
        row = pl.multiple_of(hi * half, half)
        return pltpu.make_async_copy(
            partial[a].at[pl.ds(row, half)], own.at[a], own_c.at[a]
        )

    def across(a, q):
        row = pl.multiple_of((1 - hi) * half + q * rows, rows)
        return remote(
            partial[a].at[pl.ds(row, rows)], across_buf.at[a, q], y_s.at[a, q], y_r.at[a, q], dev(z, 1 - hi, lo)
        )

    def near(a, q):
        return remote(
            own.at[a, pl.ds(q * rows, rows)], near_buf.at[a, lo], near_s.at[a, q], near_r.at[a, lo], dev(z, hi, q)
        )

    def near_arrival(a, q):
        piece = near_buf.at[a, q]
        return remote(piece, piece, near_s.at[a, q], near_r.at[a, q], dev(z, hi, q))

    def along(a, seq, way):
        buf = (up_buf, down_buf)[way]
        return remote(
            near_buf.at[a, lay.lo_of_seq[seq]], buf.at[a, seq], z_s.at[a, seq], z_r.at[a, seq, way],
            dev((z + 1 - 2 * way + nz) % nz, hi, lo),
        )

    def start_across(a):
        load_own(a).start()
        for q in range(nlo):
            across(a, q).start()

    def across_event(a, q):
        if q == 0:
            load_own(a).wait()
        across(a, q).wait_recv()
        mine = own.at[a, pl.ds(q * rows, rows)]

        @pl.when(lo == q)
        def _():
            add_rows(near_buf.at[a, q], mine, across_buf.at[a, q], 16)

        @pl.when(lo != q)
        def _():
            add_rows(mine, mine, across_buf.at[a, q], 16)
            near(a, q).start()

    def chain_event(a, seq, way):
        q = lay.lo_of_seq[seq]
        active = (z < seq) if way == 0 else (z > seq)
        first = (z == 0) if way == 0 else (z == nz - 1)
        buf = (up_buf, down_buf)[way]

        @pl.when(active)
        def _():
            @pl.when(lo != q)
            def _():
                near_arrival(a, q).wait_recv()

            @pl.when(jnp.logical_not(first))
            def _():
                along(a, seq, way).wait_recv()
                add_rows(near_buf.at[a, q], near_buf.at[a, q], buf.at[a, seq], 16)

            along(a, seq, way).start()

    def final_event(a):
        late = z // (nz // 2)
        home = (1 - late) * (2 * z) + late * (2 * (nz - 1 - z) + 1)
        piece = near_buf.at[a, home]

        @pl.when(lo != home)
        def _():
            remote(piece, piece, near_s.at[a, 0], near_r.at[a, home], dev(z, hi, home)).wait_recv()

        @pl.when(z > 0)
        def _():
            arrived = up_buf.at[a, z]
            remote(arrived, arrived, z_s.at[a, 0], z_r.at[a, z, 0], dev(z, hi, lo)).wait_recv()

        @pl.when(z < nz - 1)
        def _():
            arrived = down_buf.at[a, z]
            remote(arrived, arrived, z_s.at[a, 0], z_r.at[a, z, 1], dev(z, hi, lo)).wait_recv()

        def body(k, carry):
            at = pl.ds(pl.multiple_of(k * 16, 16), 16)
            total = piece[at, :].astype(jnp.float32)
            total = total + jnp.where(z > 0, up_buf[a, z, at, :].astype(jnp.float32), 0.0)
            total = total + jnp.where(z < nz - 1, down_buf[a, z, at, :].astype(jnp.float32), 0.0)
            summed[a][at, :] = total
            return carry

        lax.fori_loop(0, rows // 16, body, 0)

    sources = (wg_down, wg_up, wg_qkv)
    targets = (all_down, all_up, all_qkv)

    def rows_of(g, h, rel):
        source, first, wide, _, _ = chunks[g]
        row = (h * nlo + flip(lo, rel, nlo)) * span
        return sources[source].at[pl.ds(pl.multiple_of(row, span), span), pl.ds(first, wide)]

    def load_acc(g, h, rel):
        return pltpu.make_async_copy(rows_of(g, h, rel), acc[g].at[h, rel // 2], acc_c.at[g, h, rel // 2])

    def stage_pieces(t):
        return [rel for rel in range(nlo) if rel % (2 << t) == (1 << t)]

    def stage_send(g, t, h, rel):
        src = rows_of(g, h, rel) if t == 0 else acc[g].at[h, rel // 2]
        k = rel >> (t + 1)
        return remote(
            src, got[g][t].at[h, k], st_s.at[g, t, h, k], st_r.at[g, t, h, k], dev(z, hi, flip(lo, 1 << t, nlo))
        )

    def stage_start(g, t):
        for h in range(nhi):
            for rel in stage_pieces(t):
                stage_send(g, t, h, rel).start()

    def start_chunk(g):
        stage_start(g, 0)
        for h in range(nhi):
            for rel in range(0, nlo, 2):
                load_acc(g, h, rel).start()

    def stage_event(g, t):
        order = list(reversed(range(0, nlo, 2 << t)))
        for h in range(nhi):
            for rel in order:
                k = rel >> (t + 1)
                if t == 0:
                    load_acc(g, h, rel).wait()
                stage_send(g, t, h, rel | (1 << t)).wait_recv()
                add_rows(acc[g].at[h, rel // 2], acc[g].at[h, rel // 2], got[g][t].at[h, k], 64)
                if t + 1 < stages and rel % (4 << t) == (2 << t):
                    stage_send(g, t + 1, h, rel).start()
        if t + 1 == stages:
            deliver(g)

    def owner_send(g, dz, dh):
        source, _, wide, column, _ = chunks[g]
        to_z, to_hi = (z + dz) % nz, flip(hi, dh, nhi)
        first = pl.multiple_of(column(rank), 128)
        k = dz * nhi + dh
        return remote(
            acc[g].at[to_hi, 0, pl.ds(pl.multiple_of(to_z * grain, grain), grain)],
            targets[source].at[:, pl.ds(first, wide)],
            g_s.at[g, k], g_r.at[g, k], dev(to_z, to_hi, lo),
        )

    def owner_arrival(g, dz, dh):
        source, _, wide, column, _ = chunks[g]
        from_z, from_hi = (z + nz - dz) % nz, flip(hi, dh, nhi)
        first = pl.multiple_of(column(from_z * nhi + from_hi), 128)
        piece = targets[source].at[:, pl.ds(first, wide)]
        k = dz * nhi + dh
        return remote(piece, piece, g_s.at[g, k], g_r.at[g, k], dev(from_z, from_hi, lo))

    def keep(g):
        source, _, wide, column, _ = chunks[g]
        first = pl.multiple_of(column(rank), 128)
        return pltpu.make_async_copy(
            acc[g].at[hi, 0, pl.ds(pl.multiple_of(z * grain, grain), grain)],
            targets[source].at[:, pl.ds(first, wide)], keep_c.at[g],
        )

    others = [(dz, dh) for dz in range(nz) for dh in range(nhi) if dz or dh]

    def when_sent(g, from_hi, act):
        if chunks[g][4]:
            act()
        else:
            pl.when(from_hi % repeat == 0)(act)

    def deliver(g):
        def act():
            for dz, dh in others:
                owner_send(g, dz, dh).start()
            keep(g).start()

        when_sent(g, hi, act)

    def finish_chunk(g):
        def sent():
            for dz, dh in others:
                owner_send(g, dz, dh).wait_send()
            keep(g).wait()

        when_sent(g, hi, sent)
        for dz, dh in others:
            when_sent(g, flip(hi, dh, nhi), lambda dz=dz, dh=dh: owner_arrival(g, dz, dh).wait_recv())

    def out_rows(rel):
        return wg_out.at[pl.ds(pl.multiple_of(flip(lo, rel, nlo) * grain, grain), grain)]

    def out_load(rel):
        return pltpu.make_async_copy(out_rows(rel), out_acc.at[rel // 2], out_c.at[rel // 2])

    def out_send(t, rel):
        src = out_rows(rel) if t == 0 else out_acc.at[rel // 2]
        k = rel >> (t + 1)
        return remote(src, out_got[t].at[k], out_s.at[t, k], out_r.at[t, k], dev(z, hi, flip(lo, 1 << t, nlo)))

    def out_start():
        for rel in stage_pieces(0):
            out_send(0, rel).start()
        for rel in range(0, nlo, 2):
            out_load(rel).start()

    def out_event(t):
        for rel in reversed(range(0, nlo, 2 << t)):
            if t == 0:
                out_load(rel).wait()
            out_send(t, rel | (1 << t)).wait_recv()
            add_rows(out_acc.at[rel // 2], out_acc.at[rel // 2], out_got[t].at[rel >> (t + 1)], 16)
            if t + 1 < stages and rel % (4 << t) == (2 << t):
                out_send(t + 1, rel).start()
        if t + 1 == stages:
            @pl.when(moves)
            def _():
                out_move().start()

            @pl.when(jnp.logical_not(moves))
            def _():
                out_stay().start()

    def out_move():
        return remote(out_acc.at[0], all_out, move_s, move_r, (rank, lo))

    def out_stay():
        return pltpu.make_async_copy(out_acc.at[0], all_out, move_s)

    doubling = (
        [dev(z, hi, flip(lo, b, nlo)) for b in lay.bits]
        + [dev(z, flip(hi, 1, nhi), lo)]
        + [dev(flip(z, b, nz), hi, lo) for b in lay.bits]
    )

    def small_send(t):
        src = small if t == 0 else small_buf.at[t - 1]
        return remote(src, small_got.at[t], sm_s.at[t], sm_r.at[t], doubling[t])

    def small_event(t):
        small_send(t).wait_recv()
        mine = small if t == 0 else small_buf.at[t - 1]
        into = small_sum if t + 1 == len(doubling) else small_buf.at[t]
        into[...] = mine[...] + small_got[t]
        if t + 1 < len(doubling):
            small_send(t + 1).start()

    act = dict(
        Y=start_across, A=across_event, B=chain_event, F=final_event, C=start_chunk, X=stage_event, G=finish_chunk,
        P=out_start, Q=out_event, M=lambda: small_send(0).start(), N=small_event,
    )
    for item in scatter_schedule(nz, nlo, n, stages):
        act[item[0]](*item[1:])

    for a in range(2):
        for q in range(nlo):
            across(a, q).wait_send()

            @pl.when(lo != q)
            def _(a=a, q=q):
                near(a, q).wait_send()

        for seq in range(nz):
            @pl.when(z != seq)
            def _(a=a, seq=seq):
                along(a, seq, 0).wait_send()

    for g in range(n):
        for t in range(stages):
            for h in range(nhi):
                for rel in stage_pieces(t):
                    stage_send(g, t, h, rel).wait_send()
    for t in range(stages):
        for rel in stage_pieces(t):
            out_send(t, rel).wait_send()

    @pl.when(moves)
    def _():
        out_move().wait()

    @pl.when(jnp.logical_not(moves))
    def _():
        out_stay().wait()

    for t in range(len(doubling)):
        small_send(t).wait_send()


def scatter_all(lay, partial_o, partial_s, wg_down, wg_up, wg_qkv, wg_out, small):
    total, width = partial_o.shape
    nz, nlo, nhi = lay.nz, lay.nlo, lay.nhi
    rows = total // (nhi * nlo)
    ranks = nz * nhi
    ff = wg_down.shape[1]
    repeat = max(1, ranks // H)
    grain = width // (ranks * nlo)
    span = nz * grain
    stages = len(lay.bits)
    chunks = scatter_chunks(width, ff, repeat)
    n = len(chunks)
    steps = 2 * stages + 1
    anywhere = pl.BlockSpec(memory_space=pl.ANY)
    inside = pl.BlockSpec(memory_space=pltpu.VMEM)
    dma = pltpu.SemaphoreType.DMA
    bf16, f32 = jnp.bfloat16, jnp.float32
    scratch = [
        pltpu.VMEM((2, nlo * rows, width), bf16),
        pltpu.VMEM((2, nlo, rows, width), bf16),
        pltpu.VMEM((2, nlo, rows, width), bf16),
        pltpu.VMEM((2, nz, rows, width), bf16),
        pltpu.VMEM((2, nz, rows, width), bf16),
    ]
    for chunk in chunks:
        scratch.append(pltpu.VMEM((nhi, nlo // 2, span, chunk[2]), bf16))
    for chunk in chunks:
        for t in range(stages):
            scratch.append(pltpu.VMEM((nhi, nlo >> (t + 1), span, chunk[2]), bf16))
    scratch.append(pltpu.VMEM((nlo // 2, grain, width), bf16))
    for t in range(stages):
        scratch.append(pltpu.VMEM((nlo >> (t + 1), grain, width), bf16))
    scratch += [pltpu.VMEM((steps,) + small.shape, f32), pltpu.VMEM((steps,) + small.shape, f32)]
    most = nlo // 2
    scratch += [
        dma((2,)), dma((2, nlo)), dma((2, nlo)), dma((2, nlo)), dma((2, nlo)), dma((2, nz, 2)), dma((2, nz)),
        dma((n, nhi, most)), dma((n, stages, nhi, most)), dma((n, stages, nhi, most)), dma((n, ranks)), dma((n, ranks)),
        dma((n,)), dma((most,)), dma((stages, most)), dma((stages, most)), dma, dma, dma((steps,)), dma((steps,)),
    ]
    return pl.pallas_call(
        functools.partial(scatter_kernel, lay, (rows, width, ff, repeat)),
        out_shape=[
            jax.ShapeDtypeStruct((rows, width), f32),
            jax.ShapeDtypeStruct((rows, width), f32),
            jax.ShapeDtypeStruct((grain, ff * ranks), bf16),
            jax.ShapeDtypeStruct((grain, ff * ranks), bf16),
            jax.ShapeDtypeStruct((grain, 3 * width), bf16),
            jax.ShapeDtypeStruct((grain, width), bf16),
            jax.ShapeDtypeStruct(small.shape, f32),
        ],
        in_specs=[anywhere] * 6 + [inside],
        out_specs=[inside, inside, anywhere, anywhere, anywhere, anywhere, inside],
        scratch_shapes=scratch,
        compiler_params=pltpu.CompilerParams(
            collective_id=2, has_side_effects=True, vmem_limit_bytes=60 * 1024 * 1024
        ),
        name="scatter_all",
    )(partial_o, partial_s, wg_down, wg_up, wg_qkv, wg_out, small)


def local_block(
    lay,
    tokens,
    qkv_weight,
    qkv_bias,
    out_weight,
    out_bias,
    up_weight,
    up_bias,
    down_weight,
    down_bias,
    attn_norm_gain,
    attn_norm_bias,
    mlp_norm_gain,
    mlp_norm_bias,
    cotangent,
):
    f32, bf16 = jnp.float32, jnp.bfloat16
    nz, nlo, nhi = lay.nz, lay.nlo, lay.nhi
    ranks = nz * nhi
    rows = tokens.shape[1]
    width = tokens.shape[2]
    hidden_width = up_weight.shape[1]
    weight_rows = qkv_weight.shape[0]
    half = nlo * rows
    ctx = lax.axis_index("ctx")
    z = lax.axis_index("shard")
    hi, lo = ctx // nlo, ctx % nlo
    rank = z * nhi + hi
    ff = hidden_width // ranks
    repeat = max(1, ranks // H)
    head = rank // repeat
    score_scale = HD ** (-0.5)
    own = tokens[0]
    own_cotangent = cotangent[0]
    seq_tokens, seq_cotangent, qkv_here, up_here, down_here = gather_all(
        lay, own, own_cotangent, qkv_weight, up_weight, down_weight
    )
    own_qkv = jnp.concatenate(
        [
            lax.dynamic_slice(qkv_weight, (0, part * width + head * HD), (weight_rows, HD))
            for part in range(3)
        ],
        axis=1,
    )
    own_up = lax.dynamic_slice(up_weight, (0, rank * ff), (weight_rows, ff))
    own_down = lax.dynamic_slice(down_weight, (0, rank * ff), (weight_rows, ff))
    qkv_here = lax.dynamic_update_slice(qkv_here, own_qkv, (z * weight_rows, 0))
    up_here = lax.dynamic_update_slice(up_here, own_up, (z * weight_rows, 0))
    down_here = lax.dynamic_update_slice(down_here, own_down, (z * weight_rows, 0))
    out_head = lax.dynamic_slice(out_weight, (head * HD - z * weight_rows, 0), (HD, width))
    out_rows = width // ranks
    out_at = rank * out_rows - head * HD

    positions = jnp.arange(2 * half, dtype=jnp.int32)

    normed, _ = normalize(seq_tokens.astype(f32))
    attn_in = (normed * attn_norm_gain + attn_norm_bias).astype(bf16)
    mlp_in = (normed * mlp_norm_gain + mlp_norm_bias).astype(bf16)
    bias_here = jnp.concatenate(
        [lax.dynamic_slice(qkv_bias, (part * width + head * HD,), (HD,)) for part in range(3)]
    )
    projected = dot32(attn_in, qkv_here) + bias_here
    queries = rotary(projected[:, :HD], positions).astype(bf16)
    keys = rotary(projected[:, HD : 2 * HD], positions).astype(bf16)
    values = projected[:, 2 * HD :].astype(bf16)
    causal = positions[:, None] >= positions[None, :]
    scores = jnp.where(causal, dot32(queries, keys, contract_last) * score_scale, masked_score)
    top = jnp.max(scores, axis=-1, keepdims=True)
    weights = jnp.where(causal, jnp.exp(scores - top), 0.0)
    total = jnp.sum(weights, axis=-1, keepdims=True)
    mixed_full = dot32(weights.astype(bf16), values) / total
    log_total = top + jnp.log(total)
    mixed = mixed_full.astype(bf16)
    mixed_mine = lax.dynamic_slice(mixed, (0, out_at), (mixed.shape[0], out_rows))
    out_mine = lax.dynamic_slice(out_head, (out_at, 0), (out_rows, width))
    hidden = dot32(mlp_in, up_here) + lax.dynamic_slice(up_bias, (rank * ff,), (ff,))
    activated_full, gelu_pull = jax.vjp(exact_gelu, hidden)
    activated = activated_full.astype(bf16)
    out_partial = dot32(mixed_mine, out_mine) + dot32(activated, down_here, contract_last)
    down_grad = dot32(seq_cotangent, activated, contract_first)
    out_grad = dot32(mixed_mine, seq_cotangent, contract_first)
    grad_hidden = gelu_pull(dot32(seq_cotangent, down_here))[0].astype(bf16)
    up_grad = dot32(mlp_in, grad_hidden, contract_first)
    grad_mixed = dot32(seq_cotangent, out_head, contract_last).astype(bf16)
    row_dot = jnp.sum(grad_mixed.astype(f32) * mixed_full, axis=-1, keepdims=True)
    probs = jnp.where(causal, jnp.exp(scores - log_total), 0.0)
    grad_values = dot32(probs.astype(bf16), grad_mixed, contract_first)
    grad_probs = dot32(grad_mixed, values, contract_last)
    grad_scores = (probs * (grad_probs - row_dot)).astype(bf16)
    grad_queries = dot32(grad_scores, keys) * score_scale
    grad_keys = dot32(grad_scores, queries, contract_first) * score_scale
    grad_projected = jnp.concatenate(
        [rotary(grad_queries, -positions), rotary(grad_keys, -positions), grad_values], axis=1
    ).astype(bf16)
    qkv_grad = dot32(attn_in, grad_projected, contract_first)
    grad_attn_in = dot32(grad_projected, qkv_here, contract_last) * (1.0 / repeat)
    grad_mlp_in = dot32(grad_hidden, up_here, contract_last)
    in_partial = grad_attn_in * attn_norm_gain + grad_mlp_in * mlp_norm_gain

    first_copy = jnp.where(rank % repeat == 0, 1.0, 0.0)
    qkv_bias_part = jnp.sum(grad_projected.astype(f32), axis=0) * first_copy
    qkv_bias_full = jnp.zeros((3, width), f32)
    qkv_bias_full = lax.dynamic_update_slice(
        qkv_bias_full, qkv_bias_part.reshape(3, HD), (0, head * HD)
    ).reshape(-1)
    up_bias_full = lax.dynamic_update_slice(
        jnp.zeros((hidden_width,), f32),
        jnp.sum(grad_hidden.astype(f32), axis=0),
        (rank * ff,),
    )
    small = jnp.concatenate(
        [
            qkv_bias_full,
            up_bias_full,
            jnp.sum(own_cotangent.astype(f32), axis=0),
            jnp.sum(grad_attn_in * normed, axis=0),
            jnp.sum(grad_attn_in, axis=0),
            jnp.sum(grad_mlp_in * normed, axis=0),
            jnp.sum(grad_mlp_in, axis=0),
        ]
    ).reshape(-1, 128)
    summed_out, summed_in, all_down, all_up, all_qkv, all_out, small = scatter_all(
        lay,
        out_partial.astype(bf16),
        in_partial.astype(bf16),
        down_grad.astype(bf16),
        up_grad.astype(bf16),
        qkv_grad.astype(bf16),
        out_grad.astype(bf16),
        small,
    )
    output = (own.astype(f32) + summed_out + (out_bias + down_bias)).astype(bf16)[None]
    own_normed, own_scale = normalize(own.astype(f32))
    input_grad = own_scale * (
        summed_in
        - jnp.mean(summed_in, axis=-1, keepdims=True)
        - own_normed * jnp.mean(summed_in * own_normed, axis=-1, keepdims=True)
    )
    tokens_grad = (own_cotangent.astype(f32) + input_grad)[None]

    small = small.reshape(-1)
    cuts = [3 * width, hidden_width, width, width, width, width, width]
    small_parts, at = [], 0
    for size in cuts:
        small_parts.append(small[at : at + size])
        at += size

    qkv_weight_grad = all_qkv.astype(f32)
    out_weight_grad = all_out.astype(f32)
    up_weight_grad = all_up.astype(f32)
    down_weight_grad = all_down.astype(f32)
    return (
        output,
        tokens_grad,
        qkv_weight_grad,
        small_parts[0],
        out_weight_grad,
        small_parts[2],
        up_weight_grad,
        small_parts[1],
        down_weight_grad,
        small_parts[2],
        small_parts[3],
        small_parts[4],
        small_parts[5],
        small_parts[6],
    )


def solution(mesh):
    lay = Layout(mesh)

    def local(*args):
        return local_block(lay, *args)

    sharded = P("shard", "ctx", None)
    by_rows = P("shard", None)
    owned = P(("ctx", "shard"), None)
    in_specs = (
        sharded, by_rows, P(), by_rows, P(), by_rows, P(), by_rows, P(),
        P(), P(), P(), P(), sharded,
    )
    out_specs = (
        sharded, sharded, owned, P(), owned, P(), owned, P(), owned,
        P(), P(), P(), P(), P(),
    )
    return jax.shard_map(
        local, mesh=mesh, in_specs=in_specs, out_specs=out_specs, check_vma=False
    )
```

```python
import functools

import jax
import jax.numpy as jnp
from jax import lax
from jax.experimental import pallas as pl
from jax.experimental.pallas import tpu as pltpu
from jax.sharding import PartitionSpec as P

H = 8
HD = 256
ROT = 64
AXES = ("ctx", "shard")
MESH = pl.DeviceIdType.MESH

norm_epsilon = 1e-05
masked_score = -1e30
contract_last = (((1,), (1,)), ((), ()))
contract_first = (((0,), (0,)), ((), ()))


def dot32(left, right, dims=(((1,), (0,)), ((), ()))):
    return lax.dot_general(left, right, dims, preferred_element_type=jnp.float32)


def normalize(values):
    center = values - jnp.mean(values, axis=-1, keepdims=True)
    spread = jnp.mean(center * center, axis=-1, keepdims=True)
    scale = lax.rsqrt(spread + norm_epsilon)
    return center * scale, scale


def rotary(values, positions):
    half_rot = ROT // 2
    inv_freq = 10000.0 ** (-(jnp.arange(half_rot, dtype=jnp.float32) * 2.0) / ROT)
    angles = positions.astype(jnp.float32)[:, None] * inv_freq[None, :]
    cosine = jnp.cos(angles)
    sine = jnp.sin(angles)
    first_half = values[:, :half_rot]
    second_half = values[:, half_rot:ROT]
    return jnp.concatenate(
        [
            first_half * cosine - second_half * sine,
            second_half * cosine + first_half * sine,
            values[:, ROT:],
        ],
        axis=-1,
    )


def exact_gelu(values):
    return jax.nn.gelu(values, approximate=False)


class Layout:
    def __init__(self, mesh):
        self.nz = mesh.shape["shard"]
        self.nc = mesh.shape["ctx"]
        self.nlo = self.nz
        self.nhi = self.nc // self.nlo
        assert self.nhi == 2 and self.nz * self.nhi == self.nc
        self.bits = [1 << b for b in range(self.nlo.bit_length() - 1)]
        assert 1 << len(self.bits) == self.nlo
        self.seq_of_lo = [
            lo // 2 if lo % 2 == 0 else self.nz - 1 - lo // 2 for lo in range(self.nlo)
        ]
        self.lo_of_seq = [self.seq_of_lo.index(s) for s in range(self.nz)]

    def flat(self, z, hi, lo):
        return (hi * self.nlo + lo) * self.nz + z


def flip(value, mask, count):
    bit = 1
    while bit < count:
        if mask & bit:
            value = value + bit - 2 * bit * ((value // bit) % 2)
        bit *= 2
    return value


def low_bit(mask):
    return mask & -mask


def place(lay):
    ctx = lax.axis_index("ctx")
    z = lax.axis_index("shard")
    return z, ctx // lay.nlo, ctx % lay.nlo


def remote(src, dst, send, recv, device):
    return pltpu.make_async_remote_copy(
        src_ref=src, dst_ref=dst, send_sem=send, recv_sem=recv, device_id=device, device_id_type=MESH
    )


def enter(devices):
    barrier = pltpu.get_barrier_semaphore()
    for device in devices:
        pl.semaphore_signal(barrier, inc=1, device_id=device, device_id_type=MESH)
    pl.semaphore_wait(barrier, len(devices))


def gather_schedule(order_w, nlo, by_bit, n_groups):
    w = [("W", g, i) for g, i in order_w]
    arrive = [("E", g, i, 0) for g, i in order_w]
    last = [("E", g, i, r) for r in by_bit for g, i in order_w]

    def tokens(a):
        events = [("D", a, 0)]
        for k in range(1, nlo):
            events += [("Z", a, k), ("D", a, k)]
        return events

    first, second = tokens(0), tokens(1)
    events = [("N", 0)] + first[:3] + [("N", 1)] + first[3:]
    k = 0
    for item in second:
        events += [item] + arrive[k : k + 2]
        k += 2
    events += arrive[k:] + last
    window, start = 3, 4
    schedule, k = [], window
    for n, item in enumerate(events):
        if n == start:
            schedule += w[:window]
        schedule.append(item)
        if item[0] == "E" and item[3] == 0 and k < len(w):
            schedule.append(w[k])
            k += 1
    return schedule


def gather_kernel(lay, sizes, tok, cot, qkv, up, down, seq_t, seq_c, w_qkv, w_up, w_down, stage_t, stage_c,
                  near_r, near_s, home_c, z_r, z_s, y_r, y_s, wz_r, wz_s, wf_r, wf_s):
    rows, width, weight_rows, ff, repeat = sizes
    nz, nlo, nhi = lay.nz, lay.nlo, lay.nhi
    z, hi, lo = place(lay)
    half, quarter = nlo * rows, weight_rows // nlo
    odd = lo % 2
    s = (1 - odd) * (lo // 2) + odd * (nz - 1 - lo // 2)

    def dev(z, hi, lo):
        return (hi * nlo + lo, z)

    enter(
        [dev((z + i) % nz, hi, lo) for i in range(1, nz)]
        + [dev(z, hi, flip(lo, r, nlo)) for r in range(1, nlo)]
        + [dev(z, 1 - hi, lo)]
    )

    groups = []
    for part in range(3):
        groups.append((qkv, w_qkv, lambda rank, part=part: part * width + (rank // repeat) * HD, part * HD, HD))
    groups.append((up, w_up, lambda rank: rank * ff, 0, ff))
    groups.append((down, w_down, lambda rank: rank * ff, 0, ff))
    bits = list(reversed(lay.bits))

    def weight_z(g, i):
        src, dst, column, at, wide = groups[g]
        to = (z + i) % nz
        first = pl.multiple_of(column(to * nhi + hi), 128)
        return remote(
            src.at[pl.ds(pl.multiple_of(lo * quarter, quarter), quarter), pl.ds(first, wide)],
            dst.at[pl.ds(pl.multiple_of(z * weight_rows + lo * quarter, quarter), quarter), pl.ds(at, wide)],
            wz_s.at[g, i - 1], wz_r.at[g, i - 1], dev(to, hi, lo),
        )

    def weight_forward(g, i, r, b):
        _, dst, _, at, wide = groups[g]
        row = ((z + nz - i) % nz) * weight_rows + flip(lo, r, nlo) * quarter
        piece = dst.at[pl.ds(pl.multiple_of(row, quarter), quarter), pl.ds(at, wide)]
        k = bits.index(b)
        return remote(piece, piece, wf_s.at[g, i - 1, r, k], wf_r.at[g, i - 1, r ^ b], dev(z, hi, flip(lo, b, nlo)))

    inputs, staged, sequences = (tok, cot), (stage_t, stage_c), (seq_t, seq_c)
    distance = jnp.abs(z - s)

    def home_of(seq):
        late = seq // (nz // 2)
        return (1 - late) * (2 * seq) + late * (2 * (nz - 1 - seq) + 1)

    def seq_rows(a, which, r):
        row = which * half + flip(lo, r, nlo) * rows
        return sequences[a].at[pl.ds(pl.multiple_of(row, rows), rows)]

    def along(a, src, seq, way):
        return remote(src, staged[a].at[seq], z_s.at[a, seq, way], z_r.at[a, seq], dev((z + 1 - 2 * way + nz) % nz, hi, lo))

    def near(a, src, seq):
        return remote(src, seq_rows(a, hi, 0), near_s.at[a, seq], near_r.at[a, lo], dev(z, hi, home_of(seq)))

    def near_arrival(a, r):
        piece = seq_rows(a, hi, r)
        return remote(piece, piece, near_s.at[a, 0], near_r.at[a, flip(lo, r, nlo)], dev(z, hi, flip(lo, r, nlo)))

    def stay(a, src):
        return pltpu.make_async_copy(src, seq_rows(a, hi, 0), home_c.at[a])

    def across(a, src, r):
        return remote(src, seq_rows(a, hi, r), y_s.at[a, r], y_r.at[a, r], dev(z, 1 - hi, lo))

    def across_arrival(a, r):
        piece = seq_rows(a, 1 - hi, r)
        return remote(piece, piece, y_s.at[a, r], y_r.at[a, r], dev(z, 1 - hi, lo))

    def sources(a):
        yield (z >= 0, inputs[a], z, z < nz - 1, z > 0)
        for k in range(1, nz):
            yield (z >= k, staged[a].at[(z + nz - k) % nz], (z + nz - k) % nz, z < nz - 1, z < 0)
            yield (z < nz - k, staged[a].at[(z + k) % nz], (z + k) % nz, z < 0, z > 0)

    def dispatch(a, which):
        valid, src, seq, up, down = list(sources(a))[which]

        @pl.when(valid & up)
        def _():
            along(a, src, seq, 0).start()

        @pl.when(valid & down)
        def _():
            along(a, src, seq, 1).start()

        @pl.when(valid & (lo == home_of(seq)))
        def _():
            across(a, src, 0).start()
            stay(a, src).start()

        @pl.when(valid & (lo != home_of(seq)))
        def _():
            near(a, src, seq).start()

    def settle(a, which):
        valid, src, seq, up, down = list(sources(a))[which]

        @pl.when(valid & up)
        def _():
            along(a, src, seq, 0).wait_send()

        @pl.when(valid & down)
        def _():
            along(a, src, seq, 1).wait_send()

        @pl.when(valid & (lo == home_of(seq)))
        def _():
            across(a, src, 0).wait_send()
            stay(a, src).wait()

        @pl.when(valid & (lo != home_of(seq)))
        def _():
            near(a, src, seq).wait_send()

    def chain_event(a, k):
        for which, valid, seq in ((2 * k - 1, z >= k, (z + nz - k) % nz), (2 * k, z < nz - k, (z + k) % nz)):
            @pl.when(valid)
            def _(seq=seq):
                along(a, staged[a].at[seq], seq, 0).wait_recv()

            dispatch(a, which)

    def near_event(a, d):
        @pl.when(distance == d)
        def _():
            for r in range(1, nlo):
                near_arrival(a, r).wait_recv()
                across(a, seq_rows(a, hi, r), r).start()

    def forward_from(g, i, r):
        for b in bits:
            if r == 0 or b < low_bit(r):
                weight_forward(g, i, r, b).start()

    def weight_event(g, i, r):
        if r == 0:
            weight_z(g, i).wait_recv()
        else:
            weight_forward(g, i, r ^ low_bit(r), low_bit(r)).wait_recv()
        forward_from(g, i, r)

    order_w = [(g, i) for g in range(len(groups)) for i in range(1, nz)]
    by_bit = sorted(range(1, nlo), key=lambda r: -low_bit(r))
    act = dict(N=lambda a: dispatch(a, 0), Z=chain_event, D=near_event, W=lambda g, i: weight_z(g, i).start(), E=weight_event)
    for item in gather_schedule(order_w, nlo, by_bit, len(groups)):
        act[item[0]](*item[1:])
    for a in range(2):
        for j in range(nlo):
            across_arrival(a, j).wait_recv()
    for g, i in order_w:
        weight_z(g, i).wait_send()
        for r in range(nlo):
            for b in bits:
                if r == 0 or b < low_bit(r):
                    weight_forward(g, i, r, b).wait_send()
    for a in range(2):
        for which in range(2 * nz - 1):
            settle(a, which)
        for r in range(1, nlo):
            across(a, seq_rows(a, hi, r), r).wait_send()


def gather_all(lay, tok, cot, qkv, up, down):
    rows, width = tok.shape
    nz, nlo = lay.nz, lay.nlo
    ranks = nz * lay.nhi
    ff = up.shape[1] // ranks
    repeat = max(1, ranks // H)
    sizes = (rows, width, qkv.shape[0], ff, repeat)
    bits = len(lay.bits)
    anywhere = pl.BlockSpec(memory_space=pl.ANY)
    dma = pltpu.SemaphoreType.DMA
    bf16 = jnp.bfloat16
    total = 2 * nlo * rows
    return pl.pallas_call(
        functools.partial(gather_kernel, lay, sizes),
        out_shape=[
            jax.ShapeDtypeStruct((total, width), bf16),
            jax.ShapeDtypeStruct((total, width), bf16),
            jax.ShapeDtypeStruct((width, 3 * HD), bf16),
            jax.ShapeDtypeStruct((width, ff), bf16),
            jax.ShapeDtypeStruct((width, ff), bf16),
            jax.ShapeDtypeStruct((nz, rows, width), bf16),
            jax.ShapeDtypeStruct((nz, rows, width), bf16),
        ],
        in_specs=[anywhere] * 5,
        out_specs=[anywhere] * 7,
        scratch_shapes=[
            dma((2, nlo)), dma((2, nz)), dma((2,)), dma((2, nz)), dma((2, nz, 2)), dma((2, nlo)), dma((2, nlo)),
            dma((5, nz - 1)), dma((5, nz - 1)), dma((5, nz - 1, nlo)), dma((5, nz - 1, nlo, bits)),
        ],
        compiler_params=pltpu.CompilerParams(collective_id=1, has_side_effects=True),
        name="gather_all",
    )(tok, cot, qkv, up, down)[:5]

def turn(values, cosine, sine):
    left = values[:, :128]
    lane = lax.broadcasted_iota(jnp.int32, left.shape, 1)
    swapped = jnp.where(lane < ROT // 2, pltpu.roll(left, 128 - ROT // 2, 1), pltpu.roll(left, ROT // 2, 1))
    return jnp.concatenate([left * cosine + swapped * sine, values[:, 128:]], axis=1)


def block_schedule(order_w, nlo, by_bit, n_groups, blocks, n_short):
    timed = [(t, ("N", a)) for a, t in ((0, -9), (1, 10))]
    timed += [(-5, ("WO",))]
    for a, (first, step) in enumerate(((12, 12), (40, 12))):
        timed.append((first - 1, ("D", a, 0)))
        for k in range(1, nlo):
            timed.append((first + step * (k - 1), ("Z", a, k)))
            timed.append((first + step * (k - 1) + 8, ("D", a, k)))
    sizes = [1, 1, 1, 4, 4]
    sent = 0.0
    for g, i in order_w:
        timed.append((20 + 2.5 * sent, ("W", g, i)))
        timed.append((20 + 2.5 * sent + 20, ("E", g, i, 0)))
        for r in by_bit:
            timed.append((20 + 2.5 * sent + 20 + (20 if low_bit(r) > 1 else 20 + 8), ("E", g, i, r)))
        sent += sizes[g]
    after = {}

    def put(name, time, item):
        timed.append((time, item))
        after[name] = max(after.get(name, 0), time) + 0.01

    ready = [max(t for t, item in timed if item[0] == "E" and item[1] == g) for g in range(n_groups)]
    seen = [max(t for t, item in timed if item[0] == "D" and item[1] == a) for a in range(2)]
    put("H", max(50, seen[0] + 0.1), ("H", 0))
    put("H", max(70, after["H"]), ("H", 1))
    put("CO", max(100, seen[1] + 0.1, after["H"]), ("CO",))
    for k in range(blocks):
        put("K", max(after["H"], max(ready[:3])) + 0.1 + 0.01 * k, ("K", k))
    for k in range(blocks):
        put("AF", after["K"] + 0.01 * k, ("AF", k))
    for k in range(blocks):
        put("U", max(after["AF"], ready[3]) + 0.1 + 0.01 * k, ("U", k))
    for k in range(blocks):
        put("GM", max(after["CO"], after["U"]) + 0.1 + 0.01 * k, ("GM", k))
    for k in range(blocks):
        put("AB", after["GM"] + 0.1 + 0.01 * k, ("AB", k))
    put("BP", after["AB"] + 0.1, ("BP",))
    for k in range(blocks):
        put("O", max(after["BP"], max(ready)) + 0.1 + 0.01 * k, ("O", k))
    for k in range(blocks):
        put("GH", max(after["O"], max(ready)) + 0.1 + 0.01 * k, ("GH", k))
    for k in range(n_short):
        put("S", max(after["GH"], after["BP"]) + 0.1, ("S", k))
    timed.sort(key=lambda entry: entry[0])
    return [entry[1] for entry in timed]


def block_kernel(lay, sizes, *refs):
    rows, width, weight_rows, ff = sizes
    nz, nlo, nhi = lay.nz, lay.nlo, lay.nhi
    f32, bf16 = jnp.float32, jnp.bfloat16
    refs = list(refs)

    def take(count):
        taken = refs[:count]
        del refs[:count]
        return taken

    tok, cot, qkv, up, down, out_w = take(6)
    qkv_b, up_b, gain_a, shift_a, gain_m, shift_m, cos_t, sin_t = take(8)
    seq_c_out, attn_out, mlp_out, act_out, gh_out, gp_out, mixed_out, o_out, s_out, stage_t, stage_c = take(11)
    vec_out, qkv_b_out, up_b_out = take(3)
    seq_t, seq_c, w_qkv, w_up, w_down, w_out = take(6)
    attn_in, mlp_in, q_ref, k_ref, v_ref, mixed, mixed_full, lse, slope, act, gh, gm = take(12)
    dq, dk, dv, gp, o_buf, s_buf, means, scales = take(8)
    near_r, near_s, home_c, z_r, z_s, y_r, y_s, wz_r, wz_s, wf_r, wf_s, own_c, out_c, o_c, s_c = take(15)

    z, hi, lo = place(lay)
    half, quarter = nlo * rows, weight_rows // nlo
    total = 2 * half
    rank = z * nhi + hi
    odd = lo % 2
    s = (1 - odd) * (lo // 2) + odd * (nz - 1 - lo // 2)
    score_scale = HD ** (-0.5)

    def dev(z, hi, lo):
        return (hi * nlo + lo, z)

    enter(
        [dev((z + i) % nz, hi, lo) for i in range(1, nz)]
        + [dev(z, hi, flip(lo, r, nlo)) for r in range(1, nlo)]
        + [dev(z, 1 - hi, lo)]
    )

    groups = []
    for part in range(3):
        groups.append((qkv, w_qkv, lambda rank, part=part: part * width + rank * HD, part * HD, HD))
    groups.append((up, w_up, lambda rank: rank * ff, 0, ff))
    groups.append((down, w_down, lambda rank: rank * ff, 0, ff))
    bits = list(reversed(lay.bits))

    def weight_z(g, i):
        src, dst, column, at, wide = groups[g]
        to = (z + i) % nz
        first = pl.multiple_of(column(to * nhi + hi), 128)
        return remote(
            src.at[pl.ds(pl.multiple_of(lo * quarter, quarter), quarter), pl.ds(first, wide)],
            dst.at[pl.ds(pl.multiple_of(z * weight_rows + lo * quarter, quarter), quarter), pl.ds(at, wide)],
            wz_s.at[g, i - 1], wz_r.at[g, i - 1], dev(to, hi, lo),
        )

    def weight_forward(g, i, r, b):
        _, dst, _, at, wide = groups[g]
        row = ((z + nz - i) % nz) * weight_rows + flip(lo, r, nlo) * quarter
        piece = dst.at[pl.ds(pl.multiple_of(row, quarter), quarter), pl.ds(at, wide)]
        k = bits.index(b)
        return remote(piece, piece, wf_s.at[g, i - 1, r, k], wf_r.at[g, i - 1, r ^ b], dev(z, hi, flip(lo, b, nlo)))

    inputs, staged, sequences = (tok, cot), (stage_t, stage_c), (seq_t, seq_c)
    distance = jnp.abs(z - s)

    def home_of(seq):
        late = seq // (nz // 2)
        return (1 - late) * (2 * seq) + late * (2 * (nz - 1 - seq) + 1)

    def seq_rows(a, which, r):
        row = which * half + flip(lo, r, nlo) * rows
        return sequences[a].at[pl.ds(pl.multiple_of(row, rows), rows)]

    def along(a, src, seq, way):
        return remote(src, staged[a].at[seq], z_s.at[a, seq, way], z_r.at[a, seq], dev((z + 1 - 2 * way + nz) % nz, hi, lo))

    def near(a, src, seq):
        return remote(src, seq_rows(a, hi, 0), near_s.at[a, seq], near_r.at[a, lo], dev(z, hi, home_of(seq)))

    def near_arrival(a, r):
        piece = seq_rows(a, hi, r)
        return remote(piece, piece, near_s.at[a, 0], near_r.at[a, flip(lo, r, nlo)], dev(z, hi, flip(lo, r, nlo)))

    def stay(a, src):
        return pltpu.make_async_copy(src, seq_rows(a, hi, 0), home_c.at[a])

    def across(a, src, r):
        return remote(src, seq_rows(a, hi, r), y_s.at[a, r], y_r.at[a, r], dev(z, 1 - hi, lo))

    def across_arrival(a, r):
        piece = seq_rows(a, 1 - hi, r)
        return remote(piece, piece, y_s.at[a, r], y_r.at[a, r], dev(z, 1 - hi, lo))

    def sources(a):
        yield (z >= 0, inputs[a], z, z < nz - 1, z > 0)
        for k in range(1, nz):
            yield (z >= k, staged[a].at[(z + nz - k) % nz], (z + nz - k) % nz, z < nz - 1, z < 0)
            yield (z < nz - k, staged[a].at[(z + k) % nz], (z + k) % nz, z < 0, z > 0)

    def dispatch(a, which):
        valid, src, seq, up, down = list(sources(a))[which]

        @pl.when(valid & up)
        def _():
            along(a, src, seq, 0).start()

        @pl.when(valid & down)
        def _():
            along(a, src, seq, 1).start()

        @pl.when(valid & (lo == home_of(seq)))
        def _():
            across(a, src, 0).start()
            stay(a, src).start()

        @pl.when(valid & (lo != home_of(seq)))
        def _():
            near(a, src, seq).start()

    def settle(a, which):
        valid, src, seq, up, down = list(sources(a))[which]

        @pl.when(valid & up)
        def _():
            along(a, src, seq, 0).wait_send()

        @pl.when(valid & down)
        def _():
            along(a, src, seq, 1).wait_send()

        @pl.when(valid & (lo == home_of(seq)))
        def _():
            across(a, src, 0).wait_send()

        @pl.when(valid & (lo != home_of(seq)))
        def _():
            near(a, src, seq).wait_send()

    def chain_event(a, k):
        for which, valid, seq in ((2 * k - 1, z >= k, (z + nz - k) % nz), (2 * k, z < nz - k, (z + k) % nz)):
            @pl.when(valid)
            def _(seq=seq):
                along(a, staged[a].at[seq], seq, 0).wait_recv()

            dispatch(a, which)

    def near_event(a, d):
        @pl.when(distance == d)
        def _():
            for r in range(1, nlo):
                near_arrival(a, r).wait_recv()
                across(a, seq_rows(a, hi, r), r).start()

    def forward_from(g, i, r):
        for b in bits:
            if r == 0 or b < low_bit(r):
                weight_forward(g, i, r, b).start()

    def weight_event(g, i, r):
        if r == 0:
            weight_z(g, i).wait_recv()
        else:
            weight_forward(g, i, r ^ low_bit(r), low_bit(r)).wait_recv()
        forward_from(g, i, r)

    def own_weight(g):
        if g == len(groups):
            first = pl.multiple_of(rank * HD - z * weight_rows, HD)
            return pltpu.make_async_copy(out_w.at[pl.ds(first, HD)], w_out, own_c.at[g])
        src, dst, column, at, wide = groups[g]
        first = pl.multiple_of(column(rank), 128)
        return pltpu.make_async_copy(
            src.at[:, pl.ds(first, wide)],
            dst.at[pl.ds(pl.multiple_of(z * weight_rows, weight_rows), weight_rows), pl.ds(at, wide)],
            own_c.at[g],
        )

    def own_start():
        for g in range(len(groups) + 1):
            own_weight(g).start()

    tall = 256
    blocks = total // tall
    kept = ((seq_c, seq_c_out), (attn_in, attn_out), (mlp_in, mlp_out), (act, act_out), (gh, gh_out), (gp, gp_out), (mixed, mixed_out))

    def save(k):
        return pltpu.make_async_copy(*kept[k], out_c.at[k])

    def at_block(i):
        return pl.ds(i * tall, tall)

    def norm(which):
        if which == 0:
            stay(0, tok).wait()
        else:
            for r in range(nlo):
                across_arrival(0, r).wait_recv()
        start = (hi if which == 0 else 1 - hi) * half
        step = 64

        def body(i, carry):
            at = pl.ds(pl.multiple_of(start + i * step, step), step)
            values = seq_t[at, :].astype(f32)
            mean = jnp.mean(values, axis=-1, keepdims=True)
            center = values - mean
            scale = lax.rsqrt(jnp.mean(center * center, axis=-1, keepdims=True) + norm_epsilon)
            normed = center * scale
            attn_in[at, :] = (normed * gain_a[...] + shift_a[...]).astype(bf16)
            mlp_in[at, :] = (normed * gain_m[...] + shift_m[...]).astype(bf16)
            means[at, :] = jnp.broadcast_to(mean, (step, 128))
            scales[at, :] = jnp.broadcast_to(scale, (step, 128))
            return carry

        lax.fori_loop(0, half // step, body, 0)
        if which == 1:
            save(1).start()
            save(2).start()

    def project(i):
        if i == 0:
            for g in range(3):
                own_weight(g).wait()
        at = at_block(i)
        raw = jnp.dot(attn_in[at, :], w_qkv[...], preferred_element_type=f32) + qkv_b[...]
        q_ref[at, :] = turn(raw[:, :HD], cos_t[at, :], sin_t[at, :]).astype(bf16)
        k_ref[at, :] = turn(raw[:, HD : 2 * HD], cos_t[at, :], sin_t[at, :]).astype(bf16)
        v_ref[at, :] = raw[:, 2 * HD :].astype(bf16)

    def scores_of(i):
        reach = (i + 1) * tall
        scores = dot32(q_ref[at_block(i), :], k_ref[:reach, :], contract_last) * score_scale
        row = lax.broadcasted_iota(jnp.int32, scores.shape, 0) + i * tall
        column = lax.broadcasted_iota(jnp.int32, scores.shape, 1)
        return jnp.where(row >= column, scores, masked_score), reach

    def attend(i):
        scores, reach = scores_of(i)
        top = jnp.max(scores, axis=-1, keepdims=True)
        weights = jnp.exp(scores - top)
        summed = jnp.sum(weights, axis=-1, keepdims=True)
        full = dot32(weights.astype(bf16), v_ref[:reach, :]) / summed
        at = at_block(i)
        mixed_full[at, :] = full
        mixed[at, :] = full.astype(bf16)
        lse[at, :] = jnp.broadcast_to(top + jnp.log(summed), (tall, 128))
        if i == blocks - 1:
            save(6).start()

    def hidden(i):
        if i == 0:
            own_weight(3).wait()
        at = at_block(i)
        value = jnp.dot(mlp_in[at, :], w_up[...], preferred_element_type=f32) + up_b[...]
        cdf = (1.0 + lax.erf(value * (0.5 ** 0.5))) * 0.5
        act[at, :] = (value * cdf).astype(bf16)
        slope[at, :] = cdf + value * jnp.exp(value * value * (-0.5)) * 0.3989422804014327
        if i == blocks - 1:
            save(3).start()

    def cotangent_here():
        stay(1, cot).wait()
        for r in range(nlo):
            across_arrival(1, r).wait_recv()
        save(0).start()
        own_weight(5).wait()

    def back_mixed(i):
        at = at_block(i)
        gm[at, :] = dot32(seq_c[at, :], w_out[...], contract_last).astype(bf16)

    def back_hidden(i):
        if i == 0:
            up_b_out[...] = jnp.zeros_like(up_b_out)
        at = at_block(i)
        part = (jnp.dot(seq_c[at, :], w_down[...], preferred_element_type=f32) * slope[at, :]).astype(bf16)
        gh[at, :] = part
        up_b_out[...] += jnp.sum(part.astype(f32), axis=0, keepdims=True)
        if i == blocks - 1:
            save(4).start()

    def out_store(i):
        return pltpu.make_async_copy(o_buf.at[at_block(i)], o_out.at[at_block(i)], o_c.at[i])

    def out_block(i):
        if i == 0:
            own_weight(4).wait()
        at = at_block(i)
        part = jnp.dot(mixed[at, :], w_out[...], preferred_element_type=f32)
        part = part + dot32(act[at, :], w_down[...], contract_last)
        o_buf[at, :] = part.astype(bf16)
        out_store(i).start()

    def back_attend(i):
        if i == 0:
            dk[...] = jnp.zeros_like(dk)
            dv[...] = jnp.zeros_like(dv)
        at = at_block(i)
        scores, reach = scores_of(i)
        probs = jnp.exp(scores - lse[at, :1])
        grad = gm[at, :]
        row_dot = jnp.sum(grad.astype(f32) * mixed_full[at, :], axis=-1, keepdims=True)
        dv[:reach, :] += dot32(probs.astype(bf16), grad, contract_first)
        grad_scores = (probs * (dot32(grad, v_ref[:reach, :], contract_last) - row_dot)).astype(bf16)
        dq[at, :] = dot32(grad_scores, k_ref[:reach, :]) * score_scale
        dk[:reach, :] += dot32(grad_scores, q_ref[at, :], contract_first) * score_scale

    def back_project():
        qkv_b_out[...] = jnp.zeros_like(qkv_b_out)
        for i in range(blocks):
            at = at_block(i)
            part = jnp.concatenate(
                [turn(dq[at, :], cos_t[at, :], -sin_t[at, :]), turn(dk[at, :], cos_t[at, :], -sin_t[at, :]), dv[at, :]],
                axis=1,
            ).astype(bf16)
            gp[at, :] = part
            qkv_b_out[...] += jnp.sum(part.astype(f32), axis=0, keepdims=True)
        save(5).start()

    short = 128

    def in_store(i):
        return pltpu.make_async_copy(s_buf.at[pl.ds(i * short, short)], s_out.at[pl.ds(i * short, short)], s_c.at[i])

    def in_block(i):
        if i == 0:
            vec_out[...] = jnp.zeros_like(vec_out)
        at = pl.ds(i * short, short)
        grad_a = dot32(gp[at, :], w_qkv[...], contract_last)
        grad_m = dot32(gh[at, :], w_up[...], contract_last)
        s_buf[at, :] = (grad_a * gain_a[...] + grad_m * gain_m[...]).astype(bf16)
        normed = (seq_t[at, :].astype(f32) - means[at, :1]) * scales[at, :1]
        for k, term in enumerate((grad_a * normed, grad_a, grad_m * normed, grad_m)):
            vec_out[k : k + 1, :] += jnp.sum(term, axis=0, keepdims=True)
        in_store(i).start()

    act_of = dict(
        N=lambda a: dispatch(a, 0), Z=chain_event, D=near_event, W=lambda g, i: weight_z(g, i).start(), E=weight_event,
        WO=own_start, H=norm, K=project, AF=attend, U=hidden, CO=cotangent_here, GM=back_mixed, GH=back_hidden,
        O=out_block, AB=back_attend, BP=back_project, S=in_block,
    )
    order_w = [(g, i) for g in range(len(groups)) for i in range(1, nz)]
    by_bit = sorted(range(1, nlo), key=lambda r: -low_bit(r))
    for item in block_schedule(order_w, nlo, by_bit, len(groups), blocks, total // short):
        act_of[item[0]](*item[1:])

    for k in range(len(kept)):
        save(k).wait()
    for i in range(blocks):
        out_store(i).wait()
    for i in range(total // short):
        in_store(i).wait()
    for g, i in order_w:
        weight_z(g, i).wait_send()
        for r in range(nlo):
            for b in bits:
                if r == 0 or b < low_bit(r):
                    weight_forward(g, i, r, b).wait_send()
    for a in range(2):
        for which in range(2 * nz - 1):
            settle(a, which)
        for r in range(1, nlo):
            across(a, seq_rows(a, hi, r), r).wait_send()


def block_all(lay, tok, cot, qkv, up, down, out_w, qkv_b, up_b, gains, cos_t, sin_t):
    rows, width = tok.shape
    nz, nlo = lay.nz, lay.nlo
    ff = up_b.shape[1]
    bits = len(lay.bits)
    anywhere = pl.BlockSpec(memory_space=pl.ANY)
    inside = pl.BlockSpec(memory_space=pltpu.VMEM)
    dma = pltpu.SemaphoreType.DMA
    bf16, f32 = jnp.bfloat16, jnp.float32
    total = 2 * nlo * rows

    def shape(*dims, kind=bf16):
        return jax.ShapeDtypeStruct(dims, kind)

    def vmem(*dims, kind=bf16):
        return pltpu.VMEM(dims, kind)

    return pl.pallas_call(
        functools.partial(block_kernel, lay, (rows, width, qkv.shape[0], ff)),
        out_shape=[
            shape(total, width), shape(total, width), shape(total, width), shape(total, ff), shape(total, ff),
            shape(total, 3 * HD), shape(total, HD), shape(total, width), shape(total, width),
            shape(nz, rows, width), shape(nz, rows, width),
            shape(4, width, kind=f32), shape(1, 3 * HD, kind=f32), shape(1, ff, kind=f32),
        ],
        in_specs=[anywhere] * 6 + [inside] * 8,
        out_specs=[anywhere] * 11 + [inside] * 3,
        scratch_shapes=[
            vmem(total, width), vmem(total, width), vmem(width, 3 * HD), vmem(width, ff), vmem(width, ff), vmem(HD, width),
            vmem(total, width), vmem(total, width), vmem(total, HD), vmem(total, HD), vmem(total, HD), vmem(total, HD),
            vmem(total, HD, kind=f32), vmem(total, 128, kind=f32), vmem(total, ff, kind=f32), vmem(total, ff),
            vmem(total, ff), vmem(total, HD),
            vmem(total, HD, kind=f32), vmem(total, HD, kind=f32), vmem(total, HD, kind=f32), vmem(total, 3 * HD),
            vmem(total, width), vmem(total, width), vmem(total, 128, kind=f32), vmem(total, 128, kind=f32),
            dma((2, nlo)), dma((2, nz)), dma((2,)), dma((2, nz)), dma((2, nz, 2)), dma((2, nlo)), dma((2, nlo)),
            dma((5, nz - 1)), dma((5, nz - 1)), dma((5, nz - 1, nlo)), dma((5, nz - 1, nlo, bits)), dma((6,)),
            dma((7,)), dma((total // 256,)), dma((total // 128,)),
        ],
        compiler_params=pltpu.CompilerParams(
            collective_id=3, has_side_effects=True, vmem_limit_bytes=62 * 1024 * 1024
        ),
        name="block_all",
    )(tok, cot, qkv, up, down, out_w, qkv_b, up_b, *gains, cos_t, sin_t)


def add_rows(into, left, right, step):
    rows = into.shape[0]
    step = min(step, rows)

    def body(k, carry):
        at = pl.ds(pl.multiple_of(k * step, step), step)
        into[at, :] = (left[at, :].astype(jnp.float32) + right[at, :].astype(jnp.float32)).astype(into.dtype)
        return carry

    lax.fori_loop(0, rows // step, body, 0)


def differ(one, other, count):
    result, bit = 0, 1
    while bit < count:
        result = result + bit * ((one // bit + other // bit) % 2)
        bit *= 2
    return result


def scatter_chunks(width, ff, repeat):
    cut = max(ff // 2, 256)
    chunks = []
    for source in (0, 1):
        for first in range(0, ff, cut):
            chunks.append((source, first, cut, lambda rank, first=first: rank * ff + first, True))
    for part in range(3):
        chunks.append((2, part * HD, HD, lambda rank, part=part: part * width + (rank // repeat) * HD, repeat == 1))
    return chunks


def scatter_schedule(nz, nlo, n_chunks, stages):
    timed = [(-4, ("M",)), (-3, ("L",)), (-2, ("Y", 0)), (30, ("Y", 1))]
    for g in range(n_chunks):
        timed.append((0 + 4 * g, ("C", g)))
        for t in range(stages):
            timed.append((10 + 14 * g + 20 * t, ("X", g, t)))
    for a, (first, step, chain, hop) in enumerate(((14, 11.4, 60, 11), (60, 11.4, 106, 11))):
        for q in range(nlo):
            timed.append((first + step * q, ("A", a, q)))
        for m in range(nz - 1):
            timed.append((chain + hop * m, ("B", a, nz - 1 - m, 0)))
            timed.append((chain + hop * m, ("B", a, m, 1)))
        timed.append((chain + hop * (nz - 1), ("F", a)))
    for t in range(stages):
        timed.append((100 + 10 * t, ("Q", t)))
    for t in range(2 * stages + 1):
        timed.append((1 + 4 * t, ("N", t)))
    timed.sort(key=lambda entry: entry[0])
    return [entry[1] for entry in timed] + [("G", g) for g in range(n_chunks)]


def scatter_kernel(lay, sizes, *refs):
    rows, width, ff, repeat = sizes
    nz, nlo, nhi = lay.nz, lay.nlo, lay.nhi
    stages = len(lay.bits)
    chunks = scatter_chunks(width, ff, repeat)
    n = len(chunks)
    refs = list(refs)

    def take(count):
        taken = refs[:count]
        del refs[:count]
        return taken

    partial_o, partial_s, x_down, x_up, x_qkv, g_down, g_up, g_qkv, g_out, small = take(10)
    sum_o, sum_s, all_down, all_up, all_qkv, all_out, small_sum = take(7)
    own, across_buf, near_buf, chain_buf = take(4)
    acc = take(n)
    got = [take(stages) for _ in range(n)]
    out_acc, = take(1)
    out_got = take(stages)
    small_buf, small_got = take(2)
    left, right_down, right_up, right_qkv, right_out, staged, out_part = take(7)
    (own_c, y_r, y_s, near_r, near_s, z_r, z_s, st_r, st_s, g_r, g_s, keep_c,
     out_r, out_s, move_r, move_s, sm_r, sm_s, left_c, right_c) = take(20)

    z, hi, lo = place(lay)
    rank = z * nhi + hi
    half = nlo * rows
    grain = width // (nz * nhi * nlo)
    span = nz * grain

    def dev(z, hi, lo):
        return (hi * nlo + lo, z)

    ctx = hi * nlo + lo
    moves = (ctx != rank) | (z != lo)
    barrier = pltpu.get_barrier_semaphore()
    mates = [
        dev((z + dz) % nz, flip(hi, dh, nhi), lo) for dz in range(nz) for dh in range(nhi) if dz or dh
    ] + [dev(z, hi, flip(lo, r, nlo)) for r in range(1, nlo)]
    for device in mates:
        pl.semaphore_signal(barrier, inc=1, device_id=device, device_id_type=MESH)

    @pl.when(moves)
    def _():
        pl.semaphore_signal(barrier, inc=1, device_id=(rank, lo), device_id_type=MESH)
        pl.semaphore_signal(barrier, inc=1, device_id=dev(ctx // nhi, ctx % nhi, z), device_id_type=MESH)
        pl.semaphore_wait(barrier, len(mates) + 2)

    @pl.when(jnp.logical_not(moves))
    def _():
        pl.semaphore_wait(barrier, len(mates))

    partial, summed = (partial_o, partial_s), (sum_o, sum_s)

    def load_own(a, q):
        row = pl.multiple_of(hi * half + q * rows, rows)
        return pltpu.make_async_copy(partial[a].at[pl.ds(row, rows)], own.at[a, q % 2], own_c.at[a, q % 2])

    def across(a, q):
        row = pl.multiple_of((1 - hi) * half + q * rows, rows)
        return remote(
            partial[a].at[pl.ds(row, rows)], across_buf.at[a, q], y_s.at[a, q], y_r.at[a, q], dev(z, 1 - hi, lo)
        )

    def near(a, q):
        return remote(
            across_buf.at[a, q], near_buf.at[a, lo], near_s.at[a, q], near_r.at[a, lo], dev(z, hi, q)
        )

    def near_arrival(a, q):
        piece = near_buf.at[a, q]
        return remote(piece, piece, near_s.at[a, q], near_r.at[a, q], dev(z, hi, q))

    def along(a, seq, way):
        slot = seq if way == 0 else jnp.where(z == seq + 1, nz, seq)
        return remote(
            near_buf.at[a, lay.lo_of_seq[seq]], chain_buf.at[a, slot], z_s.at[a, seq], z_r.at[a, seq, way],
            dev((z + 1 - 2 * way + nz) % nz, hi, lo),
        )

    def start_across(a):
        for q in range(2):
            load_own(a, q).start()
        for q in range(nlo):
            across(a, q).start()

    def across_event(a, q):
        load_own(a, q).wait()
        across(a, q).wait_recv()
        mine, arrived = own.at[a, q % 2], across_buf.at[a, q]

        @pl.when(lo == q)
        def _():
            add_rows(near_buf.at[a, q], mine, arrived, 16)

        @pl.when(lo != q)
        def _():
            add_rows(arrived, mine, arrived, 16)
            near(a, q).start()

        if q + 2 < nlo:
            load_own(a, q + 2).start()

    def chain_event(a, seq, way):
        q = lay.lo_of_seq[seq]
        active = (z < seq) if way == 0 else (z > seq)
        first = (z == 0) if way == 0 else (z == nz - 1)

        @pl.when(active)
        def _():
            @pl.when(lo != q)
            def _():
                near_arrival(a, q).wait_recv()

            @pl.when(jnp.logical_not(first))
            def _():
                along(a, seq, way).wait_recv()
                add_rows(near_buf.at[a, q], near_buf.at[a, q], chain_buf.at[a, seq], 16)

            along(a, seq, way).start()

    def final_event(a):
        late = z // (nz // 2)
        home = (1 - late) * (2 * z) + late * (2 * (nz - 1 - z) + 1)
        piece = near_buf.at[a, home]

        @pl.when(lo != home)
        def _():
            remote(piece, piece, near_s.at[a, 0], near_r.at[a, home], dev(z, hi, home)).wait_recv()

        @pl.when(z > 0)
        def _():
            arrived = chain_buf.at[a, z]
            remote(arrived, arrived, z_s.at[a, 0], z_r.at[a, z, 0], dev(z, hi, lo)).wait_recv()

        @pl.when(z < nz - 1)
        def _():
            arrived = chain_buf.at[a, nz]
            remote(arrived, arrived, z_s.at[a, 0], z_r.at[a, z, 1], dev(z, hi, lo)).wait_recv()

        def body(k, carry):
            at = pl.ds(pl.multiple_of(k * 16, 16), 16)
            total = piece[at, :].astype(jnp.float32)
            total = total + jnp.where(z > 0, chain_buf[a, z, at, :].astype(jnp.float32), 0.0)
            total = total + jnp.where(z < nz - 1, chain_buf[a, nz, at, :].astype(jnp.float32), 0.0)
            summed[a][at, :] = total
            return carry

        lax.fori_loop(0, rows // 16, body, 0)

    targets = (all_down, all_up, all_qkv)
    lefts = (x_down, x_up, x_qkv)
    n_slots = left.shape[0]
    slots = [source % n_slots for source in range(3)]
    rights = ((g_down, right_down), (g_up, right_up), (g_qkv, right_qkv), (g_out, right_out))

    def load_left(source):
        return pltpu.make_async_copy(lefts[source], left.at[slots[source]], left_c.at[source])

    def load_right(source):
        return pltpu.make_async_copy(*rights[source], right_c.at[source])

    def start_loads():
        for source in (0, 3, 1, 2):
            if source < n_slots:
                load_left(source).start()
            load_right(source).start()

    def ready(source):
        load_left(source).wait()
        load_right(source).wait()

    def product(g, h, rel):
        source, first, wide, _, _ = chunks[g]
        row = (h * nlo + differ(lo, rel, nlo)) * span
        rows_at = pl.ds(pl.multiple_of(row, span), span)
        part = lax.dot_general(
            left[slots[source], :, rows_at], rights[source][1][:, first : first + wide],
            contract_first, preferred_element_type=jnp.float32,
        )
        return part.astype(jnp.bfloat16)

    def stage_pieces(t):
        return [rel for rel in range(nlo) if rel % (2 << t) == (1 << t)]

    def stage_send(g, t, h, rel):
        if t == 0:
            src = staged.at[g % 3, h, rel // 2, :, pl.ds(0, chunks[g][2])]
        else:
            src = acc[g].at[h, rel // 2]
        k = rel >> (t + 1)
        return remote(
            src, got[g][t].at[h, k], st_s.at[g, t, h, k], st_r.at[g, t, h, k], dev(z, hi, flip(lo, 1 << t, nlo))
        )

    pairs = nhi * (nlo // 2)

    def start_chunk(g):
        source, first, wide, _, _ = chunks[g]
        if first == 0:
            ready(source)
        if g >= 3:
            for h in range(nhi):
                for rel in stage_pieces(0):
                    stage_send(g - 3, 0, h, rel).wait_send()

        def send(i, carry):
            h, k = i // (nlo // 2), i % (nlo // 2)
            staged[g % 3, h, k, :, :wide] = product(g, h, 2 * k + 1)
            stage_send(g, 0, h, 2 * k + 1).start()
            return carry

        def keep_own(i, carry):
            h, k = i // (nlo // 2), i % (nlo // 2)
            acc[g][h, k] = product(g, h, 2 * k)
            return carry

        lax.fori_loop(0, pairs, send, 0)
        lax.fori_loop(0, pairs, keep_own, 0)
        if g == 0:
            out_start()
        if (g + 1 == n or chunks[g + 1][0] != source) and source + n_slots < 3:
            load_left(source + n_slots).start()

    def stage_event(g, t):
        order = list(reversed(range(0, nlo, 2 << t)))
        for h in range(nhi):
            for rel in order:
                k = rel >> (t + 1)
                stage_send(g, t, h, rel | (1 << t)).wait_recv()
                add_rows(acc[g].at[h, rel // 2], acc[g].at[h, rel // 2], got[g][t].at[h, k], 64)
                if t + 1 < stages and rel % (4 << t) == (2 << t):
                    stage_send(g, t + 1, h, rel).start()
        if t + 1 == stages:
            deliver(g)

    def owner_send(g, dz, dh):
        source, _, wide, column, _ = chunks[g]
        to_z, to_hi = (z + dz) % nz, flip(hi, dh, nhi)
        first = pl.multiple_of(column(rank), 128)
        k = dz * nhi + dh
        return remote(
            acc[g].at[to_hi, 0, pl.ds(pl.multiple_of(to_z * grain, grain), grain)],
            targets[source].at[:, pl.ds(first, wide)],
            g_s.at[g, k], g_r.at[g, k], dev(to_z, to_hi, lo),
        )

    def owner_arrival(g, dz, dh):
        source, _, wide, column, _ = chunks[g]
        from_z, from_hi = (z + nz - dz) % nz, flip(hi, dh, nhi)
        first = pl.multiple_of(column(from_z * nhi + from_hi), 128)
        piece = targets[source].at[:, pl.ds(first, wide)]
        k = dz * nhi + dh
        return remote(piece, piece, g_s.at[g, k], g_r.at[g, k], dev(from_z, from_hi, lo))

    def keep(g):
        source, _, wide, column, _ = chunks[g]
        first = pl.multiple_of(column(rank), 128)
        return pltpu.make_async_copy(
            acc[g].at[hi, 0, pl.ds(pl.multiple_of(z * grain, grain), grain)],
            targets[source].at[:, pl.ds(first, wide)], keep_c.at[g],
        )

    others = [(dz, dh) for dz in range(nz) for dh in range(nhi) if dz or dh]

    def when_sent(g, from_hi, act):
        if chunks[g][4]:
            act()
        else:
            pl.when(from_hi % repeat == 0)(act)

    def deliver(g):
        def act():
            for dz, dh in others:
                owner_send(g, dz, dh).start()
            keep(g).start()

        when_sent(g, hi, act)

    def finish_chunk(g):
        def sent():
            for dz, dh in others:
                owner_send(g, dz, dh).wait_send()
            keep(g).wait()

        when_sent(g, hi, sent)
        for dz, dh in others:
            when_sent(g, flip(hi, dh, nhi), lambda dz=dz, dh=dh: owner_arrival(g, dz, dh).wait_recv())

    def out_rows(rel):
        return out_part.at[pl.ds(pl.multiple_of(flip(lo, rel, nlo) * grain, grain), grain)]

    def out_send(t, rel):
        src = out_rows(rel) if t == 0 else out_acc.at[rel // 2]
        k = rel >> (t + 1)
        return remote(src, out_got[t].at[k], out_s.at[t, k], out_r.at[t, k], dev(z, hi, flip(lo, 1 << t, nlo)))

    def out_start():
        load_right(3).wait()
        wide = min(512, width)

        def body(i, carry):
            at = pl.ds(pl.multiple_of(i * wide, wide), wide)
            part = lax.dot_general(
                right_out[...], left[0, :, at], contract_first, preferred_element_type=jnp.float32
            )
            out_part[:, at] = part.astype(jnp.bfloat16)
            return carry

        lax.fori_loop(0, width // wide, body, 0)
        for rel in stage_pieces(0):
            out_send(0, rel).start()

    def out_event(t):
        for rel in reversed(range(0, nlo, 2 << t)):
            out_send(t, rel | (1 << t)).wait_recv()
            mine = out_rows(rel) if t == 0 else out_acc.at[rel // 2]
            add_rows(out_acc.at[rel // 2], mine, out_got[t].at[rel >> (t + 1)], 16)
            if t + 1 < stages and rel % (4 << t) == (2 << t):
                out_send(t + 1, rel).start()
        if t + 1 == stages:
            @pl.when(moves)
            def _():
                out_move().start()

            @pl.when(jnp.logical_not(moves))
            def _():
                out_stay().start()

    def out_move():
        return remote(out_acc.at[0], all_out, move_s, move_r, (rank, lo))

    def out_stay():
        return pltpu.make_async_copy(out_acc.at[0], all_out, move_s)

    doubling = (
        [dev(z, flip(hi, 1, nhi), lo)]
        + [dev(z, hi, flip(lo, b, nlo)) for b in reversed(lay.bits)]
        + [dev(flip(z, b, nz), hi, lo) for b in lay.bits]
    )

    def small_send(t):
        src = small if t == 0 else small_buf.at[t - 1]
        return remote(src, small_got.at[t], sm_s.at[t], sm_r.at[t], doubling[t])

    def small_event(t):
        small_send(t).wait_recv()
        mine = small if t == 0 else small_buf.at[t - 1]
        into = small_sum if t + 1 == len(doubling) else small_buf.at[t]
        into[...] = mine[...] + small_got[t]
        if t + 1 < len(doubling):
            small_send(t + 1).start()

    act = dict(
        Y=start_across, A=across_event, B=chain_event, F=final_event, C=start_chunk, X=stage_event, G=finish_chunk,
        L=start_loads, Q=out_event, M=lambda: small_send(0).start(), N=small_event,
    )
    for item in scatter_schedule(nz, nlo, n, stages):
        act[item[0]](*item[1:])

    for a in range(2):
        for q in range(nlo):
            across(a, q).wait_send()

            @pl.when(lo != q)
            def _(a=a, q=q):
                near(a, q).wait_send()

        for seq in range(nz):
            @pl.when(z != seq)
            def _(a=a, seq=seq):
                along(a, seq, 0).wait_send()

    for g in range(n):
        for t in range(stages):
            if t == 0 and g + 3 < n:
                continue
            for h in range(nhi):
                for rel in stage_pieces(t):
                    stage_send(g, t, h, rel).wait_send()
    for t in range(stages):
        for rel in stage_pieces(t):
            out_send(t, rel).wait_send()

    @pl.when(moves)
    def _():
        out_move().wait()

    @pl.when(jnp.logical_not(moves))
    def _():
        out_stay().wait()

    for t in range(len(doubling)):
        small_send(t).wait_send()


def scatter_all(lay, partial_o, partial_s, x_down, x_up, x_qkv, g_down, g_up, g_qkv, g_out, small):
    total, width = partial_o.shape
    nz, nlo, nhi = lay.nz, lay.nlo, lay.nhi
    rows = total // (nhi * nlo)
    ranks = nz * nhi
    ff = g_down.shape[1]
    repeat = max(1, ranks // H)
    grain = width // (ranks * nlo)
    span = nz * grain
    stages = len(lay.bits)
    chunks = scatter_chunks(width, ff, repeat)
    n = len(chunks)
    steps = 2 * stages + 1
    anywhere = pl.BlockSpec(memory_space=pl.ANY)
    inside = pl.BlockSpec(memory_space=pltpu.VMEM)
    dma = pltpu.SemaphoreType.DMA
    bf16, f32 = jnp.bfloat16, jnp.float32
    scratch = [
        pltpu.VMEM((2, 2, rows, width), bf16),
        pltpu.VMEM((2, nlo, rows, width), bf16),
        pltpu.VMEM((2, nlo, rows, width), bf16),
        pltpu.VMEM((2, nz + 1, rows, width), bf16),
    ]
    for chunk in chunks:
        scratch.append(pltpu.VMEM((nhi, nlo // 2, span, chunk[2]), bf16))
    for chunk in chunks:
        for t in range(stages):
            scratch.append(pltpu.VMEM((nhi, nlo >> (t + 1), span, chunk[2]), bf16))
    scratch.append(pltpu.VMEM((nlo // 2, grain, width), bf16))
    for t in range(stages):
        scratch.append(pltpu.VMEM((nlo >> (t + 1), grain, width), bf16))
    scratch += [pltpu.VMEM((steps,) + small.shape, f32), pltpu.VMEM((steps,) + small.shape, f32)]
    widest = max(chunk[2] for chunk in chunks)
    scratch += [
        pltpu.VMEM((2 if total <= 1024 else 1, total, width), bf16),
        pltpu.VMEM(g_down.shape, bf16), pltpu.VMEM(g_up.shape, bf16), pltpu.VMEM(g_qkv.shape, bf16),
        pltpu.VMEM(g_out.shape, bf16),
        pltpu.VMEM((3, nhi, nlo // 2, span, widest), bf16),
        pltpu.VMEM((width // ranks, width), bf16),
    ]
    most = nlo // 2
    scratch += [
        dma((2, 2)), dma((2, nlo)), dma((2, nlo)), dma((2, nlo)), dma((2, nlo)), dma((2, nz, 2)), dma((2, nz)),
        dma((n, stages, nhi, most)), dma((n, stages, nhi, most)), dma((n, ranks)), dma((n, ranks)),
        dma((n,)), dma((stages, most)), dma((stages, most)), dma, dma, dma((steps,)), dma((steps,)), dma((3,)), dma((4,)),
    ]
    return pl.pallas_call(
        functools.partial(scatter_kernel, lay, (rows, width, ff, repeat)),
        out_shape=[
            jax.ShapeDtypeStruct((rows, width), f32),
            jax.ShapeDtypeStruct((rows, width), f32),
            jax.ShapeDtypeStruct((grain, ff * ranks), bf16),
            jax.ShapeDtypeStruct((grain, ff * ranks), bf16),
            jax.ShapeDtypeStruct((grain, 3 * width), bf16),
            jax.ShapeDtypeStruct((grain, width), bf16),
            jax.ShapeDtypeStruct(small.shape, f32),
        ],
        in_specs=[anywhere] * 9 + [inside],
        out_specs=[inside, inside, anywhere, anywhere, anywhere, anywhere, inside],
        scratch_shapes=scratch,
        compiler_params=pltpu.CompilerParams(
            collective_id=2, has_side_effects=True, vmem_limit_bytes=60 * 1024 * 1024
        ),
        name="scatter_all",
    )(partial_o, partial_s, x_down, x_up, x_qkv, g_down, g_up, g_qkv, g_out, small)


def plain_block(lay, operands):
    f32, bf16 = jnp.float32, jnp.bfloat16
    (own, own_cotangent, qkv_weight, qkv_bias, out_weight, up_weight, up_bias, down_weight,
     attn_norm_gain, attn_norm_bias, mlp_norm_gain, mlp_norm_bias) = operands
    nz, nlo, nhi = lay.nz, lay.nlo, lay.nhi
    ranks = nz * nhi
    rows, width = own.shape
    weight_rows = qkv_weight.shape[0]
    half = nlo * rows
    z, hi, lo = place(lay)
    rank = z * nhi + hi
    ff = up_weight.shape[1] // ranks
    repeat = max(1, ranks // H)
    head = rank // repeat
    score_scale = HD ** (-0.5)
    seq_tokens, seq_cotangent, qkv_here, up_here, down_here = gather_all(
        lay, own, own_cotangent, qkv_weight, up_weight, down_weight
    )
    own_qkv = jnp.concatenate(
        [
            lax.dynamic_slice(qkv_weight, (0, part * width + head * HD), (weight_rows, HD))
            for part in range(3)
        ],
        axis=1,
    )
    own_up = lax.dynamic_slice(up_weight, (0, rank * ff), (weight_rows, ff))
    own_down = lax.dynamic_slice(down_weight, (0, rank * ff), (weight_rows, ff))
    qkv_here = lax.dynamic_update_slice(qkv_here, own_qkv, (z * weight_rows, 0))
    up_here = lax.dynamic_update_slice(up_here, own_up, (z * weight_rows, 0))
    down_here = lax.dynamic_update_slice(down_here, own_down, (z * weight_rows, 0))
    out_head = lax.dynamic_slice(out_weight, (head * HD - z * weight_rows, 0), (HD, width))
    out_rows = width // ranks
    out_at = rank * out_rows - head * HD

    positions = jnp.arange(2 * half, dtype=jnp.int32)

    normed, _ = normalize(seq_tokens.astype(f32))
    attn_in = (normed * attn_norm_gain + attn_norm_bias).astype(bf16)
    mlp_in = (normed * mlp_norm_gain + mlp_norm_bias).astype(bf16)
    bias_here = jnp.concatenate(
        [lax.dynamic_slice(qkv_bias, (part * width + head * HD,), (HD,)) for part in range(3)]
    )
    projected = dot32(attn_in, qkv_here) + bias_here
    queries = rotary(projected[:, :HD], positions).astype(bf16)
    keys = rotary(projected[:, HD : 2 * HD], positions).astype(bf16)
    values = projected[:, 2 * HD :].astype(bf16)
    causal = positions[:, None] >= positions[None, :]
    scores = jnp.where(causal, dot32(queries, keys, contract_last) * score_scale, masked_score)
    top = jnp.max(scores, axis=-1, keepdims=True)
    weights = jnp.where(causal, jnp.exp(scores - top), 0.0)
    total = jnp.sum(weights, axis=-1, keepdims=True)
    mixed_full = dot32(weights.astype(bf16), values) / total
    log_total = top + jnp.log(total)
    mixed = mixed_full.astype(bf16)
    mixed_mine = lax.dynamic_slice(mixed, (0, out_at), (mixed.shape[0], out_rows))
    out_mine = lax.dynamic_slice(out_head, (out_at, 0), (out_rows, width))
    hidden = dot32(mlp_in, up_here) + lax.dynamic_slice(up_bias, (rank * ff,), (ff,))
    activated_full, gelu_pull = jax.vjp(exact_gelu, hidden)
    activated = activated_full.astype(bf16)
    out_partial = dot32(mixed_mine, out_mine) + dot32(activated, down_here, contract_last)
    grad_hidden = gelu_pull(dot32(seq_cotangent, down_here))[0].astype(bf16)
    grad_mixed = dot32(seq_cotangent, out_head, contract_last).astype(bf16)
    row_dot = jnp.sum(grad_mixed.astype(f32) * mixed_full, axis=-1, keepdims=True)
    probs = jnp.where(causal, jnp.exp(scores - log_total), 0.0)
    grad_values = dot32(probs.astype(bf16), grad_mixed, contract_first)
    grad_probs = dot32(grad_mixed, values, contract_last)
    grad_scores = (probs * (grad_probs - row_dot)).astype(bf16)
    grad_queries = dot32(grad_scores, keys) * score_scale
    grad_keys = dot32(grad_scores, queries, contract_first) * score_scale
    grad_projected = jnp.concatenate(
        [rotary(grad_queries, -positions), rotary(grad_keys, -positions), grad_values], axis=1
    ).astype(bf16)
    grad_attn_in = dot32(grad_projected, qkv_here, contract_last) * (1.0 / repeat)
    grad_mlp_in = dot32(grad_hidden, up_here, contract_last)
    in_partial = grad_attn_in * attn_norm_gain + grad_mlp_in * mlp_norm_gain
    sums = jnp.stack(
        [
            jnp.sum(grad_attn_in * normed, axis=0),
            jnp.sum(grad_attn_in, axis=0),
            jnp.sum(grad_mlp_in * normed, axis=0),
            jnp.sum(grad_mlp_in, axis=0),
        ]
    )
    first_copy = jnp.where(rank % repeat == 0, 1.0, 0.0)
    return (
        seq_cotangent, attn_in, mlp_in, activated, grad_hidden, grad_projected, mixed_mine,
        out_partial.astype(bf16), in_partial.astype(bf16), sums,
        jnp.sum(grad_projected.astype(f32), axis=0) * first_copy,
        jnp.sum(grad_hidden.astype(f32), axis=0),
    )


def fused_block(lay, operands):
    f32 = jnp.float32
    (own, own_cotangent, qkv_weight, qkv_bias, out_weight, up_weight, up_bias, down_weight,
     attn_norm_gain, attn_norm_bias, mlp_norm_gain, mlp_norm_bias) = operands
    rows, width = own.shape
    z, hi, _ = place(lay)
    rank = z * lay.nhi + hi
    ff = up_weight.shape[1] // (lay.nz * lay.nhi)
    total = lay.nhi * lay.nlo * rows
    bias_here = jnp.concatenate(
        [lax.dynamic_slice(qkv_bias, (part * width + rank * HD,), (HD,)) for part in range(3)]
    )
    half_rot = ROT // 2
    inv_freq = 10000.0 ** (-(jnp.arange(half_rot, dtype=f32) * 2.0) / ROT)
    angles = jnp.arange(total, dtype=f32)[:, None] * inv_freq[None, :]
    cosine, sine = jnp.cos(angles), jnp.sin(angles)
    rest = jnp.zeros((total, 128 - ROT), f32)
    found = block_all(
        lay, own, own_cotangent, qkv_weight, up_weight, down_weight, out_weight,
        bias_here[None], lax.dynamic_slice(up_bias, (rank * ff,), (ff,))[None],
        [v[None] for v in (attn_norm_gain, attn_norm_bias, mlp_norm_gain, mlp_norm_bias)],
        jnp.concatenate([cosine, cosine, rest + 1.0], axis=1),
        jnp.concatenate([-sine, sine, rest], axis=1),
    )
    return tuple(found[:9]) + (found[11], found[12][0], found[13][0])


def local_block(
    lay,
    tokens,
    qkv_weight,
    qkv_bias,
    out_weight,
    out_bias,
    up_weight,
    up_bias,
    down_weight,
    down_bias,
    attn_norm_gain,
    attn_norm_bias,
    mlp_norm_gain,
    mlp_norm_bias,
    cotangent,
):
    f32, bf16 = jnp.float32, jnp.bfloat16
    nz, nlo, nhi = lay.nz, lay.nlo, lay.nhi
    ranks = nz * nhi
    rows = tokens.shape[1]
    width = tokens.shape[2]
    hidden_width = up_weight.shape[1]
    weight_rows = qkv_weight.shape[0]
    half = nlo * rows
    ctx = lax.axis_index("ctx")
    z = lax.axis_index("shard")
    hi, lo = ctx // nlo, ctx % nlo
    rank = z * nhi + hi
    ff = hidden_width // ranks
    repeat = max(1, ranks // H)
    head = rank // repeat
    own = tokens[0]
    own_cotangent = cotangent[0]
    operands = (
        own, own_cotangent, qkv_weight, qkv_bias, out_weight, up_weight, up_bias, down_weight,
        attn_norm_gain, attn_norm_bias, mlp_norm_gain, mlp_norm_bias,
    )
    fits = repeat == 1 and nhi * half * width <= 1024 * 2048
    (seq_cotangent, attn_in, mlp_in, activated, grad_hidden, grad_projected, mixed_mine,
     out_partial, in_partial, sums, qkv_bias_part, up_bias_part) = (fused_block if fits else plain_block)(lay, operands)

    qkv_bias_full = jnp.zeros((3, width), f32)
    qkv_bias_full = lax.dynamic_update_slice(
        qkv_bias_full, qkv_bias_part.reshape(3, HD), (0, head * HD)
    ).reshape(-1)
    up_bias_full = lax.dynamic_update_slice(
        jnp.zeros((hidden_width,), f32),
        up_bias_part,
        (rank * ff,),
    )
    small = jnp.concatenate(
        [
            qkv_bias_full,
            up_bias_full,
            jnp.sum(own_cotangent.astype(f32), axis=0),
            sums.reshape(-1),
        ]
    ).reshape(-1, 128)
    summed_out, summed_in, all_down, all_up, all_qkv, all_out, small = scatter_all(
        lay,
        out_partial,
        in_partial,
        seq_cotangent,
        mlp_in,
        attn_in,
        activated,
        grad_hidden,
        grad_projected,
        mixed_mine,
        small,
    )
    output = (own.astype(f32) + summed_out + (out_bias + down_bias)).astype(bf16)[None]
    own_normed, own_scale = normalize(own.astype(f32))
    input_grad = own_scale * (
        summed_in
        - jnp.mean(summed_in, axis=-1, keepdims=True)
        - own_normed * jnp.mean(summed_in * own_normed, axis=-1, keepdims=True)
    )
    tokens_grad = (own_cotangent.astype(f32) + input_grad)[None]

    small = small.reshape(-1)
    cuts = [3 * width, hidden_width, width, width, width, width, width]
    small_parts, at = [], 0
    for size in cuts:
        small_parts.append(small[at : at + size])
        at += size

    qkv_weight_grad = all_qkv.astype(f32)
    out_weight_grad = all_out.astype(f32)
    up_weight_grad = all_up.astype(f32)
    down_weight_grad = all_down.astype(f32)
    return (
        output,
        tokens_grad,
        qkv_weight_grad,
        small_parts[0],
        out_weight_grad,
        small_parts[2],
        up_weight_grad,
        small_parts[1],
        down_weight_grad,
        small_parts[2],
        small_parts[3],
        small_parts[4],
        small_parts[5],
        small_parts[6],
    )


def solution(mesh):
    lay = Layout(mesh)

    def local(*args):
        return local_block(lay, *args)

    sharded = P("shard", "ctx", None)
    by_rows = P("shard", None)
    owned = P(("ctx", "shard"), None)
    in_specs = (
        sharded, by_rows, P(), by_rows, P(), by_rows, P(), by_rows, P(),
        P(), P(), P(), P(), sharded,
    )
    out_specs = (
        sharded, sharded, owned, P(), owned, P(), owned, P(), owned,
        P(), P(), P(), P(), P(),
    )
    return jax.shard_map(
        local, mesh=mesh, in_specs=in_specs, out_specs=out_specs, check_vma=False
    )
```

```python
import functools

import jax
import jax.numpy as jnp
from jax import lax
from jax.experimental import pallas as pl
from jax.experimental.pallas import tpu as pltpu
from jax.sharding import PartitionSpec as P

H = 8
HD = 256
ROT = 64
AXES = ("ctx", "shard")
MESH = pl.DeviceIdType.MESH

norm_epsilon = 1e-05
masked_score = -1e30
contract_last = (((1,), (1,)), ((), ()))
contract_first = (((0,), (0,)), ((), ()))


def dot32(left, right, dims=(((1,), (0,)), ((), ()))):
    return lax.dot_general(left, right, dims, preferred_element_type=jnp.float32)


def normalize(values):
    center = values - jnp.mean(values, axis=-1, keepdims=True)
    spread = jnp.mean(center * center, axis=-1, keepdims=True)
    scale = lax.rsqrt(spread + norm_epsilon)
    return center * scale, scale


def rotary(values, positions):
    half_rot = ROT // 2
    inv_freq = 10000.0 ** (-(jnp.arange(half_rot, dtype=jnp.float32) * 2.0) / ROT)
    angles = positions.astype(jnp.float32)[:, None] * inv_freq[None, :]
    cosine = jnp.cos(angles)
    sine = jnp.sin(angles)
    first_half = values[:, :half_rot]
    second_half = values[:, half_rot:ROT]
    return jnp.concatenate(
        [
            first_half * cosine - second_half * sine,
            second_half * cosine + first_half * sine,
            values[:, ROT:],
        ],
        axis=-1,
    )


def exact_gelu(values):
    return jax.nn.gelu(values, approximate=False)


class Layout:
    def __init__(self, mesh):
        self.nz = mesh.shape["shard"]
        self.nc = mesh.shape["ctx"]
        self.nlo = self.nz
        self.nhi = self.nc // self.nlo
        assert self.nhi == 2 and self.nz * self.nhi == self.nc
        self.bits = [1 << b for b in range(self.nlo.bit_length() - 1)]
        assert 1 << len(self.bits) == self.nlo
        self.seq_of_lo = [
            lo // 2 if lo % 2 == 0 else self.nz - 1 - lo // 2 for lo in range(self.nlo)
        ]
        self.lo_of_seq = [self.seq_of_lo.index(s) for s in range(self.nz)]

    def flat(self, z, hi, lo):
        return (hi * self.nlo + lo) * self.nz + z


def flip(value, mask, count):
    bit = 1
    while bit < count:
        if mask & bit:
            value = value + bit - 2 * bit * ((value // bit) % 2)
        bit *= 2
    return value


def low_bit(mask):
    return mask & -mask


def place(lay):
    ctx = lax.axis_index("ctx")
    z = lax.axis_index("shard")
    return z, ctx // lay.nlo, ctx % lay.nlo


def remote(src, dst, send, recv, device):
    return pltpu.make_async_remote_copy(
        src_ref=src, dst_ref=dst, send_sem=send, recv_sem=recv, device_id=device, device_id_type=MESH
    )


def enter(devices):
    barrier = pltpu.get_barrier_semaphore()
    for device in devices:
        pl.semaphore_signal(barrier, inc=1, device_id=device, device_id_type=MESH)
    pl.semaphore_wait(barrier, len(devices))


def gather_schedule(order_w, nlo, by_bit, n_groups):
    w = [("W", g, i) for g, i in order_w]
    arrive = [("E", g, i, 0) for g, i in order_w]
    last = [("E", g, i, r) for r in by_bit for g, i in order_w]

    def tokens(a):
        events = [("D", a, 0)]
        for k in range(1, nlo):
            events += [("Z", a, k), ("D", a, k)]
        return events

    first, second = tokens(0), tokens(1)
    events = [("N", 0)] + first[:3] + [("N", 1)] + first[3:]
    k = 0
    for item in second:
        events += [item] + arrive[k : k + 2]
        k += 2
    events += arrive[k:] + last
    window, start = 3, 4
    schedule, k = [], window
    for n, item in enumerate(events):
        if n == start:
            schedule += w[:window]
        schedule.append(item)
        if item[0] == "E" and item[3] == 0 and k < len(w):
            schedule.append(w[k])
            k += 1
    return schedule


def gather_kernel(lay, sizes, tok, cot, qkv, up, down, seq_t, seq_c, w_qkv, w_up, w_down, stage_t, stage_c,
                  near_r, near_s, home_c, z_r, z_s, y_r, y_s, wz_r, wz_s, wf_r, wf_s):
    rows, width, weight_rows, ff, repeat = sizes
    nz, nlo, nhi = lay.nz, lay.nlo, lay.nhi
    z, hi, lo = place(lay)
    half, quarter = nlo * rows, weight_rows // nlo
    odd = lo % 2
    s = (1 - odd) * (lo // 2) + odd * (nz - 1 - lo // 2)

    def dev(z, hi, lo):
        return (hi * nlo + lo, z)

    enter(
        [dev((z + i) % nz, hi, lo) for i in range(1, nz)]
        + [dev(z, hi, flip(lo, r, nlo)) for r in range(1, nlo)]
        + [dev(z, 1 - hi, lo)]
    )

    groups = []
    for part in range(3):
        groups.append((qkv, w_qkv, lambda rank, part=part: part * width + (rank // repeat) * HD, part * HD, HD))
    groups.append((up, w_up, lambda rank: rank * ff, 0, ff))
    groups.append((down, w_down, lambda rank: rank * ff, 0, ff))
    bits = list(reversed(lay.bits))

    def weight_z(g, i):
        src, dst, column, at, wide = groups[g]
        to = (z + i) % nz
        first = pl.multiple_of(column(to * nhi + hi), 128)
        return remote(
            src.at[pl.ds(pl.multiple_of(lo * quarter, quarter), quarter), pl.ds(first, wide)],
            dst.at[pl.ds(pl.multiple_of(z * weight_rows + lo * quarter, quarter), quarter), pl.ds(at, wide)],
            wz_s.at[g, i - 1], wz_r.at[g, i - 1], dev(to, hi, lo),
        )

    def weight_forward(g, i, r, b):
        _, dst, _, at, wide = groups[g]
        row = ((z + nz - i) % nz) * weight_rows + flip(lo, r, nlo) * quarter
        piece = dst.at[pl.ds(pl.multiple_of(row, quarter), quarter), pl.ds(at, wide)]
        k = bits.index(b)
        return remote(piece, piece, wf_s.at[g, i - 1, r, k], wf_r.at[g, i - 1, r ^ b], dev(z, hi, flip(lo, b, nlo)))

    inputs, staged, sequences = (tok, cot), (stage_t, stage_c), (seq_t, seq_c)
    distance = jnp.abs(z - s)

    def home_of(seq):
        late = seq // (nz // 2)
        return (1 - late) * (2 * seq) + late * (2 * (nz - 1 - seq) + 1)

    def seq_rows(a, which, r):
        row = which * half + flip(lo, r, nlo) * rows
        return sequences[a].at[pl.ds(pl.multiple_of(row, rows), rows)]

    def along(a, src, seq, way):
        return remote(src, staged[a].at[seq], z_s.at[a, seq, way], z_r.at[a, seq], dev((z + 1 - 2 * way + nz) % nz, hi, lo))

    def near(a, src, seq):
        return remote(src, seq_rows(a, hi, 0), near_s.at[a, seq], near_r.at[a, lo], dev(z, hi, home_of(seq)))

    def near_arrival(a, r):
        piece = seq_rows(a, hi, r)
        return remote(piece, piece, near_s.at[a, 0], near_r.at[a, flip(lo, r, nlo)], dev(z, hi, flip(lo, r, nlo)))

    def stay(a, src):
        return pltpu.make_async_copy(src, seq_rows(a, hi, 0), home_c.at[a])

    def across(a, src, r):
        return remote(src, seq_rows(a, hi, r), y_s.at[a, r], y_r.at[a, r], dev(z, 1 - hi, lo))

    def across_arrival(a, r):
        piece = seq_rows(a, 1 - hi, r)
        return remote(piece, piece, y_s.at[a, r], y_r.at[a, r], dev(z, 1 - hi, lo))

    def sources(a):
        yield (z >= 0, inputs[a], z, z < nz - 1, z > 0)
        for k in range(1, nz):
            yield (z >= k, staged[a].at[(z + nz - k) % nz], (z + nz - k) % nz, z < nz - 1, z < 0)
            yield (z < nz - k, staged[a].at[(z + k) % nz], (z + k) % nz, z < 0, z > 0)

    def dispatch(a, which):
        valid, src, seq, up, down = list(sources(a))[which]

        @pl.when(valid & up)
        def _():
            along(a, src, seq, 0).start()

        @pl.when(valid & down)
        def _():
            along(a, src, seq, 1).start()

        @pl.when(valid & (lo == home_of(seq)))
        def _():
            across(a, src, 0).start()
            stay(a, src).start()

        @pl.when(valid & (lo != home_of(seq)))
        def _():
            near(a, src, seq).start()

    def settle(a, which):
        valid, src, seq, up, down = list(sources(a))[which]

        @pl.when(valid & up)
        def _():
            along(a, src, seq, 0).wait_send()

        @pl.when(valid & down)
        def _():
            along(a, src, seq, 1).wait_send()

        @pl.when(valid & (lo == home_of(seq)))
        def _():
            across(a, src, 0).wait_send()
            stay(a, src).wait()

        @pl.when(valid & (lo != home_of(seq)))
        def _():
            near(a, src, seq).wait_send()

    def chain_event(a, k):
        for which, valid, seq in ((2 * k - 1, z >= k, (z + nz - k) % nz), (2 * k, z < nz - k, (z + k) % nz)):
            @pl.when(valid)
            def _(seq=seq):
                along(a, staged[a].at[seq], seq, 0).wait_recv()

            dispatch(a, which)

    def near_event(a, d):
        @pl.when(distance == d)
        def _():
            for r in range(1, nlo):
                near_arrival(a, r).wait_recv()
                across(a, seq_rows(a, hi, r), r).start()

    def forward_from(g, i, r):
        for b in bits:
            if r == 0 or b < low_bit(r):
                weight_forward(g, i, r, b).start()

    def weight_event(g, i, r):
        if r == 0:
            weight_z(g, i).wait_recv()
        else:
            weight_forward(g, i, r ^ low_bit(r), low_bit(r)).wait_recv()
        forward_from(g, i, r)

    order_w = [(g, i) for g in range(len(groups)) for i in range(1, nz)]
    by_bit = sorted(range(1, nlo), key=lambda r: -low_bit(r))
    act = dict(N=lambda a: dispatch(a, 0), Z=chain_event, D=near_event, W=lambda g, i: weight_z(g, i).start(), E=weight_event)
    for item in gather_schedule(order_w, nlo, by_bit, len(groups)):
        act[item[0]](*item[1:])
    for a in range(2):
        for j in range(nlo):
            across_arrival(a, j).wait_recv()
    for g, i in order_w:
        weight_z(g, i).wait_send()
        for r in range(nlo):
            for b in bits:
                if r == 0 or b < low_bit(r):
                    weight_forward(g, i, r, b).wait_send()
    for a in range(2):
        for which in range(2 * nz - 1):
            settle(a, which)
        for r in range(1, nlo):
            across(a, seq_rows(a, hi, r), r).wait_send()


def gather_all(lay, tok, cot, qkv, up, down):
    rows, width = tok.shape
    nz, nlo = lay.nz, lay.nlo
    ranks = nz * lay.nhi
    ff = up.shape[1] // ranks
    repeat = max(1, ranks // H)
    sizes = (rows, width, qkv.shape[0], ff, repeat)
    bits = len(lay.bits)
    anywhere = pl.BlockSpec(memory_space=pl.ANY)
    dma = pltpu.SemaphoreType.DMA
    bf16 = jnp.bfloat16
    total = 2 * nlo * rows
    return pl.pallas_call(
        functools.partial(gather_kernel, lay, sizes),
        out_shape=[
            jax.ShapeDtypeStruct((total, width), bf16),
            jax.ShapeDtypeStruct((total, width), bf16),
            jax.ShapeDtypeStruct((width, 3 * HD), bf16),
            jax.ShapeDtypeStruct((width, ff), bf16),
            jax.ShapeDtypeStruct((width, ff), bf16),
            jax.ShapeDtypeStruct((nz, rows, width), bf16),
            jax.ShapeDtypeStruct((nz, rows, width), bf16),
        ],
        in_specs=[anywhere] * 5,
        out_specs=[anywhere] * 7,
        scratch_shapes=[
            dma((2, nlo)), dma((2, nz)), dma((2,)), dma((2, nz)), dma((2, nz, 2)), dma((2, nlo)), dma((2, nlo)),
            dma((5, nz - 1)), dma((5, nz - 1)), dma((5, nz - 1, nlo)), dma((5, nz - 1, nlo, bits)),
        ],
        compiler_params=pltpu.CompilerParams(collective_id=1, has_side_effects=True),
        name="gather_all",
    )(tok, cot, qkv, up, down)[:5]

def turn(values, cosine, sine):
    left = values[:, :128]
    lane = lax.broadcasted_iota(jnp.int32, left.shape, 1)
    swapped = jnp.where(lane < ROT // 2, pltpu.roll(left, 128 - ROT // 2, 1), pltpu.roll(left, ROT // 2, 1))
    return jnp.concatenate([left * cosine + swapped * sine, values[:, 128:]], axis=1)


def block_schedule():
    return [
        ("N", 0), ("WO",), ("N", 1), ("D", 0, 0), ("Z", 0, 1), ("D", 0, 1), ("W", 0, 1), ("W", 0, 2), ("Z", 0, 2),
        ("W", 0, 3), ("W", 1, 1), ("W", 1, 2), ("D", 0, 2), ("W", 1, 3), ("W", 2, 1), ("Z", 0, 3), ("W", 2, 2),
        ("D", 1, 0), ("Z", 1, 1), ("E", 0, 1, 0), ("W", 2, 3), ("E", 0, 2, 0), ("W", 3, 1), ("D", 0, 3),
        ("E", 0, 3, 0), ("E", 1, 1, 0), ("D", 1, 1), ("E", 1, 2, 0), ("H", 0), ("Z", 1, 2), ("E", 1, 3, 0),
        ("W", 3, 2), ("E", 2, 1, 0), ("E", 2, 2, 0), ("D", 1, 2), ("E", 0, 1, 2), ("E", 2, 3, 0), ("E", 0, 2, 2),
        ("E", 3, 1, 0), ("W", 3, 3), ("Z", 1, 3), ("E", 0, 3, 2), ("E", 1, 1, 2), ("E", 0, 1, 1), ("E", 0, 1, 3),
        ("E", 1, 2, 2), ("H", 1), ("E", 0, 2, 1), ("E", 0, 2, 3), ("D", 1, 3), ("E", 1, 3, 2), ("E", 3, 2, 0),
        ("W", 4, 1), ("E", 0, 3, 1), ("E", 0, 3, 3), ("E", 2, 1, 2), ("E", 1, 1, 1), ("E", 1, 1, 3), ("E", 2, 2, 2),
        ("E", 1, 2, 1), ("E", 1, 2, 3), ("E", 2, 3, 2), ("E", 1, 3, 1), ("E", 1, 3, 3), ("E", 3, 1, 2),
        ("E", 3, 3, 0), ("W", 4, 2), ("E", 2, 1, 1), ("E", 2, 1, 3), ("E", 2, 2, 1), ("E", 2, 2, 3), ("E", 2, 3, 1),
        ("E", 2, 3, 3), ("K", 0), ("K", 1), ("K", 2), ("K", 3), ("AF", 0), ("AF", 1), ("AF", 2), ("AF", 3),
        ("E", 3, 1, 1), ("E", 3, 1, 3), ("E", 3, 2, 2), ("E", 4, 1, 0), ("W", 4, 3), ("CO",), ("GM", 0), ("GM", 1),
        ("GM", 2), ("GM", 3), ("E", 3, 2, 1), ("E", 3, 2, 3), ("AB", 0), ("AB", 1), ("E", 3, 3, 2), ("E", 4, 2, 0),
        ("AB", 2), ("AB", 3), ("BP",), ("E", 3, 3, 1), ("E", 3, 3, 3), ("U", 0), ("U", 1), ("E", 4, 1, 2), ("U", 2),
        ("U", 3), ("E", 4, 3, 0), ("E", 4, 1, 1), ("E", 4, 1, 3), ("V", 0), ("E", 4, 2, 2), ("E", 4, 2, 1),
        ("E", 4, 2, 3), ("V", 1), ("E", 4, 3, 2), ("VX", 0), ("E", 4, 3, 1), ("E", 4, 3, 3), ("VX", 1), ("O", 0),
        ("O", 1), ("O", 2), ("O", 3), ("VO",), ("GH", 0), ("GH", 1), ("GH", 2), ("GH", 3), ("VY", 0), ("VY", 1),
    ]


def block_kernel(lay, sizes, *refs):
    rows, width, weight_rows, ff = sizes
    nz, nlo, nhi = lay.nz, lay.nlo, lay.nhi
    f32, bf16 = jnp.float32, jnp.bfloat16
    refs = list(refs)

    def take(count):
        taken = refs[:count]
        del refs[:count]
        return taken

    tok, cot, qkv, up, down, out_w = take(6)
    qkv_b, up_b, gain_a, shift_a, gain_m, shift_m, cos_t, sin_t = take(8)
    seq_c_out, attn_out, mlp_out, act_out, gh_out, gp_out, mixed_out, o_out, stage_t, stage_c = take(10)
    seq_t_out, w_qkv_out, w_up_out, means_out, scales_out = take(5)
    early_out, part_out = take(2), take(1)[0]
    qkv_b_out, up_b_out = take(2)
    seq_t, seq_c, w_qkv, w_up, w_down, w_out = take(6)
    attn_in, mlp_in, q_ref, k_ref, v_ref, mixed, mixed_full, lse, slope, act, gh, gm = take(12)
    dq, dk, dv, gp, o_buf, means, scales, out_part, theirs = take(9)
    mine, came, last = take(2), take(2), take(2)
    near_r, near_s, home_c, z_r, z_s, y_r, y_s, wz_r, wz_s, wf_r, wf_s, own_c, out_c, o_c, pair_r, pair_s, last_r, last_s, early_c = take(19)

    z, hi, lo = place(lay)
    half, quarter = nlo * rows, weight_rows // nlo
    total = 2 * half
    rank = z * nhi + hi
    odd = lo % 2
    s = (1 - odd) * (lo // 2) + odd * (nz - 1 - lo // 2)
    score_scale = HD ** (-0.5)

    def dev(z, hi, lo):
        return (hi * nlo + lo, z)

    enter(
        [dev((z + i) % nz, hi, lo) for i in range(1, nz)]
        + [dev(z, hi, flip(lo, r, nlo)) for r in range(1, nlo)]
        + [dev(z, 1 - hi, lo)]
    )

    groups = []
    for part in range(3):
        groups.append((qkv, w_qkv, lambda rank, part=part: part * width + rank * HD, part * HD, HD))
    groups.append((up, w_up, lambda rank: rank * ff, 0, ff))
    groups.append((down, w_down, lambda rank: rank * ff, 0, ff))
    bits = list(reversed(lay.bits))

    def weight_z(g, i):
        src, dst, column, at, wide = groups[g]
        to = (z + i) % nz
        first = pl.multiple_of(column(to * nhi + hi), 128)
        return remote(
            src.at[pl.ds(pl.multiple_of(lo * quarter, quarter), quarter), pl.ds(first, wide)],
            dst.at[pl.ds(pl.multiple_of(z * weight_rows + lo * quarter, quarter), quarter), pl.ds(at, wide)],
            wz_s.at[g, i - 1], wz_r.at[g, i - 1], dev(to, hi, lo),
        )

    def weight_forward(g, i, r, b):
        _, dst, _, at, wide = groups[g]
        row = ((z + nz - i) % nz) * weight_rows + flip(lo, r, nlo) * quarter
        piece = dst.at[pl.ds(pl.multiple_of(row, quarter), quarter), pl.ds(at, wide)]
        k = bits.index(b)
        return remote(piece, piece, wf_s.at[g, i - 1, r, k], wf_r.at[g, i - 1, r ^ b], dev(z, hi, flip(lo, b, nlo)))

    inputs, staged, sequences = (tok, cot), (stage_t, stage_c), (seq_t, seq_c)
    distance = jnp.abs(z - s)

    def home_of(seq):
        late = seq // (nz // 2)
        return (1 - late) * (2 * seq) + late * (2 * (nz - 1 - seq) + 1)

    def seq_rows(a, which, r):
        row = which * half + flip(lo, r, nlo) * rows
        return sequences[a].at[pl.ds(pl.multiple_of(row, rows), rows)]

    def along(a, src, seq, way):
        return remote(src, staged[a].at[seq], z_s.at[a, seq, way], z_r.at[a, seq], dev((z + 1 - 2 * way + nz) % nz, hi, lo))

    def near(a, src, seq):
        return remote(src, seq_rows(a, hi, 0), near_s.at[a, seq], near_r.at[a, lo], dev(z, hi, home_of(seq)))

    def near_arrival(a, r):
        piece = seq_rows(a, hi, r)
        return remote(piece, piece, near_s.at[a, 0], near_r.at[a, flip(lo, r, nlo)], dev(z, hi, flip(lo, r, nlo)))

    def stay(a, src):
        return pltpu.make_async_copy(src, seq_rows(a, hi, 0), home_c.at[a])

    def across(a, src, r):
        return remote(src, seq_rows(a, hi, r), y_s.at[a, r], y_r.at[a, r], dev(z, 1 - hi, lo))

    def across_arrival(a, r):
        piece = seq_rows(a, 1 - hi, r)
        return remote(piece, piece, y_s.at[a, r], y_r.at[a, r], dev(z, 1 - hi, lo))

    def sources(a):
        yield (z >= 0, inputs[a], z, z < nz - 1, z > 0)
        for k in range(1, nz):
            yield (z >= k, staged[a].at[(z + nz - k) % nz], (z + nz - k) % nz, z < nz - 1, z < 0)
            yield (z < nz - k, staged[a].at[(z + k) % nz], (z + k) % nz, z < 0, z > 0)

    def dispatch(a, which):
        valid, src, seq, up, down = list(sources(a))[which]

        @pl.when(valid & up)
        def _():
            along(a, src, seq, 0).start()

        @pl.when(valid & down)
        def _():
            along(a, src, seq, 1).start()

        @pl.when(valid & (lo == home_of(seq)))
        def _():
            across(a, src, 0).start()
            stay(a, src).start()

        @pl.when(valid & (lo != home_of(seq)))
        def _():
            near(a, src, seq).start()

    def settle(a, which):
        valid, src, seq, up, down = list(sources(a))[which]

        @pl.when(valid & up)
        def _():
            along(a, src, seq, 0).wait_send()

        @pl.when(valid & down)
        def _():
            along(a, src, seq, 1).wait_send()

        @pl.when(valid & (lo == home_of(seq)))
        def _():
            across(a, src, 0).wait_send()

        @pl.when(valid & (lo != home_of(seq)))
        def _():
            near(a, src, seq).wait_send()

    def chain_event(a, k):
        for which, valid, seq in ((2 * k - 1, z >= k, (z + nz - k) % nz), (2 * k, z < nz - k, (z + k) % nz)):
            @pl.when(valid)
            def _(seq=seq):
                along(a, staged[a].at[seq], seq, 0).wait_recv()

            dispatch(a, which)

    def near_event(a, d):
        @pl.when(distance == d)
        def _():
            for r in range(1, nlo):
                near_arrival(a, r).wait_recv()
                across(a, seq_rows(a, hi, r), r).start()

    def forward_from(g, i, r):
        for b in bits:
            if r == 0 or b < low_bit(r):
                weight_forward(g, i, r, b).start()

    def weight_event(g, i, r):
        if r == 0:
            weight_z(g, i).wait_recv()
        else:
            weight_forward(g, i, r ^ low_bit(r), low_bit(r)).wait_recv()
        forward_from(g, i, r)

    def own_weight(g):
        if g == len(groups):
            first = pl.multiple_of(rank * HD - z * weight_rows, HD)
            return pltpu.make_async_copy(out_w.at[pl.ds(first, HD)], w_out, own_c.at[g])
        src, dst, column, at, wide = groups[g]
        first = pl.multiple_of(column(rank), 128)
        return pltpu.make_async_copy(
            src.at[:, pl.ds(first, wide)],
            dst.at[pl.ds(pl.multiple_of(z * weight_rows, weight_rows), weight_rows), pl.ds(at, wide)],
            own_c.at[g],
        )

    def own_start():
        for g in range(len(groups) + 1):
            own_weight(g).start()

    tall = 256
    blocks = total // tall
    kept = ((seq_c, seq_c_out), (attn_in, attn_out), (mlp_in, mlp_out), (act, act_out), (gh, gh_out), (gp, gp_out), (mixed, mixed_out),
            (seq_t, seq_t_out), (w_qkv, w_qkv_out), (w_up, w_up_out), (means, means_out), (scales, scales_out))

    def save(k):
        return pltpu.make_async_copy(*kept[k], out_c.at[k])

    def at_block(i):
        return pl.ds(i * tall, tall)

    def norm(which):
        if which == 0:
            stay(0, tok).wait()
        else:
            for r in range(nlo):
                across_arrival(0, r).wait_recv()
        start = (hi if which == 0 else 1 - hi) * half
        step = 64

        def body(i, carry):
            at = pl.ds(pl.multiple_of(start + i * step, step), step)
            values = seq_t[at, :].astype(f32)
            mean = jnp.mean(values, axis=-1, keepdims=True)
            center = values - mean
            scale = lax.rsqrt(jnp.mean(center * center, axis=-1, keepdims=True) + norm_epsilon)
            normed = center * scale
            attn_in[at, :] = (normed * gain_a[...] + shift_a[...]).astype(bf16)
            mlp_in[at, :] = (normed * gain_m[...] + shift_m[...]).astype(bf16)
            means[at, :] = jnp.broadcast_to(mean, (step, 128))
            scales[at, :] = jnp.broadcast_to(scale, (step, 128))
            return carry

        lax.fori_loop(0, half // step, body, 0)
        if which == 1:
            for k in (1, 2, 7, 10, 11):
                save(k).start()

    def project(i):
        if i == 0:
            for g in range(3):
                own_weight(g).wait()
            save(8).start()
        at = at_block(i)
        raw = jnp.dot(attn_in[at, :], w_qkv[...], preferred_element_type=f32) + qkv_b[...]
        q_ref[at, :] = turn(raw[:, :HD], cos_t[at, :], sin_t[at, :]).astype(bf16)
        k_ref[at, :] = turn(raw[:, HD : 2 * HD], cos_t[at, :], sin_t[at, :]).astype(bf16)
        v_ref[at, :] = raw[:, 2 * HD :].astype(bf16)

    def scores_of(i):
        reach = (i + 1) * tall
        scores = dot32(q_ref[at_block(i), :], k_ref[:reach, :], contract_last) * score_scale
        row = lax.broadcasted_iota(jnp.int32, scores.shape, 0) + i * tall
        column = lax.broadcasted_iota(jnp.int32, scores.shape, 1)
        return jnp.where(row >= column, scores, masked_score), reach

    def attend(i):
        scores, reach = scores_of(i)
        top = jnp.max(scores, axis=-1, keepdims=True)
        weights = jnp.exp(scores - top)
        summed = jnp.sum(weights, axis=-1, keepdims=True)
        full = dot32(weights.astype(bf16), v_ref[:reach, :]) / summed
        at = at_block(i)
        mixed_full[at, :] = full
        mixed[at, :] = full.astype(bf16)
        lse[at, :] = jnp.broadcast_to(top + jnp.log(summed), (tall, 128))
        if i == blocks - 1:
            save(6).start()

    def hidden(i):
        if i == 0:
            own_weight(3).wait()
            save(9).start()
        at = at_block(i)
        value = jnp.dot(mlp_in[at, :], w_up[...], preferred_element_type=f32) + up_b[...]
        cdf = (1.0 + lax.erf(value * (0.5 ** 0.5))) * 0.5
        act[at, :] = (value * cdf).astype(bf16)
        slope[at, :] = cdf + value * jnp.exp(value * value * (-0.5)) * 0.3989422804014327
        if i == blocks - 1:
            save(3).start()

    def cotangent_here():
        stay(1, cot).wait()
        for r in range(nlo):
            across_arrival(1, r).wait_recv()
        save(0).start()
        own_weight(5).wait()

    def back_mixed(i):
        at = at_block(i)
        gm[at, :] = dot32(seq_c[at, :], w_out[...], contract_last).astype(bf16)

    def back_hidden(i):
        if i == 0:
            up_b_out[...] = jnp.zeros_like(up_b_out)
        at = at_block(i)
        part = (jnp.dot(seq_c[at, :], w_down[...], preferred_element_type=f32) * slope[at, :]).astype(bf16)
        gh[at, :] = part
        up_b_out[...] += jnp.sum(part.astype(f32), axis=0, keepdims=True)
        if i == blocks - 1:
            save(4).start()

    def out_store(i):
        return pltpu.make_async_copy(o_buf.at[at_block(i)], o_out.at[at_block(i)], o_c.at[i])

    def out_block(i):
        if i == 0:
            own_weight(4).wait()
        at = at_block(i)
        part = jnp.dot(mixed[at, :], w_out[...], preferred_element_type=f32)
        part = part + dot32(act[at, :], w_down[...], contract_last)
        o_buf[at, :] = part.astype(bf16)
        out_store(i).start()

    def back_attend(i):
        if i == 0:
            dk[...] = jnp.zeros_like(dk)
            dv[...] = jnp.zeros_like(dv)
        at = at_block(i)
        scores, reach = scores_of(i)
        probs = jnp.exp(scores - lse[at, :1])
        grad = gm[at, :]
        row_dot = jnp.sum(grad.astype(f32) * mixed_full[at, :], axis=-1, keepdims=True)
        dv[:reach, :] += dot32(probs.astype(bf16), grad, contract_first)
        grad_scores = (probs * (dot32(grad, v_ref[:reach, :], contract_last) - row_dot)).astype(bf16)
        dq[at, :] = dot32(grad_scores, k_ref[:reach, :]) * score_scale
        dk[:reach, :] += dot32(grad_scores, q_ref[at, :], contract_first) * score_scale

    def back_project():
        qkv_b_out[...] = jnp.zeros_like(qkv_b_out)
        for i in range(blocks):
            at = at_block(i)
            part = jnp.concatenate(
                [turn(dq[at, :], cos_t[at, :], -sin_t[at, :]), turn(dk[at, :], cos_t[at, :], -sin_t[at, :]), dv[at, :]],
                axis=1,
            ).astype(bf16)
            gp[at, :] = part
            qkv_b_out[...] += jnp.sum(part.astype(f32), axis=0, keepdims=True)
        save(5).start()

    grain = width // (nz * nhi * nlo)
    span = nz * grain
    part_ff = ff // 2

    def product(c, h, rel):
        row = (h * nlo + differ(lo, rel, nlo)) * span
        rows_at = pl.ds(pl.multiple_of(row, span), span)
        return dot32(seq_c[:, rows_at], act[:, c * part_ff : (c + 1) * part_ff], contract_first).astype(bf16)

    def pair_send(c, h, k):
        return remote(
            theirs.at[h, k], came[c].at[h, k], pair_s.at[c, h, k], pair_r.at[c, h, k], dev(z, hi, flip(lo, 1, nlo))
        )

    def last_send(c, h):
        return remote(
            mine[c].at[h, 1], last[c].at[h], last_s.at[c, h], last_r.at[c, h], dev(z, hi, flip(lo, 2, nlo))
        )

    def pair_start(c):
        if c == 1:
            for h in range(nhi):
                for k in range(2):
                    pair_send(0, h, k).wait_send()

        def send(i, carry):
            h, k = i // 2, i % 2
            theirs[h, k] = product(c, h, 2 * k + 1)
            pair_send(c, h, k).start()
            return carry

        def keep_own(i, carry):
            h, k = i // 2, i % 2
            mine[c][h, k] = product(c, h, 2 * k)
            return carry

        lax.fori_loop(0, nhi * 2, send, 0)
        lax.fori_loop(0, nhi * 2, keep_own, 0)

    def pair_event(c):
        for k in (1, 0):
            for h in range(nhi):
                pair_send(c, h, k).wait_recv()
                add_rows(mine[c].at[h, k], mine[c].at[h, k], came[c].at[h, k], 64)
                if k == 1:
                    last_send(c, h).start()

    def early_store(c):
        return pltpu.make_async_copy(mine[c].at[:, 0], early_out[c], early_c.at[c])

    def last_event(c):
        for h in range(nhi):
            last_send(c, h).wait_recv()
            add_rows(mine[c].at[h, 0], mine[c].at[h, 0], last[c].at[h], 64)
        early_store(c).start()

    def part_store():
        return pltpu.make_async_copy(out_part, part_out, early_c.at[2])

    def out_product():
        step = min(512, width)
        for first in range(0, width, step):
            out_part[:, first : first + step] = dot32(
                mixed[...], seq_c[:, first : first + step], contract_first
            ).astype(bf16)
        part_store().start()

    act_of = dict(
        N=lambda a: dispatch(a, 0), Z=chain_event, D=near_event, W=lambda g, i: weight_z(g, i).start(), E=weight_event,
        WO=own_start, H=norm, K=project, AF=attend, U=hidden, CO=cotangent_here, GM=back_mixed, GH=back_hidden,
        O=out_block, AB=back_attend, BP=back_project,
        V=pair_start, VX=pair_event, VY=last_event, VO=out_product,
    )
    order_w = [(g, i) for g in range(len(groups)) for i in range(1, nz)]
    for item in block_schedule():
        act_of[item[0]](*item[1:])

    for k in range(len(kept)):
        save(k).wait()
    for i in range(blocks):
        out_store(i).wait()
    for c in range(2):
        early_store(c).wait()
        for h in range(nhi):
            last_send(c, h).wait_send()
            for k in range(2 if c == 1 else 0):
                pair_send(c, h, k).wait_send()
    part_store().wait()
    for g, i in order_w:
        weight_z(g, i).wait_send()
        for r in range(nlo):
            for b in bits:
                if r == 0 or b < low_bit(r):
                    weight_forward(g, i, r, b).wait_send()
    for a in range(2):
        for which in range(2 * nz - 1):
            settle(a, which)
        for r in range(1, nlo):
            across(a, seq_rows(a, hi, r), r).wait_send()


def block_all(lay, tok, cot, qkv, up, down, out_w, qkv_b, up_b, gains, cos_t, sin_t):
    rows, width = tok.shape
    nz, nlo = lay.nz, lay.nlo
    ff = up_b.shape[1]
    bits = len(lay.bits)
    anywhere = pl.BlockSpec(memory_space=pl.ANY)
    inside = pl.BlockSpec(memory_space=pltpu.VMEM)
    dma = pltpu.SemaphoreType.DMA
    bf16, f32 = jnp.bfloat16, jnp.float32
    total = 2 * nlo * rows

    def shape(*dims, kind=bf16):
        return jax.ShapeDtypeStruct(dims, kind)

    def vmem(*dims, kind=bf16):
        return pltpu.VMEM(dims, kind)

    span = width // (lay.nhi * nlo)
    return pl.pallas_call(
        functools.partial(block_kernel, lay, (rows, width, qkv.shape[0], ff)),
        out_shape=[
            shape(total, width), shape(total, width), shape(total, width), shape(total, ff), shape(total, ff),
            shape(total, 3 * HD), shape(total, HD), shape(total, width),
            shape(nz, rows, width), shape(nz, rows, width),
            shape(total, width), shape(width, 3 * HD), shape(width, ff), shape(total, 128, kind=f32), shape(total, 128, kind=f32),
            shape(lay.nhi, span, ff // 2), shape(lay.nhi, span, ff // 2), shape(HD, width),
            shape(1, 3 * HD, kind=f32), shape(1, ff, kind=f32),
        ],
        in_specs=[anywhere] * 6 + [inside] * 8,
        out_specs=[anywhere] * 18 + [inside] * 2,
        scratch_shapes=[
            vmem(total, width), vmem(total, width), vmem(width, 3 * HD), vmem(width, ff), vmem(width, ff), vmem(HD, width),
            vmem(total, width), vmem(total, width), vmem(total, HD), vmem(total, HD), vmem(total, HD), vmem(total, HD),
            vmem(total, HD, kind=f32), vmem(total, 128, kind=f32), vmem(total, ff, kind=f32), vmem(total, ff),
            vmem(total, ff), vmem(total, HD),
            vmem(total, HD, kind=f32), vmem(total, HD, kind=f32), vmem(total, HD, kind=f32), vmem(total, 3 * HD),
            vmem(total, width), vmem(total, 128, kind=f32), vmem(total, 128, kind=f32),
            vmem(HD, width), *[vmem(lay.nhi, 2, span, ff // 2)] * 5, *[vmem(lay.nhi, span, ff // 2)] * 2,
            dma((2, nlo)), dma((2, nz)), dma((2,)), dma((2, nz)), dma((2, nz, 2)), dma((2, nlo)), dma((2, nlo)),
            dma((5, nz - 1)), dma((5, nz - 1)), dma((5, nz - 1, nlo)), dma((5, nz - 1, nlo, bits)), dma((6,)),
            dma((12,)), dma((total // 256,)),
            dma((2, lay.nhi, 2)), dma((2, lay.nhi, 2)), dma((2, lay.nhi)), dma((2, lay.nhi)), dma((3,)),
        ],
        compiler_params=pltpu.CompilerParams(
            collective_id=3, has_side_effects=True, vmem_limit_bytes=63 * 1024 * 1024
        ),
        name="block_all",
    )(tok, cot, qkv, up, down, out_w, qkv_b, up_b, *gains, cos_t, sin_t)


def add_rows(into, left, right, step):
    rows = into.shape[0]
    step = min(step, rows)

    def body(k, carry):
        at = pl.ds(pl.multiple_of(k * step, step), step)
        into[at, :] = (left[at, :].astype(jnp.float32) + right[at, :].astype(jnp.float32)).astype(into.dtype)
        return carry

    lax.fori_loop(0, rows // step, body, 0)


def differ(one, other, count):
    result, bit = 0, 1
    while bit < count:
        result = result + bit * ((one // bit + other // bit) % 2)
        bit *= 2
    return result


def scatter_chunks(width, ff, repeat):
    cut = max(ff // 2, 256)
    chunks = []
    for source in (0, 1):
        for first in range(0, ff, cut):
            chunks.append((source, first, cut, lambda rank, first=first: rank * ff + first, True))
    for part in range(3):
        chunks.append((2, part * HD, HD, lambda rank, part=part: part * width + (rank // repeat) * HD, repeat == 1))
    return chunks


def scatter_schedule(nz, nlo, n_chunks, stages, n_slabs):
    if n_slabs:
        return [
            ("L",), ("Y", 0), ("Y", 1), ("C", 0), ("C", 1), ("P",), ("C", 2), ("X", 0, 0), ("X", 0, 1), ("C", 3),
            ("X", 2, 0), ("S", 0), ("X", 3, 0), ("S", 1), ("A", 0, 0), ("S", 2), ("A", 0, 1), ("S", 3), ("X", 1, 0),
            ("X", 1, 1), ("X", 2, 1), ("S", 4), ("A", 0, 2), ("S", 5), ("S", 6), ("A", 0, 3), ("S", 7), ("M",), ("C", 4),
            ("N", 0), ("A", 1, 0), ("X", 3, 1), ("C", 5), ("N", 1), ("X", 4, 0), ("N", 2), ("Y", 2), ("Y", 3), ("C", 6),
            ("A", 1, 1), ("A", 1, 2), ("B", 0, 0), ("A", 1, 3), ("N", 3), ("Q", 0), ("X", 5, 0), ("B", 0, 1),
            ("B", 1, 0), ("N", 4), ("A", 2, 0), ("X", 4, 1), ("X", 6, 0), ("A", 2, 1), ("B", 0, 2), ("B", 1, 1),
            ("X", 5, 1), ("A", 2, 2), ("X", 6, 1), ("B", 1, 2), ("A", 2, 3), ("Q", 1), ("A", 3, 0), ("B", 2, 0),
            ("A", 3, 1), ("B", 2, 1), ("A", 3, 2), ("B", 2, 2), ("A", 3, 3), ("B", 3, 0), ("F", 0), ("F", 1),
            ("B", 3, 1), ("B", 3, 2), ("F", 2), ("F", 3), ("G", 0), ("G", 1), ("G", 2), ("G", 3), ("G", 4), ("G", 5),
            ("G", 6),
        ]
    timed = [(51 if n_slabs else -4, ("M",)), (4, ("P",)), (-3, ("L",)), (-2, ("Y", 0)), (-2, ("Y", 1)), (52, ("Y", 2)), (52, ("Y", 3))]
    for k in range(n_slabs):
        timed.append((30 + 2 * k, ("S", k)))
    for g in range(n_chunks):
        timed.append((0 + 4 * g, ("C", g)))
        for t in range(stages):
            timed.append((10 + 14 * g + 25 * t, ("X", g, t)))
    for b, (first, step, chain, hop) in enumerate(((14, 11.4, 66, 11), (14, 11.4, 66, 11), (66, 11.4, 112, 11), (66, 11.4, 112, 11))):
        for q in range(nlo):
            timed.append((first + step * q, ("A", b, q)))
        for m in range(nz - 1):
            timed.append((chain + hop * m, ("B", b, m)))
        timed.append((chain + hop * (nz - 1), ("F", b)))
    for t in range(stages):
        timed.append((100 + 10 * t, ("Q", t)))
    for t in range(2 * stages + 1):
        timed.append((56 + 6 * t, ("N", t)))
    timed.sort(key=lambda entry: entry[0])
    return [entry[1] for entry in timed] + [("G", g) for g in range(n_chunks)]


def scatter_kernel(lay, sizes, *refs):
    rows, width, ff, repeat, inside = sizes
    nz, nlo, nhi = lay.nz, lay.nlo, lay.nhi
    stages = len(lay.bits)
    chunks = scatter_chunks(width, ff, repeat)
    n = len(chunks)
    refs = list(refs)

    def take(count):
        taken = refs[:count]
        del refs[:count]
        return taken

    partial_o, = take(1)
    if inside:
        x_up, x_qkv, g_up, g_qkv, small = take(5)
        x_down = g_down = g_out = None
        seq_t, w_qkv, w_up, means_in, scales_in = take(5)
        ready, part_in = take(2), take(1)[0]
        gain_a, gain_m = take(2)
    else:
        x_down, x_up, x_qkv, g_down, g_up, g_qkv, g_out, small = take(8)
        partial_s, = take(1)
        ready = []
    sum_o, sum_s, all_down, all_up, all_qkv, all_out, small_sum = take(7)
    own, across_buf, near_buf, chain_buf = take(4)
    acc = [None] * len(ready) + take(n - len(ready))
    got = [None] * len(ready) + [take(stages) for _ in range(n - len(ready))]
    out_acc, = take(1)
    out_got = take(stages)
    small_buf, small_got = take(2)
    left, = take(1)
    right_down = right_out = None
    if inside:
        right_up, right_qkv = take(2)
    else:
        right_down, right_up, right_qkv, right_out = take(4)
    staged, out_part = take(2)
    if inside:
        s_buf, ring_t, ring_q, ring_u, means, scales, small_first = take(7)
        partial_s = s_buf
    else:
        small_first = small
    (own_c, y_r, y_s, near_r, near_s, z_r, z_s, st_r, st_s, g_r, g_s, keep_c,
     out_r, out_s, move_r, move_s, sm_r, sm_s, left_c, right_c) = take(20)
    if inside:
        slab_c, stat_c = take(2)

    z, hi, lo = place(lay)
    rank = z * nhi + hi
    half = nlo * rows
    grain = width // (nz * nhi * nlo)
    span = nz * grain

    def dev(z, hi, lo):
        return (hi * nlo + lo, z)

    ctx = hi * nlo + lo
    moves = (ctx != rank) | (z != lo)
    barrier = pltpu.get_barrier_semaphore()
    mates = [
        dev((z + dz) % nz, flip(hi, dh, nhi), lo) for dz in range(nz) for dh in range(nhi) if dz or dh
    ] + [dev(z, hi, flip(lo, r, nlo)) for r in range(1, nlo)]
    for device in mates:
        pl.semaphore_signal(barrier, inc=1, device_id=device, device_id_type=MESH)

    @pl.when(moves)
    def _():
        pl.semaphore_signal(barrier, inc=1, device_id=(rank, lo), device_id_type=MESH)
        pl.semaphore_signal(barrier, inc=1, device_id=dev(ctx // nhi, ctx % nhi, z), device_id_type=MESH)
        pl.semaphore_wait(barrier, len(mates) + 2)

    @pl.when(jnp.logical_not(moves))
    def _():
        pl.semaphore_wait(barrier, len(mates))

    partial, summed = (partial_o, partial_s), (sum_o, sum_s)

    lanes = width // 2

    def part(b):
        return b // 2, pl.ds((b % 2) * lanes, lanes)

    def load_own(b, q):
        a, at = part(b)
        row = pl.multiple_of(hi * half + q * rows, rows)
        return pltpu.make_async_copy(partial[a].at[pl.ds(row, rows), at], own.at[a, q % 2, :, at], own_c.at[b, q % 2])

    def own_rows(b, q):
        a, at = part(b)
        if a == 1 and inside:
            return s_buf.at[pl.ds(pl.multiple_of(hi * half + q * rows, rows), rows), at]
        return own.at[a, q % 2, :, at]

    def across(b, q):
        a, at = part(b)
        row = pl.multiple_of((1 - hi) * half + q * rows, rows)
        return remote(
            partial[a].at[pl.ds(row, rows), at], across_buf.at[a, q, :, at], y_s.at[b, q], y_r.at[b, q], dev(z, 1 - hi, lo)
        )

    def near(b, q):
        a, at = part(b)
        return remote(
            across_buf.at[a, q, :, at], near_buf.at[a, lo, :, at], near_s.at[b, q], near_r.at[b, lo], dev(z, hi, q)
        )

    def near_arrival(b, q):
        a, at = part(b)
        piece = near_buf.at[a, q, :, at]
        return remote(piece, piece, near_s.at[b, q], near_r.at[b, q], dev(z, hi, q))

    def along(b, seq, way):
        a, at = part(b)
        slot = seq if way == 0 else jnp.where(z == seq + 1, nz, seq)
        return remote(
            near_buf.at[a, lay.lo_of_seq[seq], :, at], chain_buf.at[a, slot, :, at], z_s.at[b, seq], z_r.at[b, seq, way],
            dev((z + 1 - 2 * way + nz) % nz, hi, lo),
        )

    def start_across(b):
        a, _ = part(b)
        for q in range(0 if a == 1 and inside else 2):
            load_own(b, q).start()
        for q in range(nlo):
            across(b, q).start()

    def across_event(b, q):
        a, at = part(b)
        if not (a == 1 and inside):
            load_own(b, q).wait()
        across(b, q).wait_recv()
        mine, arrived = own_rows(b, q), across_buf.at[a, q, :, at]

        @pl.when(lo == q)
        def _():
            add_rows(near_buf.at[a, q, :, at], mine, arrived, 32)

        @pl.when(lo != q)
        def _():
            add_rows(arrived, mine, arrived, 32)
            near(b, q).start()

        if q + 2 < nlo and not (a == 1 and inside):
            load_own(b, q + 2).start()

    def chain_event(b, seq, way):
        a, at = part(b)
        q = lay.lo_of_seq[seq]
        active = (z < seq) if way == 0 else (z > seq)
        first = (z == 0) if way == 0 else (z == nz - 1)

        @pl.when(active)
        def _():
            @pl.when(lo != q)
            def _():
                near_arrival(b, q).wait_recv()

            @pl.when(jnp.logical_not(first))
            def _():
                along(b, seq, way).wait_recv()
                mine = near_buf.at[a, q, :, at]
                add_rows(mine, mine, chain_buf.at[a, seq, :, at], 32)

            along(b, seq, way).start()

    def chain_pair(b, m):
        @pl.when(z < nz // 2)
        def _():
            chain_event(b, nz - 1 - m, 0)
            chain_event(b, m, 1)

        @pl.when(z >= nz // 2)
        def _():
            chain_event(b, m, 1)
            chain_event(b, nz - 1 - m, 0)

    def final_event(b):
        a, at = part(b)
        late = z // (nz // 2)
        home = (1 - late) * (2 * z) + late * (2 * (nz - 1 - z) + 1)
        piece = near_buf.at[a, home, :, at]

        @pl.when(lo != home)
        def _():
            remote(piece, piece, near_s.at[b, 0], near_r.at[b, home], dev(z, hi, home)).wait_recv()

        @pl.when(z > 0)
        def _():
            arrived = chain_buf.at[a, z, :, at]
            remote(arrived, arrived, z_s.at[b, 0], z_r.at[b, z, 0], dev(z, hi, lo)).wait_recv()

        @pl.when(z < nz - 1)
        def _():
            arrived = chain_buf.at[a, nz, :, at]
            remote(arrived, arrived, z_s.at[b, 0], z_r.at[b, z, 1], dev(z, hi, lo)).wait_recv()

        def body(k, carry):
            line = pl.ds(pl.multiple_of(k * 16, 16), 16)
            total = piece[line, :].astype(jnp.float32)
            total = total + jnp.where(z > 0, chain_buf[a, z, line, at].astype(jnp.float32), 0.0)
            total = total + jnp.where(z < nz - 1, chain_buf[a, nz, line, at].astype(jnp.float32), 0.0)
            summed[a][line, at] = total
            return carry

        lax.fori_loop(0, rows // 16, body, 0)

    targets = (all_down, all_up, all_qkv)
    lefts = (x_down, x_up, x_qkv)
    n_slots = left.shape[0]
    slots = [0, 0, 1] if inside else [source % n_slots for source in range(3)]
    rights = ((g_down, right_down), (g_up, right_up), (g_qkv, right_qkv), (g_out, right_out))

    def load_left(source):
        return pltpu.make_async_copy(lefts[source], left.at[slots[source]], left_c.at[source])

    def load_right(source):
        return pltpu.make_async_copy(*rights[source], right_c.at[source])

    def start_loads():
        if inside:
            for copy in stat_loads() + slab_loads(0):
                copy.start()
            part_load().start()
            for source in (1, 2):
                load_left(source).start()
                load_right(source).start()
            return
        for source in (0, 3, 1, 2):
            if source < n_slots:
                load_left(source).start()
            load_right(source).start()

    def part_load():
        return pltpu.make_async_copy(part_in, out_part, right_c.at[3])

    right_waited = set()

    def right_here(source):
        if source not in right_waited:
            right_waited.add(source)
            load_right(source).wait()

    def loaded(source):
        load_left(source).wait()
        right_here(source)

    def product(g, h, rel):
        source, first, wide, _, _ = chunks[g]
        row = (h * nlo + differ(lo, rel, nlo)) * span
        rows_at = pl.ds(pl.multiple_of(row, span), span)
        part = lax.dot_general(
            left[slots[source], :, rows_at], rights[source][1][:, first : first + wide],
            contract_first, preferred_element_type=jnp.float32,
        )
        return part.astype(jnp.bfloat16)

    def stage_pieces(t):
        return [rel for rel in range(nlo) if rel % (2 << t) == (1 << t)]

    def stage_send(g, t, h, rel):
        if t == 0:
            src = staged.at[g % 3, h, rel // 2, :, pl.ds(0, chunks[g][2])]
        else:
            src = acc[g].at[h, rel // 2]
        k = rel >> (t + 1)
        return remote(
            src, got[g][t].at[h, k], st_s.at[g, t, h, k], st_r.at[g, t, h, k], dev(z, hi, flip(lo, 1 << t, nlo))
        )

    pairs = nhi * (nlo // 2)

    def start_chunk(g):
        source, first, wide, _, _ = chunks[g]
        if g < len(ready):
            return
        if first == 0:
            loaded(source)
        if g >= 3 + len(ready):
            for h in range(nhi):
                for rel in stage_pieces(0):
                    stage_send(g - 3, 0, h, rel).wait_send()

        def send(i, carry):
            h, k = i // (nlo // 2), i % (nlo // 2)
            staged[g % 3, h, k, :, :wide] = product(g, h, 2 * k + 1)
            stage_send(g, 0, h, 2 * k + 1).start()
            return carry

        def keep_own(i, carry):
            h, k = i // (nlo // 2), i % (nlo // 2)
            acc[g][h, k] = product(g, h, 2 * k)
            return carry

        lax.fori_loop(0, pairs, send, 0)
        lax.fori_loop(0, pairs, keep_own, 0)
        if inside:
            return
        if g == 0:
            out_start()
        if (g + 1 == n or chunks[g + 1][0] != source) and source + n_slots < 3:
            load_left(source + n_slots).start()

    def stage_event(g, t):
        if g < len(ready):
            if t == 0:
                deliver(g)
            return
        order = list(reversed(range(0, nlo, 2 << t)))
        for h in range(nhi):
            for rel in order:
                k = rel >> (t + 1)
                stage_send(g, t, h, rel | (1 << t)).wait_recv()
                add_rows(acc[g].at[h, rel // 2], acc[g].at[h, rel // 2], got[g][t].at[h, k], 64)
                if t + 1 < stages and rel % (4 << t) == (2 << t):
                    stage_send(g, t + 1, h, rel).start()
        if t + 1 == stages:
            deliver(g)

    def owner_send(g, dz, dh):
        source, _, wide, column, _ = chunks[g]
        to_z, to_hi = (z + dz) % nz, flip(hi, dh, nhi)
        first = pl.multiple_of(column(rank), 128)
        k = dz * nhi + dh
        from_rows = pl.ds(pl.multiple_of(to_z * grain, grain), grain)
        return remote(
            ready[g].at[to_hi, from_rows] if g < len(ready) else acc[g].at[to_hi, 0, from_rows],
            targets[source].at[:, pl.ds(first, wide)],
            g_s.at[g, k], g_r.at[g, k], dev(to_z, to_hi, lo),
        )

    def owner_arrival(g, dz, dh):
        source, _, wide, column, _ = chunks[g]
        from_z, from_hi = (z + nz - dz) % nz, flip(hi, dh, nhi)
        first = pl.multiple_of(column(from_z * nhi + from_hi), 128)
        piece = targets[source].at[:, pl.ds(first, wide)]
        k = dz * nhi + dh
        return remote(piece, piece, g_s.at[g, k], g_r.at[g, k], dev(from_z, from_hi, lo))

    def keep(g):
        source, _, wide, column, _ = chunks[g]
        first = pl.multiple_of(column(rank), 128)
        from_rows = pl.ds(pl.multiple_of(z * grain, grain), grain)
        return pltpu.make_async_copy(
            ready[g].at[hi, from_rows] if g < len(ready) else acc[g].at[hi, 0, from_rows],
            targets[source].at[:, pl.ds(first, wide)], keep_c.at[g],
        )

    others = [(dz, dh) for dz in range(nz) for dh in range(nhi) if dz or dh]

    def when_sent(g, from_hi, act):
        if chunks[g][4]:
            act()
        else:
            pl.when(from_hi % repeat == 0)(act)

    def deliver(g):
        def act():
            for dz, dh in others:
                owner_send(g, dz, dh).start()
            keep(g).start()

        when_sent(g, hi, act)

    def finish_chunk(g):
        def sent():
            for dz, dh in others:
                owner_send(g, dz, dh).wait_send()
            keep(g).wait()

        when_sent(g, hi, sent)
        for dz, dh in others:
            when_sent(g, flip(hi, dh, nhi), lambda dz=dz, dh=dh: owner_arrival(g, dz, dh).wait_recv())

    def out_rows(rel):
        return out_part.at[pl.ds(pl.multiple_of(flip(lo, rel, nlo) * grain, grain), grain)]

    def out_send(t, rel):
        src = out_rows(rel) if t == 0 else out_acc.at[rel // 2]
        k = rel >> (t + 1)
        return remote(src, out_got[t].at[k], out_s.at[t, k], out_r.at[t, k], dev(z, hi, flip(lo, 1 << t, nlo)))

    def out_start():
        if inside:
            part_load().wait()
            for rel in stage_pieces(0):
                out_send(0, rel).start()
            return
        load_right(3).wait()
        wide = min(512, width)

        def body(i, carry):
            at = pl.ds(pl.multiple_of(i * wide, wide), wide)
            part = lax.dot_general(
                right_out[...], left[0, :, at], contract_first, preferred_element_type=jnp.float32
            )
            out_part[:, at] = part.astype(jnp.bfloat16)
            return carry

        lax.fori_loop(0, width // wide, body, 0)
        for rel in stage_pieces(0):
            out_send(0, rel).start()

    def out_event(t):
        for rel in reversed(range(0, nlo, 2 << t)):
            out_send(t, rel | (1 << t)).wait_recv()
            mine = out_rows(rel) if t == 0 else out_acc.at[rel // 2]
            add_rows(out_acc.at[rel // 2], mine, out_got[t].at[rel >> (t + 1)], 16)
            if t + 1 < stages and rel % (4 << t) == (2 << t):
                out_send(t + 1, rel).start()
        if t + 1 == stages:
            @pl.when(moves)
            def _():
                out_move().start()

            @pl.when(jnp.logical_not(moves))
            def _():
                out_stay().start()

    def out_move():
        return remote(out_acc.at[0], all_out, move_s, move_r, (rank, lo))

    def out_stay():
        return pltpu.make_async_copy(out_acc.at[0], all_out, move_s)

    doubling = (
        [dev(flip(z, b, nz), hi, lo) for b in lay.bits]
        + [dev(z, hi, flip(lo, lay.bits[0], nlo))]
        + [dev(z, flip(hi, 1, nhi), lo)]
        + [dev(z, hi, flip(lo, b, nlo)) for b in lay.bits[1:]]
    )

    def small_send(t):
        src = small_first if t == 0 else small_buf.at[t - 1]
        return remote(src, small_got.at[t], sm_s.at[t], sm_r.at[t], doubling[t])

    def small_event(t):
        small_send(t).wait_recv()
        mine = small_first if t == 0 else small_buf.at[t - 1]
        into = small_sum if t + 1 == len(doubling) else small_buf.at[t]
        into[...] = mine[...] + small_got[t]
        if t + 1 < len(doubling):
            small_send(t + 1).start()

    slab = 256
    wide = slab // 128

    def slab_loads(k):
        at = pl.ds(k * slab, slab)
        return [
            pltpu.make_async_copy(seq_t.at[:, at], ring_t.at[k % 2], slab_c.at[k % 2, 0]),
            pltpu.make_async_copy(w_qkv.at[at], ring_q.at[k % 2], slab_c.at[k % 2, 1]),
            pltpu.make_async_copy(w_up.at[at], ring_u.at[k % 2], slab_c.at[k % 2, 2]),
        ]

    def stat_loads():
        return [
            pltpu.make_async_copy(means_in, means, stat_c.at[0]),
            pltpu.make_async_copy(scales_in, scales, stat_c.at[1]),
        ]

    def in_slab(k):
        if k == 0:
            small_first[...] = small[...]
            for copy in stat_loads():
                copy.wait()
            right_here(1)
            right_here(2)
        for copy in slab_loads(k):
            copy.wait()
        if (k + 1) * slab < width:
            for copy in slab_loads(k + 1):
                copy.start()
        features = pl.ds(k * slab, slab)

        def body(i, sums):
            at = pl.ds(pl.multiple_of(i * 256, 256), 256)
            grad_a = dot32(right_qkv[at, :], ring_q[k % 2], contract_last)
            grad_m = dot32(right_up[at, :], ring_u[k % 2], contract_last)
            s_buf[at, features] = (grad_a * gain_a[:, features] + grad_m * gain_m[:, features]).astype(jnp.bfloat16)
            mean, scale = jnp.concatenate([means[at, :]] * wide, axis=1), jnp.concatenate([scales[at, :]] * wide, axis=1)
            normed = (ring_t[k % 2, at, :].astype(jnp.float32) - mean) * scale
            terms = (grad_a * normed, grad_a, grad_m * normed, grad_m)
            return tuple(have + jnp.sum(term.reshape(32, 8, slab), axis=0) for have, term in zip(sums, terms))

        sums = lax.fori_loop(0, 2 * half // 256, body, (jnp.zeros((8, slab), jnp.float32),) * 4)
        first = small.shape[0] - 4 * width // 128
        for m, have in enumerate(sums):
            line = jnp.sum(have, axis=0, keepdims=True)
            for j in range(wide):
                row = first + (m * width + k * slab) // 128 + j
                small_first[row : row + 1, :] = line[:, j * 128 : (j + 1) * 128]

    act = dict(
        S=in_slab, Y=start_across, P=out_start if inside else (lambda: None), A=across_event, B=chain_pair, F=final_event, C=start_chunk, X=stage_event, G=finish_chunk,
        L=start_loads, Q=out_event, M=lambda: small_send(0).start(), N=small_event,
    )
    for item in scatter_schedule(nz, nlo, n, stages, width // slab if inside else 0):
        act[item[0]](*item[1:])

    for b in range(4):
        for q in range(nlo):
            across(b, q).wait_send()

            @pl.when(lo != q)
            def _(b=b, q=q):
                near(b, q).wait_send()

        for seq in range(nz):
            @pl.when(z != seq)
            def _(b=b, seq=seq):
                along(b, seq, 0).wait_send()

    for g in range(n):
        for t in range(stages):
            if g < len(ready) or (t == 0 and g + 3 < n):
                continue
            for h in range(nhi):
                for rel in stage_pieces(t):
                    stage_send(g, t, h, rel).wait_send()
    for t in range(stages):
        for rel in stage_pieces(t):
            out_send(t, rel).wait_send()

    @pl.when(moves)
    def _():
        out_move().wait()

    @pl.when(jnp.logical_not(moves))
    def _():
        out_stay().wait()

    for t in range(len(doubling)):
        small_send(t).wait_send()


def scatter_all(lay, partial_o, partial_s, x_down, x_up, x_qkv, g_down, g_up, g_qkv, g_out, terms, small):
    total, width = partial_o.shape
    nz, nlo, nhi = lay.nz, lay.nlo, lay.nhi
    rows = total // (nhi * nlo)
    ranks = nz * nhi
    ff = g_down.shape[1]
    repeat = max(1, ranks // H)
    grain = width // (ranks * nlo)
    span = nz * grain
    stages = len(lay.bits)
    chunks = scatter_chunks(width, ff, repeat)
    n = len(chunks)
    steps = 2 * stages + 1
    anywhere = pl.BlockSpec(memory_space=pl.ANY)
    inside = pl.BlockSpec(memory_space=pltpu.VMEM)
    dma = pltpu.SemaphoreType.DMA
    bf16, f32 = jnp.bfloat16, jnp.float32
    scratch = [
        pltpu.VMEM((2, 2, rows, width), bf16),
        pltpu.VMEM((2, nlo, rows, width), bf16),
        pltpu.VMEM((2, nlo, rows, width), bf16),
        pltpu.VMEM((2, nz + 1, rows, width), bf16),
    ]
    here = chunks[2:] if terms is not None else chunks
    for chunk in here:
        scratch.append(pltpu.VMEM((nhi, nlo // 2, span, chunk[2]), bf16))
    for chunk in here:
        for t in range(stages):
            scratch.append(pltpu.VMEM((nhi, nlo >> (t + 1), span, chunk[2]), bf16))
    scratch.append(pltpu.VMEM((nlo // 2, grain, width), bf16))
    for t in range(stages):
        scratch.append(pltpu.VMEM((nlo >> (t + 1), grain, width), bf16))
    scratch += [pltpu.VMEM((steps,) + small.shape, f32), pltpu.VMEM((steps,) + small.shape, f32)]
    widest = max(chunk[2] for chunk in chunks)
    fused = terms is not None
    scratch += [
        pltpu.VMEM((2 if total <= 1024 else 1, total, width), bf16),
        *[pltpu.VMEM(g.shape, bf16) for g in ((g_up, g_qkv) if fused else (g_down, g_up, g_qkv, g_out))],
        pltpu.VMEM((3, nhi, nlo // 2, span, widest), bf16),
        pltpu.VMEM((width // ranks, width), bf16),
    ]
    if fused:
        scratch += [
            pltpu.VMEM((total, width), bf16), pltpu.VMEM((2, total, 256), bf16), pltpu.VMEM((2, 256, 3 * HD), bf16),
            pltpu.VMEM((2, 256, ff), bf16), pltpu.VMEM((total, 128), f32), pltpu.VMEM((total, 128), f32),
            pltpu.VMEM(small.shape, f32),
        ]
    most = nlo // 2
    scratch += [
        dma((4, 2)), dma((4, nlo)), dma((4, nlo)), dma((4, nlo)), dma((4, nlo)), dma((4, nz, 2)), dma((4, nz)),
        dma((n, stages, nhi, most)), dma((n, stages, nhi, most)), dma((n, ranks)), dma((n, ranks)),
        dma((n,)), dma((stages, most)), dma((stages, most)), dma, dma, dma((steps,)), dma((steps,)), dma((3,)), dma((4,)),
    ]
    if fused:
        scratch += [dma((2, 3)), dma((2,))]
    return pl.pallas_call(
        functools.partial(scatter_kernel, lay, (rows, width, ff, repeat, fused)),
        out_shape=[
            jax.ShapeDtypeStruct((rows, width), f32),
            jax.ShapeDtypeStruct((rows, width), f32),
            jax.ShapeDtypeStruct((grain, ff * ranks), bf16),
            jax.ShapeDtypeStruct((grain, ff * ranks), bf16),
            jax.ShapeDtypeStruct((grain, 3 * width), bf16),
            jax.ShapeDtypeStruct((grain, width), bf16),
            jax.ShapeDtypeStruct(small.shape, f32),
        ],
        in_specs=([anywhere] * 5 + [inside] + [anywhere] * 8 + [inside] * 2) if fused else ([anywhere] * 8 + [inside, anywhere]),
        out_specs=[inside, inside, anywhere, anywhere, anywhere, anywhere, inside],
        scratch_shapes=scratch,
        compiler_params=pltpu.CompilerParams(
            collective_id=2, has_side_effects=True, vmem_limit_bytes=62 * 1024 * 1024
        ),
        name="scatter_all",
    )(
        partial_o,
        *((x_up, x_qkv, g_up, g_qkv, small, *terms) if fused else (x_down, x_up, x_qkv, g_down, g_up, g_qkv, g_out, small, partial_s)),
    )


def plain_block(lay, operands):
    f32, bf16 = jnp.float32, jnp.bfloat16
    (own, own_cotangent, qkv_weight, qkv_bias, out_weight, up_weight, up_bias, down_weight,
     attn_norm_gain, attn_norm_bias, mlp_norm_gain, mlp_norm_bias) = operands
    nz, nlo, nhi = lay.nz, lay.nlo, lay.nhi
    ranks = nz * nhi
    rows, width = own.shape
    weight_rows = qkv_weight.shape[0]
    half = nlo * rows
    z, hi, lo = place(lay)
    rank = z * nhi + hi
    ff = up_weight.shape[1] // ranks
    repeat = max(1, ranks // H)
    head = rank // repeat
    score_scale = HD ** (-0.5)
    seq_tokens, seq_cotangent, qkv_here, up_here, down_here = gather_all(
        lay, own, own_cotangent, qkv_weight, up_weight, down_weight
    )
    own_qkv = jnp.concatenate(
        [
            lax.dynamic_slice(qkv_weight, (0, part * width + head * HD), (weight_rows, HD))
            for part in range(3)
        ],
        axis=1,
    )
    own_up = lax.dynamic_slice(up_weight, (0, rank * ff), (weight_rows, ff))
    own_down = lax.dynamic_slice(down_weight, (0, rank * ff), (weight_rows, ff))
    qkv_here = lax.dynamic_update_slice(qkv_here, own_qkv, (z * weight_rows, 0))
    up_here = lax.dynamic_update_slice(up_here, own_up, (z * weight_rows, 0))
    down_here = lax.dynamic_update_slice(down_here, own_down, (z * weight_rows, 0))
    out_head = lax.dynamic_slice(out_weight, (head * HD - z * weight_rows, 0), (HD, width))
    out_rows = width // ranks
    out_at = rank * out_rows - head * HD

    positions = jnp.arange(2 * half, dtype=jnp.int32)

    normed, _ = normalize(seq_tokens.astype(f32))
    attn_in = (normed * attn_norm_gain + attn_norm_bias).astype(bf16)
    mlp_in = (normed * mlp_norm_gain + mlp_norm_bias).astype(bf16)
    bias_here = jnp.concatenate(
        [lax.dynamic_slice(qkv_bias, (part * width + head * HD,), (HD,)) for part in range(3)]
    )
    projected = dot32(attn_in, qkv_here) + bias_here
    queries = rotary(projected[:, :HD], positions).astype(bf16)
    keys = rotary(projected[:, HD : 2 * HD], positions).astype(bf16)
    values = projected[:, 2 * HD :].astype(bf16)
    causal = positions[:, None] >= positions[None, :]
    scores = jnp.where(causal, dot32(queries, keys, contract_last) * score_scale, masked_score)
    top = jnp.max(scores, axis=-1, keepdims=True)
    weights = jnp.where(causal, jnp.exp(scores - top), 0.0)
    total = jnp.sum(weights, axis=-1, keepdims=True)
    mixed_full = dot32(weights.astype(bf16), values) / total
    log_total = top + jnp.log(total)
    mixed = mixed_full.astype(bf16)
    mixed_mine = lax.dynamic_slice(mixed, (0, out_at), (mixed.shape[0], out_rows))
    out_mine = lax.dynamic_slice(out_head, (out_at, 0), (out_rows, width))
    hidden = dot32(mlp_in, up_here) + lax.dynamic_slice(up_bias, (rank * ff,), (ff,))
    activated_full, gelu_pull = jax.vjp(exact_gelu, hidden)
    activated = activated_full.astype(bf16)
    out_partial = dot32(mixed_mine, out_mine) + dot32(activated, down_here, contract_last)
    grad_hidden = gelu_pull(dot32(seq_cotangent, down_here))[0].astype(bf16)
    grad_mixed = dot32(seq_cotangent, out_head, contract_last).astype(bf16)
    row_dot = jnp.sum(grad_mixed.astype(f32) * mixed_full, axis=-1, keepdims=True)
    probs = jnp.where(causal, jnp.exp(scores - log_total), 0.0)
    grad_values = dot32(probs.astype(bf16), grad_mixed, contract_first)
    grad_probs = dot32(grad_mixed, values, contract_last)
    grad_scores = (probs * (grad_probs - row_dot)).astype(bf16)
    grad_queries = dot32(grad_scores, keys) * score_scale
    grad_keys = dot32(grad_scores, queries, contract_first) * score_scale
    grad_projected = jnp.concatenate(
        [rotary(grad_queries, -positions), rotary(grad_keys, -positions), grad_values], axis=1
    ).astype(bf16)
    grad_attn_in = dot32(grad_projected, qkv_here, contract_last) * (1.0 / repeat)
    grad_mlp_in = dot32(grad_hidden, up_here, contract_last)
    in_partial = grad_attn_in * attn_norm_gain + grad_mlp_in * mlp_norm_gain
    sums = jnp.stack(
        [
            jnp.sum(grad_attn_in * normed, axis=0),
            jnp.sum(grad_attn_in, axis=0),
            jnp.sum(grad_mlp_in * normed, axis=0),
            jnp.sum(grad_mlp_in, axis=0),
        ]
    )
    first_copy = jnp.where(rank % repeat == 0, 1.0, 0.0)
    return (
        seq_cotangent, attn_in, mlp_in, activated, grad_hidden, grad_projected, mixed_mine,
        out_partial.astype(bf16), in_partial.astype(bf16), sums,
        jnp.sum(grad_projected.astype(f32), axis=0) * first_copy,
        jnp.sum(grad_hidden.astype(f32), axis=0),
        None,
    )


def fused_block(lay, operands):
    f32 = jnp.float32
    (own, own_cotangent, qkv_weight, qkv_bias, out_weight, up_weight, up_bias, down_weight,
     attn_norm_gain, attn_norm_bias, mlp_norm_gain, mlp_norm_bias) = operands
    rows, width = own.shape
    z, hi, _ = place(lay)
    rank = z * lay.nhi + hi
    ff = up_weight.shape[1] // (lay.nz * lay.nhi)
    total = lay.nhi * lay.nlo * rows
    bias_here = jnp.concatenate(
        [lax.dynamic_slice(qkv_bias, (part * width + rank * HD,), (HD,)) for part in range(3)]
    )
    half_rot = ROT // 2
    inv_freq = 10000.0 ** (-(jnp.arange(half_rot, dtype=f32) * 2.0) / ROT)
    angles = jnp.arange(total, dtype=f32)[:, None] * inv_freq[None, :]
    cosine, sine = jnp.cos(angles), jnp.sin(angles)
    rest = jnp.zeros((total, 128 - ROT), f32)
    found = block_all(
        lay, own, own_cotangent, qkv_weight, up_weight, down_weight, out_weight,
        bias_here[None], lax.dynamic_slice(up_bias, (rank * ff,), (ff,))[None],
        [v[None] for v in (attn_norm_gain, attn_norm_bias, mlp_norm_gain, mlp_norm_bias)],
        jnp.concatenate([cosine, cosine, rest + 1.0], axis=1),
        jnp.concatenate([-sine, sine, rest], axis=1),
    )
    return tuple(found[:8]) + (
        None, jnp.zeros((4, width), f32), found[18][0], found[19][0],
        (*found[10:18], attn_norm_gain[None], mlp_norm_gain[None]),
    )


def local_block(
    lay,
    tokens,
    qkv_weight,
    qkv_bias,
    out_weight,
    out_bias,
    up_weight,
    up_bias,
    down_weight,
    down_bias,
    attn_norm_gain,
    attn_norm_bias,
    mlp_norm_gain,
    mlp_norm_bias,
    cotangent,
):
    f32, bf16 = jnp.float32, jnp.bfloat16
    nz, nlo, nhi = lay.nz, lay.nlo, lay.nhi
    ranks = nz * nhi
    rows = tokens.shape[1]
    width = tokens.shape[2]
    hidden_width = up_weight.shape[1]
    weight_rows = qkv_weight.shape[0]
    half = nlo * rows
    ctx = lax.axis_index("ctx")
    z = lax.axis_index("shard")
    hi, lo = ctx // nlo, ctx % nlo
    rank = z * nhi + hi
    ff = hidden_width // ranks
    repeat = max(1, ranks // H)
    head = rank // repeat
    own = tokens[0]
    own_cotangent = cotangent[0]
    operands = (
        own, own_cotangent, qkv_weight, qkv_bias, out_weight, up_weight, up_bias, down_weight,
        attn_norm_gain, attn_norm_bias, mlp_norm_gain, mlp_norm_bias,
    )
    fits = repeat == 1 and nlo == 4 and nhi * half * width <= 1024 * 2048
    (seq_cotangent, attn_in, mlp_in, activated, grad_hidden, grad_projected, mixed_mine,
     out_partial, in_partial, sums, qkv_bias_part, up_bias_part, terms) = (fused_block if fits else plain_block)(lay, operands)

    qkv_bias_full = jnp.zeros((3, width), f32)
    qkv_bias_full = lax.dynamic_update_slice(
        qkv_bias_full, qkv_bias_part.reshape(3, HD), (0, head * HD)
    ).reshape(-1)
    up_bias_full = lax.dynamic_update_slice(
        jnp.zeros((hidden_width,), f32),
        up_bias_part,
        (rank * ff,),
    )
    small = jnp.concatenate(
        [
            qkv_bias_full,
            up_bias_full,
            jnp.sum(own_cotangent.astype(f32), axis=0),
            sums.reshape(-1),
        ]
    ).reshape(-1, 128)
    summed_out, summed_in, all_down, all_up, all_qkv, all_out, small = scatter_all(
        lay,
        out_partial,
        in_partial,
        seq_cotangent,
        mlp_in,
        attn_in,
        activated,
        grad_hidden,
        grad_projected,
        mixed_mine,
        terms,
        small,
    )
    output = (own.astype(f32) + summed_out + (out_bias + down_bias)).astype(bf16)[None]
    own_normed, own_scale = normalize(own.astype(f32))
    input_grad = own_scale * (
        summed_in
        - jnp.mean(summed_in, axis=-1, keepdims=True)
        - own_normed * jnp.mean(summed_in * own_normed, axis=-1, keepdims=True)
    )
    tokens_grad = (own_cotangent.astype(f32) + input_grad)[None]

    small = small.reshape(-1)
    cuts = [3 * width, hidden_width, width, width, width, width, width]
    small_parts, at = [], 0
    for size in cuts:
        small_parts.append(small[at : at + size])
        at += size

    qkv_weight_grad = all_qkv.astype(f32)
    out_weight_grad = all_out.astype(f32)
    up_weight_grad = all_up.astype(f32)
    down_weight_grad = all_down.astype(f32)
    return (
        output,
        tokens_grad,
        qkv_weight_grad,
        small_parts[0],
        out_weight_grad,
        small_parts[2],
        up_weight_grad,
        small_parts[1],
        down_weight_grad,
        small_parts[2],
        small_parts[3],
        small_parts[4],
        small_parts[5],
        small_parts[6],
    )


def solution(mesh):
    lay = Layout(mesh)

    def local(*args):
        return local_block(lay, *args)

    sharded = P("shard", "ctx", None)
    by_rows = P("shard", None)
    owned = P(("ctx", "shard"), None)
    in_specs = (
        sharded, by_rows, P(), by_rows, P(), by_rows, P(), by_rows, P(),
        P(), P(), P(), P(), sharded,
    )
    out_specs = (
        sharded, sharded, owned, P(), owned, P(), owned, P(), owned,
        P(), P(), P(), P(), P(),
    )
    return jax.shard_map(
        local, mesh=mesh, in_specs=in_specs, out_specs=out_specs, check_vma=False
    )
```

```python
import functools

import jax
import jax.numpy as jnp
import numpy as np
from jax import lax
from jax.experimental import pallas as pl
from jax.experimental.pallas import tpu as pltpu
from jax.sharding import PartitionSpec as P

H = 8
HD = 256
ROT = 64
AXES = ("ctx", "shard")
MESH = pl.DeviceIdType.MESH

norm_epsilon = 1e-05
masked_score = -1e30
contract_last = (((1,), (1,)), ((), ()))
contract_first = (((0,), (0,)), ((), ()))


def dot32(left, right, dims=(((1,), (0,)), ((), ()))):
    return lax.dot_general(left, right, dims, preferred_element_type=jnp.float32)


def normalize(values):
    center = values - jnp.mean(values, axis=-1, keepdims=True)
    spread = jnp.mean(center * center, axis=-1, keepdims=True)
    scale = lax.rsqrt(spread + norm_epsilon)
    return center * scale, scale


def rotary(values, positions):
    half_rot = ROT // 2
    inv_freq = 10000.0 ** (-(jnp.arange(half_rot, dtype=jnp.float32) * 2.0) / ROT)
    angles = positions.astype(jnp.float32)[:, None] * inv_freq[None, :]
    cosine = jnp.cos(angles)
    sine = jnp.sin(angles)
    first_half = values[:, :half_rot]
    second_half = values[:, half_rot:ROT]
    return jnp.concatenate(
        [
            first_half * cosine - second_half * sine,
            second_half * cosine + first_half * sine,
            values[:, ROT:],
        ],
        axis=-1,
    )


def exact_gelu(values):
    return jax.nn.gelu(values, approximate=False)


class Layout:
    def __init__(self, mesh):
        self.nz = mesh.shape["shard"]
        self.nc = mesh.shape["ctx"]
        self.nlo = self.nz
        self.nhi = self.nc // self.nlo
        assert self.nhi == 2 and self.nz * self.nhi == self.nc
        self.bits = [1 << b for b in range(self.nlo.bit_length() - 1)]
        assert 1 << len(self.bits) == self.nlo
        self.seq_of_lo = [
            lo // 2 if lo % 2 == 0 else self.nz - 1 - lo // 2 for lo in range(self.nlo)
        ]
        self.lo_of_seq = [self.seq_of_lo.index(s) for s in range(self.nz)]

    def flat(self, z, hi, lo):
        return (hi * self.nlo + lo) * self.nz + z


def flip(value, mask, count):
    bit = 1
    while bit < count:
        if mask & bit:
            value = value + bit - 2 * bit * ((value // bit) % 2)
        bit *= 2
    return value


def low_bit(mask):
    return mask & -mask


def place(lay):
    ctx = lax.axis_index("ctx")
    z = lax.axis_index("shard")
    return z, ctx // lay.nlo, ctx % lay.nlo


def remote(src, dst, send, recv, device):
    return pltpu.make_async_remote_copy(
        src_ref=src, dst_ref=dst, send_sem=send, recv_sem=recv, device_id=device, device_id_type=MESH
    )


def enter(devices):
    barrier = pltpu.get_barrier_semaphore()
    for device in devices:
        pl.semaphore_signal(barrier, inc=1, device_id=device, device_id_type=MESH)
    pl.semaphore_wait(barrier, len(devices))


def gather_schedule(order_w, nlo, by_bit, n_groups):
    w = [("W", g, i) for g, i in order_w]
    arrive = [("E", g, i, 0) for g, i in order_w]
    last = [("E", g, i, r) for r in by_bit for g, i in order_w]

    def tokens(a):
        events = [("D", a, 0)]
        for k in range(1, nlo):
            events += [("Z", a, k), ("D", a, k)]
        return events

    first, second = tokens(0), tokens(1)
    events = [("N", 0)] + first[:3] + [("N", 1)] + first[3:]
    k = 0
    for item in second:
        events += [item] + arrive[k : k + 2]
        k += 2
    events += arrive[k:] + last
    window, start = 3, 4
    schedule, k = [], window
    for n, item in enumerate(events):
        if n == start:
            schedule += w[:window]
        schedule.append(item)
        if item[0] == "E" and item[3] == 0 and k < len(w):
            schedule.append(w[k])
            k += 1
    return schedule


def gather_kernel(lay, sizes, tok, cot, qkv, up, down, seq_t, seq_c, w_qkv, w_up, w_down, stage_t, stage_c,
                  near_r, near_s, home_c, z_r, z_s, y_r, y_s, wz_r, wz_s, wf_r, wf_s):
    rows, width, weight_rows, ff, repeat = sizes
    nz, nlo, nhi = lay.nz, lay.nlo, lay.nhi
    z, hi, lo = place(lay)
    half, quarter = nlo * rows, weight_rows // nlo
    odd = lo % 2
    s = (1 - odd) * (lo // 2) + odd * (nz - 1 - lo // 2)

    def dev(z, hi, lo):
        return (hi * nlo + lo, z)

    enter(
        [dev((z + i) % nz, hi, lo) for i in range(1, nz)]
        + [dev(z, hi, flip(lo, r, nlo)) for r in range(1, nlo)]
        + [dev(z, 1 - hi, lo)]
    )

    groups = []
    for part in range(3):
        groups.append((qkv, w_qkv, lambda rank, part=part: part * width + (rank // repeat) * HD, part * HD, HD))
    groups.append((up, w_up, lambda rank: rank * ff, 0, ff))
    groups.append((down, w_down, lambda rank: rank * ff, 0, ff))
    bits = list(reversed(lay.bits))

    def weight_z(g, i):
        src, dst, column, at, wide = groups[g]
        to = (z + i) % nz
        first = pl.multiple_of(column(to * nhi + hi), 128)
        return remote(
            src.at[pl.ds(pl.multiple_of(lo * quarter, quarter), quarter), pl.ds(first, wide)],
            dst.at[pl.ds(pl.multiple_of(z * weight_rows + lo * quarter, quarter), quarter), pl.ds(at, wide)],
            wz_s.at[g, i - 1], wz_r.at[g, i - 1], dev(to, hi, lo),
        )

    def weight_forward(g, i, r, b):
        _, dst, _, at, wide = groups[g]
        row = ((z + nz - i) % nz) * weight_rows + flip(lo, r, nlo) * quarter
        piece = dst.at[pl.ds(pl.multiple_of(row, quarter), quarter), pl.ds(at, wide)]
        k = bits.index(b)
        return remote(piece, piece, wf_s.at[g, i - 1, r, k], wf_r.at[g, i - 1, r ^ b], dev(z, hi, flip(lo, b, nlo)))

    inputs, staged, sequences = (tok, cot), (stage_t, stage_c), (seq_t, seq_c)
    distance = jnp.abs(z - s)

    def home_of(seq):
        late = seq // (nz // 2)
        return (1 - late) * (2 * seq) + late * (2 * (nz - 1 - seq) + 1)

    def seq_rows(a, which, r):
        row = which * half + flip(lo, r, nlo) * rows
        return sequences[a].at[pl.ds(pl.multiple_of(row, rows), rows)]

    def along(a, src, seq, way):
        return remote(src, staged[a].at[seq], z_s.at[a, seq, way], z_r.at[a, seq], dev((z + 1 - 2 * way + nz) % nz, hi, lo))

    def near(a, src, seq):
        return remote(src, seq_rows(a, hi, 0), near_s.at[a, seq], near_r.at[a, lo], dev(z, hi, home_of(seq)))

    def near_arrival(a, r):
        piece = seq_rows(a, hi, r)
        return remote(piece, piece, near_s.at[a, 0], near_r.at[a, flip(lo, r, nlo)], dev(z, hi, flip(lo, r, nlo)))

    def stay(a, src):
        return pltpu.make_async_copy(src, seq_rows(a, hi, 0), home_c.at[a])

    def across(a, src, r):
        return remote(src, seq_rows(a, hi, r), y_s.at[a, r], y_r.at[a, r], dev(z, 1 - hi, lo))

    def across_arrival(a, r):
        piece = seq_rows(a, 1 - hi, r)
        return remote(piece, piece, y_s.at[a, r], y_r.at[a, r], dev(z, 1 - hi, lo))

    def sources(a):
        yield (z >= 0, inputs[a], z, z < nz - 1, z > 0)
        for k in range(1, nz):
            yield (z >= k, staged[a].at[(z + nz - k) % nz], (z + nz - k) % nz, z < nz - 1, z < 0)
            yield (z < nz - k, staged[a].at[(z + k) % nz], (z + k) % nz, z < 0, z > 0)

    def dispatch(a, which):
        valid, src, seq, up, down = list(sources(a))[which]

        @pl.when(valid & up)
        def _():
            along(a, src, seq, 0).start()

        @pl.when(valid & down)
        def _():
            along(a, src, seq, 1).start()

        @pl.when(valid & (lo == home_of(seq)))
        def _():
            across(a, src, 0).start()
            stay(a, src).start()

        @pl.when(valid & (lo != home_of(seq)))
        def _():
            near(a, src, seq).start()

    def settle(a, which):
        valid, src, seq, up, down = list(sources(a))[which]

        @pl.when(valid & up)
        def _():
            along(a, src, seq, 0).wait_send()

        @pl.when(valid & down)
        def _():
            along(a, src, seq, 1).wait_send()

        @pl.when(valid & (lo == home_of(seq)))
        def _():
            across(a, src, 0).wait_send()
            stay(a, src).wait()

        @pl.when(valid & (lo != home_of(seq)))
        def _():
            near(a, src, seq).wait_send()

    def chain_event(a, k):
        for which, valid, seq in ((2 * k - 1, z >= k, (z + nz - k) % nz), (2 * k, z < nz - k, (z + k) % nz)):
            @pl.when(valid)
            def _(seq=seq):
                along(a, staged[a].at[seq], seq, 0).wait_recv()

            dispatch(a, which)

    def near_event(a, d):
        @pl.when(distance == d)
        def _():
            for r in range(1, nlo):
                near_arrival(a, r).wait_recv()
                across(a, seq_rows(a, hi, r), r).start()

    def forward_from(g, i, r):
        for b in bits:
            if r == 0 or b < low_bit(r):
                weight_forward(g, i, r, b).start()

    def weight_event(g, i, r):
        if r == 0:
            weight_z(g, i).wait_recv()
        else:
            weight_forward(g, i, r ^ low_bit(r), low_bit(r)).wait_recv()
        forward_from(g, i, r)

    order_w = [(g, i) for g in range(len(groups)) for i in range(1, nz)]
    by_bit = sorted(range(1, nlo), key=lambda r: -low_bit(r))
    act = dict(N=lambda a: dispatch(a, 0), Z=chain_event, D=near_event, W=lambda g, i: weight_z(g, i).start(), E=weight_event)
    for item in gather_schedule(order_w, nlo, by_bit, len(groups)):
        act[item[0]](*item[1:])
    for a in range(2):
        for j in range(nlo):
            across_arrival(a, j).wait_recv()
    for g, i in order_w:
        weight_z(g, i).wait_send()
        for r in range(nlo):
            for b in bits:
                if r == 0 or b < low_bit(r):
                    weight_forward(g, i, r, b).wait_send()
    for a in range(2):
        for which in range(2 * nz - 1):
            settle(a, which)
        for r in range(1, nlo):
            across(a, seq_rows(a, hi, r), r).wait_send()


def gather_all(lay, tok, cot, qkv, up, down):
    rows, width = tok.shape
    nz, nlo = lay.nz, lay.nlo
    ranks = nz * lay.nhi
    ff = up.shape[1] // ranks
    repeat = max(1, ranks // H)
    sizes = (rows, width, qkv.shape[0], ff, repeat)
    bits = len(lay.bits)
    anywhere = pl.BlockSpec(memory_space=pl.ANY)
    dma = pltpu.SemaphoreType.DMA
    bf16 = jnp.bfloat16
    total = 2 * nlo * rows
    return pl.pallas_call(
        functools.partial(gather_kernel, lay, sizes),
        out_shape=[
            jax.ShapeDtypeStruct((total, width), bf16),
            jax.ShapeDtypeStruct((total, width), bf16),
            jax.ShapeDtypeStruct((width, 3 * HD), bf16),
            jax.ShapeDtypeStruct((width, ff), bf16),
            jax.ShapeDtypeStruct((width, ff), bf16),
            jax.ShapeDtypeStruct((nz, rows, width), bf16),
            jax.ShapeDtypeStruct((nz, rows, width), bf16),
        ],
        in_specs=[anywhere] * 5,
        out_specs=[anywhere] * 7,
        scratch_shapes=[
            dma((2, nlo)), dma((2, nz)), dma((2,)), dma((2, nz)), dma((2, nz, 2)), dma((2, nlo)), dma((2, nlo)),
            dma((5, nz - 1)), dma((5, nz - 1)), dma((5, nz - 1, nlo)), dma((5, nz - 1, nlo, bits)),
        ],
        compiler_params=pltpu.CompilerParams(collective_id=1, has_side_effects=True),
        name="gather_all",
    )(tok, cot, qkv, up, down)[:5]

def turn(values, cosine, sine):
    left = values[:, :128]
    lane = lax.broadcasted_iota(jnp.int32, left.shape, 1)
    swapped = jnp.where(lane < ROT // 2, pltpu.roll(left, 128 - ROT // 2, 1), pltpu.roll(left, ROT // 2, 1))
    return jnp.concatenate([left * cosine + swapped * sine, values[:, 128:]], axis=1)


def block_schedule():
    return [
        ("N", 0), ("WO",), ("N", 1), ("D", 0, 0), ("Z", 0, 1), ("D", 0, 1), ("W", 0, 1), ("W", 0, 2), ("Z", 0, 2),
        ("W", 0, 3), ("W", 1, 1), ("W", 1, 2), ("D", 0, 2), ("W", 1, 3), ("W", 2, 1), ("Z", 0, 3), ("W", 2, 2),
        ("D", 1, 0), ("Z", 1, 1), ("E", 0, 1, 0), ("W", 2, 3), ("E", 0, 2, 0), ("W", 3, 1), ("D", 0, 3),
        ("E", 0, 3, 0), ("E", 1, 1, 0), ("D", 1, 1), ("E", 1, 2, 0), ("H", 0), ("Z", 1, 2), ("E", 1, 3, 0),
        ("W", 3, 2), ("E", 2, 1, 0), ("E", 2, 2, 0), ("D", 1, 2), ("E", 0, 1, 2), ("E", 2, 3, 0), ("E", 0, 2, 2),
        ("E", 3, 1, 0), ("W", 3, 3), ("Z", 1, 3), ("E", 0, 3, 2), ("E", 1, 1, 2), ("E", 0, 1, 1), ("E", 0, 1, 3),
        ("E", 1, 2, 2), ("H", 1), ("E", 0, 2, 1), ("E", 0, 2, 3), ("D", 1, 3), ("E", 1, 3, 2), ("E", 3, 2, 0),
        ("W", 4, 1), ("E", 0, 3, 1), ("E", 0, 3, 3), ("E", 2, 1, 2), ("E", 1, 1, 1), ("E", 1, 1, 3), ("E", 2, 2, 2),
        ("E", 1, 2, 1), ("E", 1, 2, 3), ("E", 2, 3, 2), ("E", 1, 3, 1), ("E", 1, 3, 3), ("E", 3, 1, 2),
        ("E", 3, 3, 0), ("W", 4, 2), ("E", 2, 1, 1), ("E", 2, 1, 3), ("E", 2, 2, 1), ("E", 2, 2, 3), ("E", 2, 3, 1),
        ("E", 2, 3, 3), ("K", 0), ("K", 1), ("K", 2), ("K", 3), ("AF", 0), ("AF", 1), ("AF", 2), ("AF", 3),
        ("E", 3, 1, 1), ("E", 3, 1, 3), ("E", 3, 2, 2), ("E", 4, 1, 0), ("W", 4, 3), ("CO",), ("GM", 0), ("GM", 1),
        ("GM", 2), ("GM", 3), ("E", 3, 2, 1), ("E", 3, 2, 3), ("AB", 0), ("AB", 1), ("E", 3, 3, 2), ("E", 4, 2, 0),
        ("AB", 2), ("AB", 3), ("BP",), ("E", 3, 3, 1), ("E", 3, 3, 3), ("U", 0), ("U", 1), ("E", 4, 1, 2), ("U", 2),
        ("U", 3), ("E", 4, 3, 0), ("E", 4, 1, 1), ("E", 4, 1, 3), ("V", 0), ("E", 4, 2, 2), ("VX", 0),
        ("E", 4, 2, 1), ("E", 4, 2, 3), ("E", 4, 3, 2), ("V", 1), ("E", 4, 3, 1), ("VX", 1), ("E", 4, 3, 3),
        ("O", 0), ("O", 1), ("O", 2), ("O", 3), ("VO",), ("GH", 0), ("GH", 1), ("GH", 2), ("GH", 3), ("VY", 0),
        ("VY", 1),
    ]


def block_kernel(lay, sizes, *refs):
    rows, width, weight_rows, ff = sizes
    nz, nlo, nhi = lay.nz, lay.nlo, lay.nhi
    f32, bf16 = jnp.float32, jnp.bfloat16
    refs = list(refs)

    def take(count):
        taken = refs[:count]
        del refs[:count]
        return taken

    tok, cot, qkv, up, down, out_w = take(6)
    qkv_b, up_b, gain_a, shift_a, gain_m, shift_m, cos_t, sin_t = take(8)
    seq_c_out, attn_out, mlp_out, act_out, gh_out, gp_out, mixed_out, o_out, stage_t, stage_c = take(10)
    seq_t_out, w_qkv_out, w_up_out, means_out, scales_out = take(5)
    early_out, part_out = take(2), take(1)[0]
    qkv_b_out, up_b_out, cot_b_out = take(3)
    seq_t, seq_c, w_qkv, w_up, w_down, w_out = take(6)
    attn_in, mlp_in, q_ref, k_ref, v_ref, mixed, mixed_full, lse, slope, act, gh, gm = take(12)
    dq, dk, dv, gp, o_buf, means, scales, out_part, theirs = take(9)
    mine, came, last = take(2), take(2), take(2)
    near_r, near_s, home_c, z_r, z_s, y_r, y_s, wz_r, wz_s, wf_r, wf_s, own_c, out_c, o_c, pair_r, pair_s, last_r, last_s, early_c = take(19)

    z, hi, lo = place(lay)
    half, quarter = nlo * rows, weight_rows // nlo
    total = 2 * half
    rank = z * nhi + hi
    odd = lo % 2
    s = (1 - odd) * (lo // 2) + odd * (nz - 1 - lo // 2)
    score_scale = HD ** (-0.5)

    def dev(z, hi, lo):
        return (hi * nlo + lo, z)

    enter(
        [dev((z + i) % nz, hi, lo) for i in range(1, nz)]
        + [dev(z, hi, flip(lo, r, nlo)) for r in range(1, nlo)]
        + [dev(z, 1 - hi, lo)]
    )

    groups = []
    for part in range(3):
        groups.append((qkv, w_qkv, lambda rank, part=part: part * width + rank * HD, part * HD, HD))
    groups.append((up, w_up, lambda rank: rank * ff, 0, ff))
    groups.append((down, w_down, lambda rank: rank * ff, 0, ff))
    bits = list(reversed(lay.bits))

    def weight_z(g, i):
        src, dst, column, at, wide = groups[g]
        to = (z + i) % nz
        first = pl.multiple_of(column(to * nhi + hi), 128)
        return remote(
            src.at[pl.ds(pl.multiple_of(lo * quarter, quarter), quarter), pl.ds(first, wide)],
            dst.at[pl.ds(pl.multiple_of(z * weight_rows + lo * quarter, quarter), quarter), pl.ds(at, wide)],
            wz_s.at[g, i - 1], wz_r.at[g, i - 1], dev(to, hi, lo),
        )

    def weight_forward(g, i, r, b):
        _, dst, _, at, wide = groups[g]
        row = ((z + nz - i) % nz) * weight_rows + flip(lo, r, nlo) * quarter
        piece = dst.at[pl.ds(pl.multiple_of(row, quarter), quarter), pl.ds(at, wide)]
        k = bits.index(b)
        return remote(piece, piece, wf_s.at[g, i - 1, r, k], wf_r.at[g, i - 1, r ^ b], dev(z, hi, flip(lo, b, nlo)))

    inputs, staged, sequences = (tok, cot), (stage_t, stage_c), (seq_t, seq_c)
    distance = jnp.abs(z - s)

    def home_of(seq):
        late = seq // (nz // 2)
        return (1 - late) * (2 * seq) + late * (2 * (nz - 1 - seq) + 1)

    def seq_rows(a, which, r):
        row = which * half + flip(lo, r, nlo) * rows
        return sequences[a].at[pl.ds(pl.multiple_of(row, rows), rows)]

    def along(a, src, seq, way):
        return remote(src, staged[a].at[seq], z_s.at[a, seq, way], z_r.at[a, seq], dev((z + 1 - 2 * way + nz) % nz, hi, lo))

    def near(a, src, seq):
        return remote(src, seq_rows(a, hi, 0), near_s.at[a, seq], near_r.at[a, lo], dev(z, hi, home_of(seq)))

    def near_arrival(a, r):
        piece = seq_rows(a, hi, r)
        return remote(piece, piece, near_s.at[a, 0], near_r.at[a, flip(lo, r, nlo)], dev(z, hi, flip(lo, r, nlo)))

    def stay(a, src):
        return pltpu.make_async_copy(src, seq_rows(a, hi, 0), home_c.at[a])

    def across(a, src, r):
        return remote(src, seq_rows(a, hi, r), y_s.at[a, r], y_r.at[a, r], dev(z, 1 - hi, lo))

    def across_arrival(a, r):
        piece = seq_rows(a, 1 - hi, r)
        return remote(piece, piece, y_s.at[a, r], y_r.at[a, r], dev(z, 1 - hi, lo))

    def sources(a):
        yield (z >= 0, inputs[a], z, z < nz - 1, z > 0)
        for k in range(1, nz):
            yield (z >= k, staged[a].at[(z + nz - k) % nz], (z + nz - k) % nz, z < nz - 1, z < 0)
            yield (z < nz - k, staged[a].at[(z + k) % nz], (z + k) % nz, z < 0, z > 0)

    def dispatch(a, which):
        valid, src, seq, up, down = list(sources(a))[which]

        @pl.when(valid & up)
        def _():
            along(a, src, seq, 0).start()

        @pl.when(valid & down)
        def _():
            along(a, src, seq, 1).start()

        @pl.when(valid & (lo == home_of(seq)))
        def _():
            across(a, src, 0).start()
            stay(a, src).start()

        @pl.when(valid & (lo != home_of(seq)))
        def _():
            near(a, src, seq).start()

    def settle(a, which):
        valid, src, seq, up, down = list(sources(a))[which]

        @pl.when(valid & up)
        def _():
            along(a, src, seq, 0).wait_send()

        @pl.when(valid & down)
        def _():
            along(a, src, seq, 1).wait_send()

        @pl.when(valid & (lo == home_of(seq)))
        def _():
            across(a, src, 0).wait_send()

        @pl.when(valid & (lo != home_of(seq)))
        def _():
            near(a, src, seq).wait_send()

    def chain_event(a, k):
        for which, valid, seq in ((2 * k - 1, z >= k, (z + nz - k) % nz), (2 * k, z < nz - k, (z + k) % nz)):
            @pl.when(valid)
            def _(seq=seq):
                along(a, staged[a].at[seq], seq, 0).wait_recv()

            dispatch(a, which)

    def near_event(a, d):
        @pl.when(distance == d)
        def _():
            for r in range(1, nlo):
                near_arrival(a, r).wait_recv()
                across(a, seq_rows(a, hi, r), r).start()

    def forward_from(g, i, r):
        for b in bits:
            if r == 0 or b < low_bit(r):
                weight_forward(g, i, r, b).start()

    def weight_event(g, i, r):
        if r == 0:
            weight_z(g, i).wait_recv()
        else:
            weight_forward(g, i, r ^ low_bit(r), low_bit(r)).wait_recv()
        forward_from(g, i, r)

    def own_weight(g):
        if g == len(groups):
            first = pl.multiple_of(rank * HD - z * weight_rows, HD)
            return pltpu.make_async_copy(out_w.at[pl.ds(first, HD)], w_out, own_c.at[g])
        src, dst, column, at, wide = groups[g]
        first = pl.multiple_of(column(rank), 128)
        return pltpu.make_async_copy(
            src.at[:, pl.ds(first, wide)],
            dst.at[pl.ds(pl.multiple_of(z * weight_rows, weight_rows), weight_rows), pl.ds(at, wide)],
            own_c.at[g],
        )

    def own_start():
        for g in range(len(groups) + 1):
            own_weight(g).start()

    tall = 256
    blocks = total // tall
    kept = ((seq_c, seq_c_out), (attn_in, attn_out), (mlp_in, mlp_out), (act, act_out), (gh, gh_out), (gp, gp_out), (mixed, mixed_out),
            (seq_t, seq_t_out), (w_qkv, w_qkv_out), (w_up, w_up_out), (means, means_out), (scales, scales_out))

    def save(k):
        return pltpu.make_async_copy(*kept[k], out_c.at[k])

    def at_block(i):
        return pl.ds(i * tall, tall)

    def norm(which):
        if which == 0:
            stay(0, tok).wait()
        else:
            for r in range(nlo):
                across_arrival(0, r).wait_recv()
        start = (hi if which == 0 else 1 - hi) * half
        step = 64

        def body(i, carry):
            at = pl.ds(pl.multiple_of(start + i * step, step), step)
            values = seq_t[at, :].astype(f32)
            mean = jnp.mean(values, axis=-1, keepdims=True)
            center = values - mean
            scale = lax.rsqrt(jnp.mean(center * center, axis=-1, keepdims=True) + norm_epsilon)
            normed = center * scale
            attn_in[at, :] = (normed * gain_a[...] + shift_a[...]).astype(bf16)
            mlp_in[at, :] = (normed * gain_m[...] + shift_m[...]).astype(bf16)
            means[at, :] = jnp.broadcast_to(mean, (step, 128))
            scales[at, :] = jnp.broadcast_to(scale, (step, 128))
            return carry

        lax.fori_loop(0, half // step, body, 0)
        if which == 1:
            for k in (1, 2, 7, 10, 11):
                save(k).start()

    def project(i):
        if i == 0:
            for g in range(3):
                own_weight(g).wait()
            save(8).start()
        at = at_block(i)
        raw = jnp.dot(attn_in[at, :], w_qkv[...], preferred_element_type=f32)
        raw = raw + jnp.concatenate(
            [qkv_b[:, pl.ds(pl.multiple_of(part * width + rank * HD, HD), HD)] for part in range(3)], axis=1
        )
        q_ref[at, :] = turn(raw[:, :HD], cos_t[at, :], sin_t[at, :]).astype(bf16)
        k_ref[at, :] = turn(raw[:, HD : 2 * HD], cos_t[at, :], sin_t[at, :]).astype(bf16)
        v_ref[at, :] = raw[:, 2 * HD :].astype(bf16)

    def scores_of(i):
        reach = (i + 1) * tall
        scores = dot32(q_ref[at_block(i), :], k_ref[:reach, :], contract_last) * score_scale
        row = lax.broadcasted_iota(jnp.int32, scores.shape, 0) + i * tall
        column = lax.broadcasted_iota(jnp.int32, scores.shape, 1)
        return jnp.where(row >= column, scores, masked_score), reach

    def attend(i):
        scores, reach = scores_of(i)
        top = jnp.max(scores, axis=-1, keepdims=True)
        weights = jnp.exp(scores - top)
        summed = jnp.sum(weights, axis=-1, keepdims=True)
        full = dot32(weights.astype(bf16), v_ref[:reach, :]) / summed
        at = at_block(i)
        mixed_full[at, :] = full
        mixed[at, :] = full.astype(bf16)
        lse[at, :] = jnp.broadcast_to(top + jnp.log(summed), (tall, 128))
        if i == blocks - 1:
            save(6).start()

    def hidden(i):
        if i == 0:
            own_weight(3).wait()
            save(9).start()
        at = at_block(i)
        value = jnp.dot(mlp_in[at, :], w_up[...], preferred_element_type=f32)
        value = value + up_b[:, pl.ds(pl.multiple_of(rank * ff, ff), ff)]
        cdf = (1.0 + lax.erf(value * (0.5 ** 0.5))) * 0.5
        act[at, :] = (value * cdf).astype(bf16)
        slope[at, :] = cdf + value * jnp.exp(value * value * (-0.5)) * 0.3989422804014327
        if i == blocks - 1:
            save(3).start()

    def cotangent_here():
        stay(1, cot).wait()
        for r in range(nlo):
            across_arrival(1, r).wait_recv()
        save(0).start()
        own_weight(5).wait()
        row = pl.multiple_of(rank * rows, rows)
        cot_b_out[...] = jnp.sum(seq_c[pl.ds(row, rows), :].astype(f32), axis=0, keepdims=True)

    def back_mixed(i):
        at = at_block(i)
        gm[at, :] = dot32(seq_c[at, :], w_out[...], contract_last).astype(bf16)

    def back_hidden(i):
        if i == 0:
            up_b_out[...] = jnp.zeros_like(up_b_out)
        at = at_block(i)
        part = (jnp.dot(seq_c[at, :], w_down[...], preferred_element_type=f32) * slope[at, :]).astype(bf16)
        gh[at, :] = part
        up_b_out[...] += jnp.sum(part.astype(f32), axis=0, keepdims=True)
        if i == blocks - 1:
            save(4).start()

    def out_store(i):
        return pltpu.make_async_copy(o_buf.at[at_block(i)], o_out.at[at_block(i)], o_c.at[i])

    def out_block(i):
        if i == 0:
            own_weight(4).wait()
        at = at_block(i)
        part = jnp.dot(mixed[at, :], w_out[...], preferred_element_type=f32)
        part = part + dot32(act[at, :], w_down[...], contract_last)
        o_buf[at, :] = part.astype(bf16)
        out_store(i).start()

    def back_attend(i):
        if i == 0:
            dk[...] = jnp.zeros_like(dk)
            dv[...] = jnp.zeros_like(dv)
        at = at_block(i)
        scores, reach = scores_of(i)
        probs = jnp.exp(scores - lse[at, :1])
        grad = gm[at, :]
        row_dot = jnp.sum(grad.astype(f32) * mixed_full[at, :], axis=-1, keepdims=True)
        dv[:reach, :] += dot32(probs.astype(bf16), grad, contract_first)
        grad_scores = (probs * (dot32(grad, v_ref[:reach, :], contract_last) - row_dot)).astype(bf16)
        dq[at, :] = dot32(grad_scores, k_ref[:reach, :]) * score_scale
        dk[:reach, :] += dot32(grad_scores, q_ref[at, :], contract_first) * score_scale

    def back_project():
        qkv_b_out[...] = jnp.zeros_like(qkv_b_out)
        for i in range(blocks):
            at = at_block(i)
            part = jnp.concatenate(
                [turn(dq[at, :], cos_t[at, :], -sin_t[at, :]), turn(dk[at, :], cos_t[at, :], -sin_t[at, :]), dv[at, :]],
                axis=1,
            ).astype(bf16)
            gp[at, :] = part
            qkv_b_out[...] += jnp.sum(part.astype(f32), axis=0, keepdims=True)
        save(5).start()

    grain = width // (nz * nhi * nlo)
    span = nz * grain
    part_ff = ff // 2

    def product(c, h, rel):
        row = (h * nlo + differ(lo, rel, nlo)) * span
        rows_at = pl.ds(pl.multiple_of(row, span), span)
        return dot32(seq_c[:, rows_at], act[:, c * part_ff : (c + 1) * part_ff], contract_first).astype(bf16)

    def pair_send(c, h, k):
        return remote(
            theirs.at[h, k], came[c].at[h, k], pair_s.at[c, h, k], pair_r.at[c, h, k], dev(z, hi, flip(lo, 1, nlo))
        )

    def last_send(c, h):
        return remote(
            mine[c].at[h, 1], last[c].at[h], last_s.at[c, h], last_r.at[c, h], dev(z, hi, flip(lo, 2, nlo))
        )

    def pair_start(c):
        if c == 1:
            for h in range(nhi):
                for k in range(2):
                    pair_send(0, h, k).wait_send()

        def send(i, carry):
            h, k = i // 2, i % 2
            theirs[h, k] = product(c, h, 2 * k + 1)
            pair_send(c, h, k).start()
            return carry

        def keep_own(i, carry):
            h, k = i // 2, i % 2
            mine[c][h, k] = product(c, h, 2 * k)
            return carry

        lax.fori_loop(0, nhi * 2, send, 0)
        lax.fori_loop(0, nhi * 2, keep_own, 0)

    def pair_event(c):
        for k in (1, 0):
            for h in range(nhi):
                pair_send(c, h, k).wait_recv()
                add_rows(mine[c].at[h, k], mine[c].at[h, k], came[c].at[h, k], 64)
                if k == 1:
                    last_send(c, h).start()

    def early_store(c):
        return pltpu.make_async_copy(mine[c].at[:, 0], early_out[c], early_c.at[c])

    def last_event(c):
        for h in range(nhi):
            last_send(c, h).wait_recv()
            add_rows(mine[c].at[h, 0], mine[c].at[h, 0], last[c].at[h], 64)
        early_store(c).start()

    def part_store():
        return pltpu.make_async_copy(out_part, part_out, early_c.at[2])

    def out_product():
        step = min(512, width)
        for first in range(0, width, step):
            out_part[:, first : first + step] = dot32(
                mixed[...], seq_c[:, first : first + step], contract_first
            ).astype(bf16)
        part_store().start()

    act_of = dict(
        N=lambda a: dispatch(a, 0), Z=chain_event, D=near_event, W=lambda g, i: weight_z(g, i).start(), E=weight_event,
        WO=own_start, H=norm, K=project, AF=attend, U=hidden, CO=cotangent_here, GM=back_mixed, GH=back_hidden,
        O=out_block, AB=back_attend, BP=back_project,
        V=pair_start, VX=pair_event, VY=last_event, VO=out_product,
    )
    order_w = [(g, i) for g in range(len(groups)) for i in range(1, nz)]
    for item in block_schedule():
        act_of[item[0]](*item[1:])

    for k in range(len(kept)):
        save(k).wait()
    for i in range(blocks):
        out_store(i).wait()
    for c in range(2):
        early_store(c).wait()
        for h in range(nhi):
            last_send(c, h).wait_send()
            for k in range(2 if c == 1 else 0):
                pair_send(c, h, k).wait_send()
    part_store().wait()
    for g, i in order_w:
        weight_z(g, i).wait_send()
        for r in range(nlo):
            for b in bits:
                if r == 0 or b < low_bit(r):
                    weight_forward(g, i, r, b).wait_send()
    for a in range(2):
        for which in range(2 * nz - 1):
            settle(a, which)
        for r in range(1, nlo):
            across(a, seq_rows(a, hi, r), r).wait_send()


def block_all(lay, tok, cot, qkv, up, down, out_w, qkv_b, up_b, gains, cos_t, sin_t):
    rows, width = tok.shape
    nz, nlo = lay.nz, lay.nlo
    ff = up_b.shape[1] // (nz * lay.nhi)
    bits = len(lay.bits)
    anywhere = pl.BlockSpec(memory_space=pl.ANY)
    inside = pl.BlockSpec(memory_space=pltpu.VMEM)
    dma = pltpu.SemaphoreType.DMA
    bf16, f32 = jnp.bfloat16, jnp.float32
    total = 2 * nlo * rows

    def shape(*dims, kind=bf16):
        return jax.ShapeDtypeStruct(dims, kind)

    def vmem(*dims, kind=bf16):
        return pltpu.VMEM(dims, kind)

    span = width // (lay.nhi * nlo)
    return pl.pallas_call(
        functools.partial(block_kernel, lay, (rows, width, qkv.shape[0], ff)),
        out_shape=[
            shape(total, width), shape(total, width), shape(total, width), shape(total, ff), shape(total, ff),
            shape(total, 3 * HD), shape(total, HD), shape(total, width),
            shape(nz, rows, width), shape(nz, rows, width),
            shape(total, width), shape(width, 3 * HD), shape(width, ff), shape(total, 128, kind=f32), shape(total, 128, kind=f32),
            shape(lay.nhi, span, ff // 2), shape(lay.nhi, span, ff // 2), shape(HD, width),
            shape(1, 3 * HD, kind=f32), shape(1, ff, kind=f32), shape(1, width, kind=f32),
        ],
        in_specs=[anywhere] * 6 + [inside] * 8,
        out_specs=[anywhere] * 18 + [inside] * 3,
        scratch_shapes=[
            vmem(total, width), vmem(total, width), vmem(width, 3 * HD), vmem(width, ff), vmem(width, ff), vmem(HD, width),
            vmem(total, width), vmem(total, width), vmem(total, HD), vmem(total, HD), vmem(total, HD), vmem(total, HD),
            vmem(total, HD, kind=f32), vmem(total, 128, kind=f32), vmem(total, ff, kind=f32), vmem(total, ff),
            vmem(total, ff), vmem(total, HD),
            vmem(total, HD, kind=f32), vmem(total, HD, kind=f32), vmem(total, HD, kind=f32), vmem(total, 3 * HD),
            vmem(total, width), vmem(total, 128, kind=f32), vmem(total, 128, kind=f32),
            vmem(HD, width), *[vmem(lay.nhi, 2, span, ff // 2)] * 5, *[vmem(lay.nhi, span, ff // 2)] * 2,
            dma((2, nlo)), dma((2, nz)), dma((2,)), dma((2, nz)), dma((2, nz, 2)), dma((2, nlo)), dma((2, nlo)),
            dma((5, nz - 1)), dma((5, nz - 1)), dma((5, nz - 1, nlo)), dma((5, nz - 1, nlo, bits)), dma((6,)),
            dma((12,)), dma((total // 256,)),
            dma((2, lay.nhi, 2)), dma((2, lay.nhi, 2)), dma((2, lay.nhi)), dma((2, lay.nhi)), dma((3,)),
        ],
        compiler_params=pltpu.CompilerParams(
            collective_id=3, has_side_effects=True, vmem_limit_bytes=63 * 1024 * 1024
        ),
        name="block_all",
    )(tok, cot, qkv, up, down, out_w, qkv_b, up_b, *gains, cos_t, sin_t)


def add_rows(into, left, right, step):
    rows = into.shape[0]
    step = min(step, rows)

    def body(k, carry):
        at = pl.ds(pl.multiple_of(k * step, step), step)
        into[at, :] = (left[at, :].astype(jnp.float32) + right[at, :].astype(jnp.float32)).astype(into.dtype)
        return carry

    lax.fori_loop(0, rows // step, body, 0)


def differ(one, other, count):
    result, bit = 0, 1
    while bit < count:
        result = result + bit * ((one // bit + other // bit) % 2)
        bit *= 2
    return result


def scatter_chunks(width, ff, repeat):
    cut = max(ff // 2, 256)
    chunks = []
    for source in (0, 1):
        for first in range(0, ff, cut):
            chunks.append((source, first, cut, lambda rank, first=first: rank * ff + first, True))
    for part in range(3):
        chunks.append((2, part * HD, HD, lambda rank, part=part: part * width + (rank // repeat) * HD, repeat == 1))
    return chunks


def scatter_schedule(nz, nlo, n_chunks, stages, n_slabs):
    if n_slabs:
        return [
            ("L",), ("Y", 0), ("Y", 1), ("C", 0), ("C", 1), ("P",), ("C", 2), ("X", 0, 0), ("X", 0, 1), ("C", 3),
            ("X", 2, 0), ("S", 0), ("X", 3, 0), ("S", 1), ("A", 0, 0), ("S", 2), ("A", 0, 1), ("S", 3), ("X", 1, 0),
            ("X", 1, 1), ("A", 0, 2), ("X", 2, 1), ("S", 4), ("S", 5), ("S", 6), ("A", 0, 3), ("S", 7), ("M",), ("C", 4),
            ("N", 0), ("A", 1, 0), ("X", 3, 1), ("C", 5), ("N", 1), ("X", 4, 0), ("N", 2), ("Y", 2), ("Y", 3), ("C", 6),
            ("A", 1, 1), ("A", 1, 2), ("B", 0, 0), ("A", 1, 3), ("N", 3), ("Q", 0), ("X", 5, 0), ("B", 0, 1),
            ("B", 1, 0), ("N", 4), ("A", 2, 0), ("X", 4, 1), ("X", 6, 0), ("A", 2, 1), ("B", 0, 2), ("B", 1, 1),
            ("X", 5, 1), ("A", 2, 2), ("X", 6, 1), ("B", 1, 2), ("A", 2, 3), ("Q", 1), ("A", 3, 0), ("B", 2, 0),
            ("A", 3, 1), ("B", 2, 1), ("A", 3, 2), ("B", 2, 2), ("A", 3, 3), ("B", 3, 0), ("F", 0), ("F", 1), ("F", 2),
            ("B", 3, 1), ("B", 3, 2), ("F", 3), ("G", 0), ("G", 1), ("G", 2), ("G", 3), ("G", 4), ("G", 5), ("G", 6),
        ]
    timed = [(51 if n_slabs else -4, ("M",)), (4, ("P",)), (-3, ("L",)), (-2, ("Y", 0)), (-2, ("Y", 1)), (52, ("Y", 2)), (52, ("Y", 3))]
    for k in range(n_slabs):
        timed.append((30 + 2 * k, ("S", k)))
    for g in range(n_chunks):
        timed.append((0 + 4 * g, ("C", g)))
        for t in range(stages):
            timed.append((10 + 14 * g + 25 * t, ("X", g, t)))
    for b, (first, step, chain, hop) in enumerate(((14, 11.4, 66, 11), (14, 11.4, 66, 11), (66, 11.4, 112, 11), (66, 11.4, 112, 11))):
        for q in range(nlo):
            timed.append((first + step * q, ("A", b, q)))
        for m in range(nz - 1):
            timed.append((chain + hop * m, ("B", b, m)))
        timed.append((chain + hop * (nz - 1), ("F", b)))
    for t in range(stages):
        timed.append((100 + 10 * t, ("Q", t)))
    for t in range(2 * stages + 1):
        timed.append((56 + 6 * t, ("N", t)))
    timed.sort(key=lambda entry: entry[0])
    return [entry[1] for entry in timed] + [("G", g) for g in range(n_chunks)]


def scatter_kernel(lay, sizes, *refs):
    rows, width, ff, repeat, inside = sizes
    nz, nlo, nhi = lay.nz, lay.nlo, lay.nhi
    stages = len(lay.bits)
    chunks = scatter_chunks(width, ff, repeat)
    n = len(chunks)
    refs = list(refs)

    def take(count):
        taken = refs[:count]
        del refs[:count]
        return taken

    partial_o, = take(1)
    if inside:
        x_up, x_qkv, g_up, g_qkv = take(4)
        x_down = g_down = g_out = None
        seq_t, w_qkv, w_up, means_in, scales_in = take(5)
        ready, part_in = take(2), take(1)[0]
        gain_a, gain_m, qkv_sums, up_sums, cot_sums = take(5)
    else:
        x_down, x_up, x_qkv, g_down, g_up, g_qkv, g_out, small = take(8)
        partial_s, = take(1)
        ready = []
    sum_o, sum_s, all_down, all_up, all_qkv, all_out, small_sum = take(7)
    own, across_buf, near_buf, chain_buf = take(4)
    acc = [None] * len(ready) + take(n - len(ready))
    got = [None] * len(ready) + [take(stages) for _ in range(n - len(ready))]
    out_acc, = take(1)
    out_got = take(stages)
    small_buf, small_got = take(2)
    left, = take(1)
    right_down = right_out = None
    if inside:
        right_up, right_qkv = take(2)
    else:
        right_down, right_up, right_qkv, right_out = take(4)
    staged, out_part = take(2)
    if inside:
        s_buf, ring_t, ring_q, ring_u, means, scales, small_first = take(7)
        partial_s = s_buf
    else:
        small_first = small
    (own_c, y_r, y_s, near_r, near_s, z_r, z_s, st_r, st_s, g_r, g_s, keep_c,
     out_r, out_s, move_r, move_s, sm_r, sm_s, left_c, right_c) = take(20)
    if inside:
        slab_c, stat_c = take(2)

    z, hi, lo = place(lay)
    rank = z * nhi + hi
    ranks = nz * nhi
    half = nlo * rows
    grain = width // (nz * nhi * nlo)
    span = nz * grain

    def dev(z, hi, lo):
        return (hi * nlo + lo, z)

    ctx = hi * nlo + lo
    moves = (ctx != rank) | (z != lo)
    barrier = pltpu.get_barrier_semaphore()
    mates = [
        dev((z + dz) % nz, flip(hi, dh, nhi), lo) for dz in range(nz) for dh in range(nhi) if dz or dh
    ] + [dev(z, hi, flip(lo, r, nlo)) for r in range(1, nlo)]
    for device in mates:
        pl.semaphore_signal(barrier, inc=1, device_id=device, device_id_type=MESH)

    @pl.when(moves)
    def _():
        pl.semaphore_signal(barrier, inc=1, device_id=(rank, lo), device_id_type=MESH)
        pl.semaphore_signal(barrier, inc=1, device_id=dev(ctx // nhi, ctx % nhi, z), device_id_type=MESH)
        pl.semaphore_wait(barrier, len(mates) + 2)

    @pl.when(jnp.logical_not(moves))
    def _():
        pl.semaphore_wait(barrier, len(mates))

    partial, summed = (partial_o, partial_s), (sum_o, sum_s)

    lanes = width // 2

    def part(b):
        return b // 2, pl.ds((b % 2) * lanes, lanes)

    def load_own(b, q):
        a, at = part(b)
        row = pl.multiple_of(hi * half + q * rows, rows)
        return pltpu.make_async_copy(partial[a].at[pl.ds(row, rows), at], own.at[a, q % 2, :, at], own_c.at[b, q % 2])

    def own_rows(b, q):
        a, at = part(b)
        if a == 1 and inside:
            return s_buf.at[pl.ds(pl.multiple_of(hi * half + q * rows, rows), rows), at]
        return own.at[a, q % 2, :, at]

    def across(b, q):
        a, at = part(b)
        row = pl.multiple_of((1 - hi) * half + q * rows, rows)
        return remote(
            partial[a].at[pl.ds(row, rows), at], across_buf.at[a, q, :, at], y_s.at[b, q], y_r.at[b, q], dev(z, 1 - hi, lo)
        )

    def near(b, q):
        a, at = part(b)
        return remote(
            across_buf.at[a, q, :, at], near_buf.at[a, lo, :, at], near_s.at[b, q], near_r.at[b, lo], dev(z, hi, q)
        )

    def near_arrival(b, q):
        a, at = part(b)
        piece = near_buf.at[a, q, :, at]
        return remote(piece, piece, near_s.at[b, q], near_r.at[b, q], dev(z, hi, q))

    def along(b, seq, way):
        a, at = part(b)
        slot = seq if way == 0 else jnp.where(z == seq + 1, nz, seq)
        return remote(
            near_buf.at[a, lay.lo_of_seq[seq], :, at], chain_buf.at[a, slot, :, at], z_s.at[b, seq], z_r.at[b, seq, way],
            dev((z + 1 - 2 * way + nz) % nz, hi, lo),
        )

    def start_across(b):
        a, _ = part(b)
        for q in range(0 if a == 1 and inside else 2):
            load_own(b, q).start()
        for q in range(nlo):
            across(b, q).start()

    def across_event(b, q):
        a, at = part(b)
        if not (a == 1 and inside):
            load_own(b, q).wait()
        across(b, q).wait_recv()
        mine, arrived = own_rows(b, q), across_buf.at[a, q, :, at]

        @pl.when(lo == q)
        def _():
            add_rows(near_buf.at[a, q, :, at], mine, arrived, 32)

        @pl.when(lo != q)
        def _():
            add_rows(arrived, mine, arrived, 32)
            near(b, q).start()

        if q + 2 < nlo and not (a == 1 and inside):
            load_own(b, q + 2).start()

    def chain_event(b, seq, way):
        a, at = part(b)
        q = lay.lo_of_seq[seq]
        active = (z < seq) if way == 0 else (z > seq)
        first = (z == 0) if way == 0 else (z == nz - 1)

        @pl.when(active)
        def _():
            @pl.when(lo != q)
            def _():
                near_arrival(b, q).wait_recv()

            @pl.when(jnp.logical_not(first))
            def _():
                along(b, seq, way).wait_recv()
                mine = near_buf.at[a, q, :, at]
                add_rows(mine, mine, chain_buf.at[a, seq, :, at], 32)

            along(b, seq, way).start()

    def chain_pair(b, m):
        @pl.when(z < nz // 2)
        def _():
            chain_event(b, nz - 1 - m, 0)
            chain_event(b, m, 1)

        @pl.when(z >= nz // 2)
        def _():
            chain_event(b, m, 1)
            chain_event(b, nz - 1 - m, 0)

    def final_event(b):
        a, at = part(b)
        late = z // (nz // 2)
        home = (1 - late) * (2 * z) + late * (2 * (nz - 1 - z) + 1)
        piece = near_buf.at[a, home, :, at]

        @pl.when(lo != home)
        def _():
            remote(piece, piece, near_s.at[b, 0], near_r.at[b, home], dev(z, hi, home)).wait_recv()

        @pl.when(z > 0)
        def _():
            arrived = chain_buf.at[a, z, :, at]
            remote(arrived, arrived, z_s.at[b, 0], z_r.at[b, z, 0], dev(z, hi, lo)).wait_recv()

        @pl.when(z < nz - 1)
        def _():
            arrived = chain_buf.at[a, nz, :, at]
            remote(arrived, arrived, z_s.at[b, 0], z_r.at[b, z, 1], dev(z, hi, lo)).wait_recv()

        def body(k, carry):
            line = pl.ds(pl.multiple_of(k * 16, 16), 16)
            total = piece[line, :].astype(jnp.float32)
            total = total + jnp.where(z > 0, chain_buf[a, z, line, at].astype(jnp.float32), 0.0)
            total = total + jnp.where(z < nz - 1, chain_buf[a, nz, line, at].astype(jnp.float32), 0.0)
            summed[a][line, at] = total
            return carry

        lax.fori_loop(0, rows // 16, body, 0)

    targets = (all_down, all_up, all_qkv)
    lefts = (x_down, x_up, x_qkv)
    n_slots = left.shape[0]
    slots = [0, 0, 1] if inside else [source % n_slots for source in range(3)]
    rights = ((g_down, right_down), (g_up, right_up), (g_qkv, right_qkv), (g_out, right_out))

    def load_left(source):
        return pltpu.make_async_copy(lefts[source], left.at[slots[source]], left_c.at[source])

    def load_right(source):
        return pltpu.make_async_copy(*rights[source], right_c.at[source])

    def start_loads():
        if inside:
            for copy in stat_loads() + slab_loads(0):
                copy.start()
            part_load().start()
            for source in (1, 2):
                load_left(source).start()
                load_right(source).start()
            return
        for source in (0, 3, 1, 2):
            if source < n_slots:
                load_left(source).start()
            load_right(source).start()

    def part_load():
        return pltpu.make_async_copy(part_in, out_part, right_c.at[3])

    right_waited = set()

    def right_here(source):
        if source not in right_waited:
            right_waited.add(source)
            load_right(source).wait()

    def loaded(source):
        load_left(source).wait()
        right_here(source)

    def product(g, h, rel):
        source, first, wide, _, _ = chunks[g]
        row = (h * nlo + differ(lo, rel, nlo)) * span
        rows_at = pl.ds(pl.multiple_of(row, span), span)
        part = lax.dot_general(
            left[slots[source], :, rows_at], rights[source][1][:, first : first + wide],
            contract_first, preferred_element_type=jnp.float32,
        )
        return part.astype(jnp.bfloat16)

    def stage_pieces(t):
        return [rel for rel in range(nlo) if rel % (2 << t) == (1 << t)]

    def stage_send(g, t, h, rel):
        if t == 0:
            src = staged.at[g % 3, h, rel // 2, :, pl.ds(0, chunks[g][2])]
        else:
            src = acc[g].at[h, rel // 2]
        k = rel >> (t + 1)
        return remote(
            src, got[g][t].at[h, k], st_s.at[g, t, h, k], st_r.at[g, t, h, k], dev(z, hi, flip(lo, 1 << t, nlo))
        )

    pairs = nhi * (nlo // 2)

    def start_chunk(g):
        source, first, wide, _, _ = chunks[g]
        if g < len(ready):
            return
        if first == 0:
            loaded(source)
        if g >= 3 + len(ready):
            for h in range(nhi):
                for rel in stage_pieces(0):
                    stage_send(g - 3, 0, h, rel).wait_send()

        def send(i, carry):
            h, k = i // (nlo // 2), i % (nlo // 2)
            staged[g % 3, h, k, :, :wide] = product(g, h, 2 * k + 1)
            stage_send(g, 0, h, 2 * k + 1).start()
            return carry

        def keep_own(i, carry):
            h, k = i // (nlo // 2), i % (nlo // 2)
            acc[g][h, k] = product(g, h, 2 * k)
            return carry

        lax.fori_loop(0, pairs, send, 0)
        lax.fori_loop(0, pairs, keep_own, 0)
        if inside:
            return
        if g == 0:
            out_start()
        if (g + 1 == n or chunks[g + 1][0] != source) and source + n_slots < 3:
            load_left(source + n_slots).start()

    def stage_event(g, t):
        if g < len(ready):
            if t == 0:
                deliver(g)
            return
        order = list(reversed(range(0, nlo, 2 << t)))
        for h in range(nhi):
            for rel in order:
                k = rel >> (t + 1)
                stage_send(g, t, h, rel | (1 << t)).wait_recv()
                add_rows(acc[g].at[h, rel // 2], acc[g].at[h, rel // 2], got[g][t].at[h, k], 64)
                if t + 1 < stages and rel % (4 << t) == (2 << t):
                    stage_send(g, t + 1, h, rel).start()
        if t + 1 == stages:
            deliver(g)

    def owner_send(g, dz, dh):
        source, _, wide, column, _ = chunks[g]
        to_z, to_hi = (z + dz) % nz, flip(hi, dh, nhi)
        first = pl.multiple_of(column(rank), 128)
        k = dz * nhi + dh
        from_rows = pl.ds(pl.multiple_of(to_z * grain, grain), grain)
        return remote(
            ready[g].at[to_hi, from_rows] if g < len(ready) else acc[g].at[to_hi, 0, from_rows],
            targets[source].at[:, pl.ds(first, wide)],
            g_s.at[g, k], g_r.at[g, k], dev(to_z, to_hi, lo),
        )

    def owner_arrival(g, dz, dh):
        source, _, wide, column, _ = chunks[g]
        from_z, from_hi = (z + nz - dz) % nz, flip(hi, dh, nhi)
        first = pl.multiple_of(column(from_z * nhi + from_hi), 128)
        piece = targets[source].at[:, pl.ds(first, wide)]
        k = dz * nhi + dh
        return remote(piece, piece, g_s.at[g, k], g_r.at[g, k], dev(from_z, from_hi, lo))

    def keep(g):
        source, _, wide, column, _ = chunks[g]
        first = pl.multiple_of(column(rank), 128)
        from_rows = pl.ds(pl.multiple_of(z * grain, grain), grain)
        return pltpu.make_async_copy(
            ready[g].at[hi, from_rows] if g < len(ready) else acc[g].at[hi, 0, from_rows],
            targets[source].at[:, pl.ds(first, wide)], keep_c.at[g],
        )

    others = [(dz, dh) for dz in range(nz) for dh in range(nhi) if dz or dh]

    def when_sent(g, from_hi, act):
        if chunks[g][4]:
            act()
        else:
            pl.when(from_hi % repeat == 0)(act)

    def deliver(g):
        def act():
            for dz, dh in others:
                owner_send(g, dz, dh).start()
            keep(g).start()

        when_sent(g, hi, act)

    def finish_chunk(g):
        def sent():
            for dz, dh in others:
                owner_send(g, dz, dh).wait_send()
            keep(g).wait()

        when_sent(g, hi, sent)
        for dz, dh in others:
            when_sent(g, flip(hi, dh, nhi), lambda dz=dz, dh=dh: owner_arrival(g, dz, dh).wait_recv())

    def out_rows(rel):
        return out_part.at[pl.ds(pl.multiple_of(flip(lo, rel, nlo) * grain, grain), grain)]

    def out_send(t, rel):
        src = out_rows(rel) if t == 0 else out_acc.at[rel // 2]
        k = rel >> (t + 1)
        return remote(src, out_got[t].at[k], out_s.at[t, k], out_r.at[t, k], dev(z, hi, flip(lo, 1 << t, nlo)))

    def out_start():
        if inside:
            part_load().wait()
            for rel in stage_pieces(0):
                out_send(0, rel).start()
            return
        load_right(3).wait()
        wide = min(512, width)

        def body(i, carry):
            at = pl.ds(pl.multiple_of(i * wide, wide), wide)
            part = lax.dot_general(
                right_out[...], left[0, :, at], contract_first, preferred_element_type=jnp.float32
            )
            out_part[:, at] = part.astype(jnp.bfloat16)
            return carry

        lax.fori_loop(0, width // wide, body, 0)
        for rel in stage_pieces(0):
            out_send(0, rel).start()

    def out_event(t):
        for rel in reversed(range(0, nlo, 2 << t)):
            out_send(t, rel | (1 << t)).wait_recv()
            mine = out_rows(rel) if t == 0 else out_acc.at[rel // 2]
            add_rows(out_acc.at[rel // 2], mine, out_got[t].at[rel >> (t + 1)], 16)
            if t + 1 < stages and rel % (4 << t) == (2 << t):
                out_send(t + 1, rel).start()
        if t + 1 == stages:
            @pl.when(moves)
            def _():
                out_move().start()

            @pl.when(jnp.logical_not(moves))
            def _():
                out_stay().start()

    def out_move():
        return remote(out_acc.at[0], all_out, move_s, move_r, (rank, lo))

    def out_stay():
        return pltpu.make_async_copy(out_acc.at[0], all_out, move_s)

    doubling = (
        [dev(flip(z, b, nz), hi, lo) for b in lay.bits]
        + [dev(z, hi, flip(lo, lay.bits[0], nlo))]
        + [dev(z, flip(hi, 1, nhi), lo)]
        + [dev(z, hi, flip(lo, b, nlo)) for b in lay.bits[1:]]
    )

    def small_send(t):
        src = small_first if t == 0 else small_buf.at[t - 1]
        return remote(src, small_got.at[t], sm_s.at[t], sm_r.at[t], doubling[t])

    def small_event(t):
        small_send(t).wait_recv()
        mine = small_first if t == 0 else small_buf.at[t - 1]
        into = small_sum if t + 1 == len(doubling) else small_buf.at[t]
        into[...] = mine[...] + small_got[t]
        if t + 1 < len(doubling):
            small_send(t + 1).start()

    slab = 256
    wide = slab // 128

    def slab_loads(k):
        at = pl.ds(k * slab, slab)
        return [
            pltpu.make_async_copy(seq_t.at[:, at], ring_t.at[k % 2], slab_c.at[k % 2, 0]),
            pltpu.make_async_copy(w_qkv.at[at], ring_q.at[k % 2], slab_c.at[k % 2, 1]),
            pltpu.make_async_copy(w_up.at[at], ring_u.at[k % 2], slab_c.at[k % 2, 2]),
        ]

    def stat_loads():
        return [
            pltpu.make_async_copy(means_in, means, stat_c.at[0]),
            pltpu.make_async_copy(scales_in, scales, stat_c.at[1]),
        ]

    def in_slab(k):
        if k == 0:
            small_first[...] = jnp.zeros_like(small_first)
            for place_at, values in (
                (rank * (HD // 128), qkv_sums[:, :HD]),
                (width // 128 + rank * (HD // 128), qkv_sums[:, HD : 2 * HD]),
                (2 * width // 128 + rank * (HD // 128), qkv_sums[:, 2 * HD :]),
                (3 * width // 128 + rank * (ff // 128), up_sums[...]),
                ((3 * width + ranks * ff) // 128, cot_sums[...]),
            ):
                for j in range(values.shape[1] // 128):
                    small_first[pl.ds(place_at + j, 1), :] = values[:, j * 128 : (j + 1) * 128]
            for copy in stat_loads():
                copy.wait()
            right_here(1)
            right_here(2)
        for copy in slab_loads(k):
            copy.wait()
        if (k + 1) * slab < width:
            for copy in slab_loads(k + 1):
                copy.start()
        features = pl.ds(k * slab, slab)

        def body(i, sums):
            at = pl.ds(pl.multiple_of(i * 256, 256), 256)
            grad_a = dot32(right_qkv[at, :], ring_q[k % 2], contract_last)
            grad_m = dot32(right_up[at, :], ring_u[k % 2], contract_last)
            s_buf[at, features] = (grad_a * gain_a[:, features] + grad_m * gain_m[:, features]).astype(jnp.bfloat16)
            mean, scale = jnp.concatenate([means[at, :]] * wide, axis=1), jnp.concatenate([scales[at, :]] * wide, axis=1)
            normed = (ring_t[k % 2, at, :].astype(jnp.float32) - mean) * scale
            terms = (grad_a * normed, grad_a, grad_m * normed, grad_m)
            return tuple(have + jnp.sum(term.reshape(32, 8, slab), axis=0) for have, term in zip(sums, terms))

        sums = lax.fori_loop(0, 2 * half // 256, body, (jnp.zeros((8, slab), jnp.float32),) * 4)
        first = small_first.shape[0] - 4 * width // 128
        for m, have in enumerate(sums):
            line = jnp.sum(have, axis=0, keepdims=True)
            for j in range(wide):
                row = first + (m * width + k * slab) // 128 + j
                small_first[row : row + 1, :] = line[:, j * 128 : (j + 1) * 128]

    act = dict(
        S=in_slab, Y=start_across, P=out_start if inside else (lambda: None), A=across_event, B=chain_pair, F=final_event, C=start_chunk, X=stage_event, G=finish_chunk,
        L=start_loads, Q=out_event, M=lambda: small_send(0).start(), N=small_event,
    )
    for item in scatter_schedule(nz, nlo, n, stages, width // slab if inside else 0):
        act[item[0]](*item[1:])

    for b in range(4):
        for q in range(nlo):
            across(b, q).wait_send()

            @pl.when(lo != q)
            def _(b=b, q=q):
                near(b, q).wait_send()

        for seq in range(nz):
            @pl.when(z != seq)
            def _(b=b, seq=seq):
                along(b, seq, 0).wait_send()

    for g in range(n):
        for t in range(stages):
            if g < len(ready) or (t == 0 and g + 3 < n):
                continue
            for h in range(nhi):
                for rel in stage_pieces(t):
                    stage_send(g, t, h, rel).wait_send()
    for t in range(stages):
        for rel in stage_pieces(t):
            out_send(t, rel).wait_send()

    @pl.when(moves)
    def _():
        out_move().wait()

    @pl.when(jnp.logical_not(moves))
    def _():
        out_stay().wait()

    for t in range(len(doubling)):
        small_send(t).wait_send()


def scatter_all(lay, partial_o, partial_s, x_down, x_up, x_qkv, g_down, g_up, g_qkv, g_out, terms, small):
    total, width = partial_o.shape
    nz, nlo, nhi = lay.nz, lay.nlo, lay.nhi
    rows = total // (nhi * nlo)
    ranks = nz * nhi
    ff = g_down.shape[1]
    repeat = max(1, ranks // H)
    grain = width // (ranks * nlo)
    span = nz * grain
    stages = len(lay.bits)
    chunks = scatter_chunks(width, ff, repeat)
    n = len(chunks)
    steps = 2 * stages + 1
    small_shape = ((3 * width + ranks * ff + 5 * width) // 128, 128)
    anywhere = pl.BlockSpec(memory_space=pl.ANY)
    inside = pl.BlockSpec(memory_space=pltpu.VMEM)
    dma = pltpu.SemaphoreType.DMA
    bf16, f32 = jnp.bfloat16, jnp.float32
    scratch = [
        pltpu.VMEM((2, 2, rows, width), bf16),
        pltpu.VMEM((2, nlo, rows, width), bf16),
        pltpu.VMEM((2, nlo, rows, width), bf16),
        pltpu.VMEM((2, nz + 1, rows, width), bf16),
    ]
    here = chunks[2:] if terms is not None else chunks
    for chunk in here:
        scratch.append(pltpu.VMEM((nhi, nlo // 2, span, chunk[2]), bf16))
    for chunk in here:
        for t in range(stages):
            scratch.append(pltpu.VMEM((nhi, nlo >> (t + 1), span, chunk[2]), bf16))
    scratch.append(pltpu.VMEM((nlo // 2, grain, width), bf16))
    for t in range(stages):
        scratch.append(pltpu.VMEM((nlo >> (t + 1), grain, width), bf16))
    scratch += [pltpu.VMEM((steps,) + small_shape, f32), pltpu.VMEM((steps,) + small_shape, f32)]
    widest = max(chunk[2] for chunk in chunks)
    fused = terms is not None
    scratch += [
        pltpu.VMEM((2 if total <= 1024 else 1, total, width), bf16),
        *[pltpu.VMEM(g.shape, bf16) for g in ((g_up, g_qkv) if fused else (g_down, g_up, g_qkv, g_out))],
        pltpu.VMEM((3, nhi, nlo // 2, span, widest), bf16),
        pltpu.VMEM((width // ranks, width), bf16),
    ]
    if fused:
        scratch += [
            pltpu.VMEM((total, width), bf16), pltpu.VMEM((2, total, 256), bf16), pltpu.VMEM((2, 256, 3 * HD), bf16),
            pltpu.VMEM((2, 256, ff), bf16), pltpu.VMEM((total, 128), f32), pltpu.VMEM((total, 128), f32),
            pltpu.VMEM(small_shape, f32),
        ]
    most = nlo // 2
    scratch += [
        dma((4, 2)), dma((4, nlo)), dma((4, nlo)), dma((4, nlo)), dma((4, nlo)), dma((4, nz, 2)), dma((4, nz)),
        dma((n, stages, nhi, most)), dma((n, stages, nhi, most)), dma((n, ranks)), dma((n, ranks)),
        dma((n,)), dma((stages, most)), dma((stages, most)), dma, dma, dma((steps,)), dma((steps,)), dma((3,)), dma((4,)),
    ]
    if fused:
        scratch += [dma((2, 3)), dma((2,))]
    return pl.pallas_call(
        functools.partial(scatter_kernel, lay, (rows, width, ff, repeat, fused)),
        out_shape=[
            jax.ShapeDtypeStruct((rows, width), f32),
            jax.ShapeDtypeStruct((rows, width), f32),
            jax.ShapeDtypeStruct((grain, ff * ranks), bf16),
            jax.ShapeDtypeStruct((grain, ff * ranks), bf16),
            jax.ShapeDtypeStruct((grain, 3 * width), bf16),
            jax.ShapeDtypeStruct((grain, width), bf16),
            jax.ShapeDtypeStruct(small_shape, f32),
        ],
        in_specs=([anywhere] * 13 + [inside] * 5) if fused else ([anywhere] * 8 + [inside, anywhere]),
        out_specs=[inside, inside, anywhere, anywhere, anywhere, anywhere, inside],
        scratch_shapes=scratch,
        compiler_params=pltpu.CompilerParams(
            collective_id=2, has_side_effects=True, vmem_limit_bytes=62 * 1024 * 1024
        ),
        name="scatter_all",
    )(
        partial_o,
        *((x_up, x_qkv, g_up, g_qkv, *terms) if fused else (x_down, x_up, x_qkv, g_down, g_up, g_qkv, g_out, small, partial_s)),
    )


def plain_block(lay, operands):
    f32, bf16 = jnp.float32, jnp.bfloat16
    (own, own_cotangent, qkv_weight, qkv_bias, out_weight, up_weight, up_bias, down_weight,
     attn_norm_gain, attn_norm_bias, mlp_norm_gain, mlp_norm_bias) = operands
    nz, nlo, nhi = lay.nz, lay.nlo, lay.nhi
    ranks = nz * nhi
    rows, width = own.shape
    weight_rows = qkv_weight.shape[0]
    half = nlo * rows
    z, hi, lo = place(lay)
    rank = z * nhi + hi
    ff = up_weight.shape[1] // ranks
    repeat = max(1, ranks // H)
    head = rank // repeat
    score_scale = HD ** (-0.5)
    seq_tokens, seq_cotangent, qkv_here, up_here, down_here = gather_all(
        lay, own, own_cotangent, qkv_weight, up_weight, down_weight
    )
    own_qkv = jnp.concatenate(
        [
            lax.dynamic_slice(qkv_weight, (0, part * width + head * HD), (weight_rows, HD))
            for part in range(3)
        ],
        axis=1,
    )
    own_up = lax.dynamic_slice(up_weight, (0, rank * ff), (weight_rows, ff))
    own_down = lax.dynamic_slice(down_weight, (0, rank * ff), (weight_rows, ff))
    qkv_here = lax.dynamic_update_slice(qkv_here, own_qkv, (z * weight_rows, 0))
    up_here = lax.dynamic_update_slice(up_here, own_up, (z * weight_rows, 0))
    down_here = lax.dynamic_update_slice(down_here, own_down, (z * weight_rows, 0))
    out_head = lax.dynamic_slice(out_weight, (head * HD - z * weight_rows, 0), (HD, width))
    out_rows = width // ranks
    out_at = rank * out_rows - head * HD

    positions = jnp.arange(2 * half, dtype=jnp.int32)

    normed, _ = normalize(seq_tokens.astype(f32))
    attn_in = (normed * attn_norm_gain + attn_norm_bias).astype(bf16)
    mlp_in = (normed * mlp_norm_gain + mlp_norm_bias).astype(bf16)
    bias_here = jnp.concatenate(
        [lax.dynamic_slice(qkv_bias, (part * width + head * HD,), (HD,)) for part in range(3)]
    )
    projected = dot32(attn_in, qkv_here) + bias_here
    queries = rotary(projected[:, :HD], positions).astype(bf16)
    keys = rotary(projected[:, HD : 2 * HD], positions).astype(bf16)
    values = projected[:, 2 * HD :].astype(bf16)
    causal = positions[:, None] >= positions[None, :]
    scores = jnp.where(causal, dot32(queries, keys, contract_last) * score_scale, masked_score)
    top = jnp.max(scores, axis=-1, keepdims=True)
    weights = jnp.where(causal, jnp.exp(scores - top), 0.0)
    total = jnp.sum(weights, axis=-1, keepdims=True)
    mixed_full = dot32(weights.astype(bf16), values) / total
    log_total = top + jnp.log(total)
    mixed = mixed_full.astype(bf16)
    mixed_mine = lax.dynamic_slice(mixed, (0, out_at), (mixed.shape[0], out_rows))
    out_mine = lax.dynamic_slice(out_head, (out_at, 0), (out_rows, width))
    hidden = dot32(mlp_in, up_here) + lax.dynamic_slice(up_bias, (rank * ff,), (ff,))
    activated_full, gelu_pull = jax.vjp(exact_gelu, hidden)
    activated = activated_full.astype(bf16)
    out_partial = dot32(mixed_mine, out_mine) + dot32(activated, down_here, contract_last)
    grad_hidden = gelu_pull(dot32(seq_cotangent, down_here))[0].astype(bf16)
    grad_mixed = dot32(seq_cotangent, out_head, contract_last).astype(bf16)
    row_dot = jnp.sum(grad_mixed.astype(f32) * mixed_full, axis=-1, keepdims=True)
    probs = jnp.where(causal, jnp.exp(scores - log_total), 0.0)
    grad_values = dot32(probs.astype(bf16), grad_mixed, contract_first)
    grad_probs = dot32(grad_mixed, values, contract_last)
    grad_scores = (probs * (grad_probs - row_dot)).astype(bf16)
    grad_queries = dot32(grad_scores, keys) * score_scale
    grad_keys = dot32(grad_scores, queries, contract_first) * score_scale
    grad_projected = jnp.concatenate(
        [rotary(grad_queries, -positions), rotary(grad_keys, -positions), grad_values], axis=1
    ).astype(bf16)
    grad_attn_in = dot32(grad_projected, qkv_here, contract_last) * (1.0 / repeat)
    grad_mlp_in = dot32(grad_hidden, up_here, contract_last)
    in_partial = grad_attn_in * attn_norm_gain + grad_mlp_in * mlp_norm_gain
    sums = jnp.stack(
        [
            jnp.sum(grad_attn_in * normed, axis=0),
            jnp.sum(grad_attn_in, axis=0),
            jnp.sum(grad_mlp_in * normed, axis=0),
            jnp.sum(grad_mlp_in, axis=0),
        ]
    )
    first_copy = jnp.where(rank % repeat == 0, 1.0, 0.0)
    return (
        seq_cotangent, attn_in, mlp_in, activated, grad_hidden, grad_projected, mixed_mine,
        out_partial.astype(bf16), in_partial.astype(bf16), sums,
        jnp.sum(grad_projected.astype(f32), axis=0) * first_copy,
        jnp.sum(grad_hidden.astype(f32), axis=0),
        None,
    )


def fused_block(lay, operands):
    f32 = jnp.float32
    (own, own_cotangent, qkv_weight, qkv_bias, out_weight, up_weight, up_bias, down_weight,
     attn_norm_gain, attn_norm_bias, mlp_norm_gain, mlp_norm_bias) = operands
    rows, width = own.shape
    total = lay.nhi * lay.nlo * rows
    half_rot = ROT // 2
    inv_freq = np.float32(10000.0) ** (-(np.arange(half_rot, dtype=np.float32) * np.float32(2.0)) / np.float32(ROT))
    angles = np.arange(total, dtype=np.float32)[:, None] * inv_freq[None, :]
    cosine, sine = np.cos(angles).astype(np.float32), np.sin(angles).astype(np.float32)
    rest = np.zeros((total, 128 - ROT), np.float32)
    found = block_all(
        lay, own, own_cotangent, qkv_weight, up_weight, down_weight, out_weight,
        qkv_bias[None], up_bias[None],
        [v[None] for v in (attn_norm_gain, attn_norm_bias, mlp_norm_gain, mlp_norm_bias)],
        jnp.asarray(np.concatenate([cosine, cosine, rest + np.float32(1.0)], axis=1)),
        jnp.asarray(np.concatenate([-sine, sine, rest], axis=1)),
    )
    return tuple(found[:8]) + (
        None, None, None, None,
        (*found[10:18], attn_norm_gain[None], mlp_norm_gain[None], *found[18:21]),
    )


def local_block(
    lay,
    tokens,
    qkv_weight,
    qkv_bias,
    out_weight,
    out_bias,
    up_weight,
    up_bias,
    down_weight,
    down_bias,
    attn_norm_gain,
    attn_norm_bias,
    mlp_norm_gain,
    mlp_norm_bias,
    cotangent,
):
    f32, bf16 = jnp.float32, jnp.bfloat16
    nz, nlo, nhi = lay.nz, lay.nlo, lay.nhi
    ranks = nz * nhi
    rows = tokens.shape[1]
    width = tokens.shape[2]
    hidden_width = up_weight.shape[1]
    weight_rows = qkv_weight.shape[0]
    half = nlo * rows
    ctx = lax.axis_index("ctx")
    z = lax.axis_index("shard")
    hi, lo = ctx // nlo, ctx % nlo
    rank = z * nhi + hi
    ff = hidden_width // ranks
    repeat = max(1, ranks // H)
    head = rank // repeat
    own = tokens[0]
    own_cotangent = cotangent[0]
    operands = (
        own, own_cotangent, qkv_weight, qkv_bias, out_weight, up_weight, up_bias, down_weight,
        attn_norm_gain, attn_norm_bias, mlp_norm_gain, mlp_norm_bias,
    )
    fits = repeat == 1 and nlo == 4 and nhi * half * width <= 1024 * 2048
    (seq_cotangent, attn_in, mlp_in, activated, grad_hidden, grad_projected, mixed_mine,
     out_partial, in_partial, sums, qkv_bias_part, up_bias_part, terms) = (fused_block if fits else plain_block)(lay, operands)

    small = None
    if not fits:
        qkv_bias_full = jnp.zeros((3, width), f32)
        qkv_bias_full = lax.dynamic_update_slice(
            qkv_bias_full, qkv_bias_part.reshape(3, HD), (0, head * HD)
        ).reshape(-1)
        up_bias_full = lax.dynamic_update_slice(
            jnp.zeros((hidden_width,), f32),
            up_bias_part,
            (rank * ff,),
        )
        small = jnp.concatenate(
            [
                qkv_bias_full,
                up_bias_full,
                jnp.sum(own_cotangent.astype(f32), axis=0),
                sums.reshape(-1),
            ]
        ).reshape(-1, 128)
    summed_out, summed_in, all_down, all_up, all_qkv, all_out, small = scatter_all(
        lay,
        out_partial,
        in_partial,
        seq_cotangent,
        mlp_in,
        attn_in,
        activated,
        grad_hidden,
        grad_projected,
        mixed_mine,
        terms,
        small,
    )
    output = (own.astype(f32) + summed_out + (out_bias + down_bias)).astype(bf16)[None]
    own_normed, own_scale = normalize(own.astype(f32))
    input_grad = own_scale * (
        summed_in
        - jnp.mean(summed_in, axis=-1, keepdims=True)
        - own_normed * jnp.mean(summed_in * own_normed, axis=-1, keepdims=True)
    )
    tokens_grad = (own_cotangent.astype(f32) + input_grad)[None]

    small = small.reshape(-1)
    cuts = [3 * width, hidden_width, width, width, width, width, width]
    small_parts, at = [], 0
    for size in cuts:
        small_parts.append(small[at : at + size])
        at += size

    qkv_weight_grad = all_qkv.astype(f32)
    out_weight_grad = all_out.astype(f32)
    up_weight_grad = all_up.astype(f32)
    down_weight_grad = all_down.astype(f32)
    return (
        output,
        tokens_grad,
        qkv_weight_grad,
        small_parts[0],
        out_weight_grad,
        small_parts[2],
        up_weight_grad,
        small_parts[1],
        down_weight_grad,
        small_parts[2],
        small_parts[3],
        small_parts[4],
        small_parts[5],
        small_parts[6],
    )


def solution(mesh):
    lay = Layout(mesh)

    def local(*args):
        return local_block(lay, *args)

    sharded = P("shard", "ctx", None)
    by_rows = P("shard", None)
    owned = P(("ctx", "shard"), None)
    in_specs = (
        sharded, by_rows, P(), by_rows, P(), by_rows, P(), by_rows, P(),
        P(), P(), P(), P(), sharded,
    )
    out_specs = (
        sharded, sharded, owned, P(), owned, P(), owned, P(), owned,
        P(), P(), P(), P(), P(),
    )
    return jax.shard_map(
        local, mesh=mesh, in_specs=in_specs, out_specs=out_specs, check_vma=False
    )
```
